32 devices in a mesh: groups: 2 (over x), row: 8 (over z, y), col: 2 (over core).
Axes of the slice: x: 2, y: 2, z: 4, core: 2. Of those that a mesh axis runs over, the one named last changes fastest.
Arguments:
- eigvecs: bfloat16 [1024, 512], P(('groups', 'row'), 'col'), parts along dimension 0, may hold values from -0.25 to 0.25
- eigvals: float32 [1024], P(('groups', 'col')), parts along dimension 0, may hold values from 0.05 to 20
- expression: bfloat16 [1024, 1024], P(('groups', 'row')), parts along dimension 0, may hold values from -6 to 6
- dosage: bfloat16 [1024, 1536], P(('groups', 'row')), parts along dimension 0, may hold values from 0 to 2
- delta: float32 [2048], P('groups'), parts along dimension 0, may hold values from 0.1 to 10
- window_start: int32 [2048], P('groups'), parts along dimension 0, may hold values from 0 to 1280
- window_valid: int32 [2048], P('groups'), parts along dimension 0, may hold values from 32 to 256
- gene_owner: int32 [2048], P('groups'), parts along dimension 0, may hold values from 0 to 7, as said below
Outputs:
- zscore: float32 [2048, 256], P(('groups', 'row'), 'col'), parts along dimension 0
The draws below stay inside these ranges and needn't reach their ends.
There are 2 independent parts, one for each index of `groups`. The reference program is written for one: setup_inputs(seed, part) draws one part's arguments, and reference() takes and returns one part's arrays. A program takes and returns all parts, laid end to end along the dimension named above; each array names one. Nothing has to cross between parts.
Inputs may be any that keep to these rules, and one draw needn't show every extreme that they name: `gene_owner`: slice s holds genes s * 128 to (s + 1) * 128 - 1. Every owner holds exactly 128 genes, and the genes of one slice go to one owner in groups of exactly 16 genes or not at all.
All inputs are finite; a program needn't handle non-finite values.
Results may differ from the reference program's by a relative error of at most 0.004.
Values may be sent and summed in bfloat16 or wider, within the bound.
No kernel may reach another device: no remote copies, remote signals or barrier semaphores. Data moves between devices by JAX's collectives and lax.ppermute only.
A program may use at most 64 MiB of HBM per device.

```python
import math
import jax
import jax.numpy as jnp
from jax import lax

N = 512
G_DEV = 128
G = 1024
V = 1536
W = 256
CAP = 16


def draw_gene_owner(key, part):
    key = jax.random.fold_in(key, 7)
    owners = G // G_DEV
    blocks = G_DEV // CAP
    key_relabel, key_rows, key_cols, key_shuffle = jax.random.split(key, 4)
    relabel = jax.random.permutation(key_relabel, owners)
    rowshift = jax.random.permutation(key_rows, owners)
    colshift = jax.random.permutation(key_cols, owners)[:blocks]
    shuffles = jax.vmap(lambda inner_key: jax.random.permutation(inner_key, G_DEV))(jax.random.split(key_shuffle, owners))
    block_of = shuffles // CAP
    latin = (rowshift[:, None] + colshift[block_of]) % owners
    return relabel[latin].reshape(G).astype(jnp.int32)


def set_ends(values, stream_key, smallest, largest):
    dims = values.shape
    index_at = [jax.random.randint(jax.random.fold_in(stream_key, axis), (), 0, dims[axis]) for axis in range(len(dims))]
    values = values.at[tuple(index_at)].set(smallest)
    longest = dims.index(max(dims))
    index_at[longest] = (index_at[longest] + 1) % dims[longest]
    return values.at[tuple(index_at)].set(largest)


def steps_of(key, shape, shards, least, high):
    loudness = 1.0
    for dim, parts in shards:
        heights = jax.random.uniform(jax.random.fold_in(jax.random.fold_in(key, 6), dim), (parts,), jnp.float32, least / len(shards), high / len(shards))
        loudness = loudness * jnp.repeat(jnp.exp(heights), shape[dim] // parts).reshape((-1,) + (1,) * (len(shape) - 1 - dim))
    return loudness


def gaussian(own_key, shape, scale, reach, shards=(), kind=jnp.bfloat16):
    array = jax.random.normal(own_key, shape, jnp.float32) * scale
    if len(shards) > 0:
        array = steps_of(own_key, shape, shards, -0.22, 0.18) * array
    return jnp.clip(array, min=-reach, max=reach).astype(kind)


def setup_inputs(seed: int = 0, part: int = 0) -> dict:
    splits = jax.random.split(jax.random.key(seed), 9)
    part_splits = jax.random.split(jax.random.fold_in(splits[8], part), 9)
    eigvecs = gaussian(part_splits[0], (N, N), N ** -0.5, 0.25, ((0, 8), (1, 2)))
    eigvals = jnp.clip(jnp.exp(math.log(20.0) - 5.9914645 * jax.random.uniform(part_splits[1], (N,), jnp.float32) ** steps_of(part_splits[1], (N,), ((0, 2),), -0.2, 0.2)), 0.05, 20.0)
    expression = gaussian(part_splits[2], (N, G), 1.0, 6.0, ((0, 8),))
    dosage = jnp.clip(2.0 * jax.random.uniform(part_splits[3], (N, V), jnp.float32) ** steps_of(part_splits[3], (N, V), ((0, 8),), -0.2, 0.2), 0.0, 2.0).astype(jnp.bfloat16)
    delta = jnp.clip(jnp.exp(jax.random.uniform(part_splits[4], (G,), jnp.float32, math.log(0.1), math.log(10.0))), 0.1, 10.0)
    window_start = set_ends(jax.random.randint(part_splits[5], (G,), 0, V - W + 1), jax.random.fold_in(part_splits[5], 1), 0, V - W).astype(jnp.int32)
    window_valid = set_ends(jax.random.randint(part_splits[6], (G,), W // 8, W + 1), jax.random.fold_in(part_splits[6], 1), W // 8, W).astype(jnp.int32)
    gene_owner = draw_gene_owner(jax.random.fold_in(jax.random.fold_in(splits[8], part), 71), part)
    return dict(eigvecs=eigvecs, eigvals=eigvals, expression=expression, dosage=dosage, delta=delta, window_start=window_start, window_valid=window_valid, gene_owner=gene_owner)


def reference(eigvecs, eigvals, expression, dosage, delta, window_start, window_valid, gene_owner):
    rot_expr = jnp.dot(eigvecs.T, expression, preferred_element_type=jnp.float32).astype(jnp.bfloat16)
    rot_dose = jnp.dot(eigvecs.T, dosage, preferred_element_type=jnp.float32).astype(jnp.bfloat16)
    weight = 1.0 / (eigvals[None, :] + delta[:, None])
    expr_float = rot_expr.T.astype(jnp.float32)
    expr_power = lax.optimization_barrier(jnp.sum(weight * expr_float * expr_float, axis=1))
    weighted = (weight * expr_float).astype(jnp.bfloat16)
    weight_low = weight.astype(jnp.bfloat16)
    dose_sq = jnp.square(rot_dose.astype(jnp.float32)).astype(jnp.bfloat16)
    cross_all = jnp.dot(weighted, rot_dose, preferred_element_type=jnp.float32)
    power_all = jnp.dot(weight_low, dose_sq, preferred_element_type=jnp.float32)
    slot_index = jnp.arange(W, dtype=jnp.int32)
    columns = window_start[:, None] + slot_index[None, :]
    cross_sum = jnp.take_along_axis(cross_all, columns, axis=1)
    dose_power = jnp.take_along_axis(power_all, columns, axis=1)
    scale = jnp.sqrt(jnp.float32(N))
    zscore = jnp.where(slot_index[None, :] < window_valid[:, None], scale * cross_sum / jnp.sqrt(dose_power * expr_power[:, None]), 0.0)
    owner_order = jnp.argsort(gene_owner * G + jnp.arange(G, dtype=jnp.int32))
    return zscore[owner_order]
```

```python
import jax
import jax.numpy as jnp
from jax import lax
from jax.experimental import pallas as pl
from jax.experimental.pallas import tpu as pltpu
from jax.sharding import PartitionSpec as P

W = 256
LANES = 128
VMEM_LIMIT = 32 * 1024 * 1024
NT = (((1,), (1,)), ((), ()))
f32 = jnp.float32
bf16 = jnp.bfloat16


def owner_listing(gene_owner):
    total = gene_owner.shape[0]
    return jnp.argsort(gene_owner * total + jnp.arange(total, dtype=jnp.int32))


def earlier_equal(labels):
    places = jnp.arange(labels.shape[0], dtype=jnp.int32)
    same = labels[:, None] == labels[None, :]
    before = places[:, None] > places[None, :]
    return jnp.sum((same & before).astype(jnp.int32), axis=1)


def shift_windows(tables, starts, largest):
    moved_tables = tables
    step_size = 1
    while step_size <= largest:
        bit_set = starts // step_size % 2 == 1
        filler = jnp.zeros(moved_tables.shape[:-1] + (step_size,), moved_tables.dtype)
        moved = jnp.concatenate([moved_tables[..., step_size:], filler], axis=-1)
        moved_tables = jnp.where(bit_set[None, :, None], moved, moved_tables)
        step_size = step_size * 2
    return moved_tables


def wide_body(eigvecs, eigvals, expression, dosage, delta, window_start, window_valid, gene_owner):
    row_count = lax.axis_size("row")
    row_index = lax.axis_index("row")
    genes_all = expression.shape[1]
    own_count = genes_all // row_count
    half_samples = eigvecs.shape[1]
    samples = half_samples * lax.axis_size("col")
    owner_order = owner_listing(gene_owner)
    my_genes = lax.dynamic_slice_in_dim(owner_order, row_index * own_count, own_count)
    expr_panel, dose_panel = (
        lax.all_to_all(expression, "row", split_axis=1, concat_axis=0, tiled=True),
        lax.all_to_all(dosage, "row", split_axis=1, concat_axis=0, tiled=True),
    )
    panel_data = jnp.concatenate([expr_panel, dose_panel], axis=1)
    rotated = lax.dot_general(
        panel_data,
        lax.all_gather(eigvecs, "row", axis=0, tiled=True),
        (((0,), (0,)), ((), ())),
        preferred_element_type=jnp.float32,
    ).astype(jnp.bfloat16)
    rot_expr = rotated[:own_count]
    rot_dose = rotated[own_count:]
    dose_all = lax.all_gather(rot_dose, "row", axis=0, tiled=True)
    capacity = max(2, own_count // row_count)
    destination = lax.dynamic_slice_in_dim(gene_owner, row_index * own_count, own_count)
    position = destination * capacity + earlier_equal(destination)
    slot_ids = jnp.arange(row_count * capacity, dtype=jnp.int32)
    placement_map = (slot_ids[:, None] == position[None, :]).astype(jnp.bfloat16)
    buckets = jnp.dot(placement_map, rot_expr, preferred_element_type=jnp.float32).astype(
        jnp.bfloat16
    )
    received = lax.all_to_all(buckets, "row", split_axis=0, concat_axis=0, tiled=True)
    source = my_genes // own_count
    owned_expr = jnp.take(received, source * capacity + earlier_equal(source), axis=0)
    own_delta = jnp.take(delta, my_genes)
    own_start = jnp.take(window_start, my_genes)
    own_valid = jnp.take(window_valid, my_genes)
    weight = 1.0 / (eigvals[None, :] + own_delta[:, None])
    expr_float = owned_expr.astype(jnp.float32)
    expr_power = jnp.sum(weight * expr_float * expr_float, axis=1)
    weighted = (weight * expr_float).astype(jnp.bfloat16)
    weight_low = weight.astype(jnp.bfloat16)
    dose_sq = jnp.square(dose_all.astype(jnp.float32)).astype(jnp.bfloat16)
    slot_index = jnp.arange(W, dtype=jnp.int32)
    contract = (((1,), (1,)), ((), ()))
    cross_all = lax.dot_general(weighted, dose_all, contract, preferred_element_type=jnp.float32)
    power_all = lax.dot_general(weight_low, dose_sq, contract, preferred_element_type=jnp.float32)
    stacked = jnp.stack([cross_all, power_all], axis=0)
    variants = dose_all.shape[0]
    shifted = shift_windows(stacked, own_start, variants - W)
    cross_sum = shifted[0, :, :W]
    dose_power = shifted[1, :, :W]
    cross_sum, dose_power, expr_power = lax.psum((cross_sum, dose_power, expr_power), "col")
    scale = jnp.sqrt(jnp.float32(samples))
    zscore = jnp.where(
        slot_index[None, :] < own_valid[:, None],
        scale * cross_sum / jnp.sqrt(dose_power * expr_power[:, None]),
        0.0,
    )
    width_part = W // lax.axis_size("col")
    return lax.dynamic_slice_in_dim(zscore, lax.axis_index("col") * width_part, width_part, 1)


def route_kernel(place_ref, owner_ref, delta_ref, start_ref, valid_ref, vecs_ref, expr_ref, send_ref, gene_ref):
    slices = owner_ref.shape[0]
    capacity = LANES // slices
    half = vecs_ref.shape[1]
    owner = owner_ref[...]
    before = lax.broadcasted_iota(jnp.int32, (LANES, LANES), 0) < lax.broadcasted_iota(
        jnp.int32, (LANES, LANES), 1
    )
    before = before.astype(bf16)
    rank = jnp.zeros(owner.shape, f32)
    for o in range(slices):
        same = (owner == o).astype(f32)
        rank += same * jnp.dot(same.astype(bf16), before, preferred_element_type=f32)
    bucket = owner * capacity + rank.astype(jnp.int32)
    slot = lax.broadcasted_iota(jnp.int32, (LANES, LANES), 0)
    own_slot = lax.broadcasted_iota(jnp.int32, (capacity, LANES), 0) + place_ref[0] * capacity
    lane = lax.broadcasted_iota(jnp.int32, (capacity, LANES), 1)
    sorted_slices = []
    for s in range(slices):
        here = bucket[s : s + 1, :]
        pick = (slot == here).astype(bf16)
        sorted_slices.append(
            lax.dot_general(pick, expr_ref[:, s * LANES : (s + 1) * LANES], NT, preferred_element_type=f32)
        )
        mine = (own_slot == here).astype(f32)
        figures = jnp.zeros((capacity, LANES), f32)
        for i, ref in enumerate((delta_ref, start_ref, valid_ref)):
            row = ref[s : s + 1, :].astype(f32)
            figures = jnp.where(lane == i, jnp.sum(mine * row, axis=1, keepdims=True), figures)
        gene_ref[s * capacity : (s + 1) * capacity, :] = figures
    for o in range(slices):
        rows = jnp.concatenate([x[o * capacity : (o + 1) * capacity, :] for x in sorted_slices], axis=0)
        send_ref[o, :, :half] = vecs_ref[...]
        send_ref[o, :, half:] = rows.T.astype(bf16)


def weight_kernel(place_ref, recv_ref, other_ref, vals_ref, gene_ref, turned_ref, weighted_ref, low_ref, power_ref):
    rows, samples, _ = recv_ref.shape
    half = other_ref.shape[2]
    row = place_ref[0]
    for m in range(rows):
        r = row ^ m
        cols = pl.ds(m * samples, samples)
        turned_ref[:half, cols] = recv_ref[r, :, :half].astype(f32).T.astype(bf16)
        turned_ref[half:, cols] = other_ref[r].astype(f32).T.astype(bf16)
    data = jnp.concatenate([recv_ref[r, :, half:] for r in range(rows)], axis=0)
    data = data.astype(f32).T.astype(bf16)
    delta = gene_ref[:, 0:1]
    total = jnp.zeros((data.shape[0], 1), f32)
    for c in range(2):
        if c == 0:
            vecs = jnp.concatenate([recv_ref[r, :, :half] for r in range(rows)], axis=0)
        else:
            vecs = jnp.concatenate([other_ref[r] for r in range(rows)], axis=0)
        cols = pl.ds(c * half, half)
        rotated = jnp.dot(data, vecs, preferred_element_type=f32).astype(bf16).astype(f32)
        weight = 1.0 / (vals_ref[:, cols] + delta)
        total += jnp.sum(weight * rotated * rotated, axis=1, keepdims=True)
        weighted_ref[:, cols] = (weight * rotated).astype(bf16)
        low_ref[:, cols] = weight.astype(bf16)
    power_ref[...] = jnp.broadcast_to(total, power_ref.shape)


def score_kernel(place_ref, gene_ref, power_ref, turned_ref, weighted_ref, low_ref, *refs):
    *dose_refs, keep_ref, pass_ref, dose_scr = refs
    samples, variants = dose_refs[0].shape
    for m, ref in enumerate(dose_refs):
        dose_scr[m * samples : (m + 1) * samples, :] = ref[...]
    rotated = jnp.dot(turned_ref[...], dose_scr[...], preferred_element_type=f32).astype(bf16)
    squared = jnp.square(rotated.astype(f32)).astype(bf16)
    cross = jnp.dot(weighted_ref[...], rotated, preferred_element_type=f32)
    power = jnp.dot(low_ref[...], squared, preferred_element_type=f32)
    core = place_ref[1]
    start = gene_ref[:, 1:2].astype(jnp.int32)
    valid = gene_ref[:, 2:3].astype(jnp.int32)
    genes = cross.shape[0]
    lane = lax.broadcasted_iota(jnp.int32, (genes, LANES), 1)
    own_power = power_ref[...]
    scale = jnp.sqrt(f32(samples * len(dose_refs)))
    blocks = variants // LANES
    for out_ref, half in ((keep_ref, core), (pass_ref, 1 - core)):
        offset = start + half * LANES - core * variants
        block = offset >> 7
        shift = offset & (LANES - 1)
        at = lane + shift
        wrapped = at >= LANES
        at = at & (LANES - 1)
        here = block + wrapped.astype(jnp.int32)
        picked = []
        for array in (cross, power):
            low = jnp.zeros((genes, LANES), f32)
            high = low
            for b in range(blocks):
                part = array[:, b * LANES : (b + 1) * LANES]
                low = jnp.where(block == b, part, low)
                high = jnp.where(block + 1 == b, part, high)
            low = jnp.take_along_axis(low, at, axis=1)
            high = jnp.take_along_axis(high, at, axis=1)
            picked.append(jnp.where(wrapped, high, low))
        live = (here >= 0) & (here < blocks) & (lane + half * LANES < valid)
        score = scale * picked[0] / jnp.sqrt(picked[1] * own_power)
        out_ref[...] = jnp.where(live, score, 0.0)


def call(kernel, outs, scratch=(), smem=1, count=0):
    vmem = pl.BlockSpec(memory_space=pltpu.VMEM)
    return pl.pallas_call(
        kernel,
        out_shape=[jax.ShapeDtypeStruct(*o) for o in outs],
        in_specs=[pl.BlockSpec(memory_space=pltpu.SMEM)] * smem + [vmem] * (count - smem),
        out_specs=[vmem] * len(outs),
        scratch_shapes=list(scratch),
        compiler_params=pltpu.CompilerParams(vmem_limit_bytes=VMEM_LIMIT),
    )


def near_body(eigvecs, eigvals, expression, dosage, delta, window_start, window_valid, gene_owner):
    rows = lax.axis_size("row")
    row = lax.axis_index("row")
    core = lax.axis_index("col")
    panel, half = eigvecs.shape
    samples = panel * rows
    variants = dosage.shape[1] // 2
    place = jnp.stack([row, core]).astype(jnp.int32)

    def swap(x, m):
        return lax.ppermute(x, "row", [(i, i ^ m) for i in range(rows)])

    def other_core(x):
        return lax.ppermute(x, "col", [(0, 1), (1, 0)])

    chunks = [None] * rows
    chunks[0] = lax.dynamic_slice_in_dim(dosage, core * variants, variants, 1)
    for m in range(2, rows, 2):
        chunks[m] = swap(chunks[0], m)
    for m in range(0, rows, 2):
        chunks[m + 1] = swap(chunks[m], 1)
    vals = jnp.concatenate([eigvals, other_core(eigvals)])[None, :]
    send, gene = call(
        route_kernel,
        [((rows, panel, half + LANES), bf16), ((LANES, LANES), f32)],
        count=7,
    )(
        place,
        gene_owner.reshape(rows, LANES),
        delta.reshape(rows, LANES),
        window_start.reshape(rows, LANES),
        window_valid.reshape(rows, LANES),
        eigvecs,
        expression,
    )
    received = lax.all_to_all(send, "row", split_axis=0, concat_axis=0, tiled=True)
    other = other_core(received[:, :, :half])
    turned, weighted, low, power = call(
        weight_kernel,
        [((2 * half, samples), bf16), ((LANES, 2 * half), bf16), ((LANES, 2 * half), bf16), ((LANES, LANES), f32)],
        count=5,
    )(place, received, other, vals, gene)
    keep, passed = call(
        score_kernel,
        [((LANES, LANES), f32)] * 2,
        scratch=[pltpu.VMEM((samples, variants), bf16)],
        count=6 + rows,
    )(place, gene, power, turned, weighted, low, *chunks)
    return keep + other_core(passed)


def body(eigvecs, eigvals, expression, dosage, delta, window_start, window_valid, gene_owner):
    rows = lax.axis_size("row")
    samples = eigvecs.shape[0] * rows
    own = expression.shape[1] // rows
    fits = (
        lax.axis_size("col") == 2
        and own == LANES
        and W == 2 * LANES
        and rows & (rows - 1) == 0
        and own // rows % 16 == 0
        and dosage.shape[1] % (2 * LANES) == 0
        and samples * (samples + dosage.shape[1]) <= VMEM_LIMIT // 16
    )
    run = near_body if fits else wide_body
    return run(eigvecs, eigvals, expression, dosage, delta, window_start, window_valid, gene_owner)


def solution(mesh):
    placed = (
        P(("groups", "row"), "col"),
        P(("groups", "col")),
        P(("groups", "row"), None),
        P(("groups", "row"), None),
        P("groups"),
        P("groups"),
        P("groups"),
        P("groups"),
    )
    return jax.shard_map(
        body, mesh=mesh, in_specs=placed, out_specs=P(("groups", "row"), "col"), check_vma=False
    )
```

```python
import jax
import jax.numpy as jnp
from jax import lax
from jax.experimental import pallas as pl
from jax.experimental.pallas import tpu as pltpu
from jax.sharding import PartitionSpec as P

W = 256
LANES = 128
VMEM_LIMIT = 32 * 1024 * 1024
NT = (((1,), (1,)), ((), ()))
f32 = jnp.float32
bf16 = jnp.bfloat16


def owner_listing(gene_owner):
    total = gene_owner.shape[0]
    return jnp.argsort(gene_owner * total + jnp.arange(total, dtype=jnp.int32))


def earlier_equal(labels):
    places = jnp.arange(labels.shape[0], dtype=jnp.int32)
    same = labels[:, None] == labels[None, :]
    before = places[:, None] > places[None, :]
    return jnp.sum((same & before).astype(jnp.int32), axis=1)


def shift_windows(tables, starts, largest):
    moved_tables = tables
    step_size = 1
    while step_size <= largest:
        bit_set = starts // step_size % 2 == 1
        filler = jnp.zeros(moved_tables.shape[:-1] + (step_size,), moved_tables.dtype)
        moved = jnp.concatenate([moved_tables[..., step_size:], filler], axis=-1)
        moved_tables = jnp.where(bit_set[None, :, None], moved, moved_tables)
        step_size = step_size * 2
    return moved_tables


def wide_body(eigvecs, eigvals, expression, dosage, delta, window_start, window_valid, gene_owner):
    row_count = lax.axis_size("row")
    row_index = lax.axis_index("row")
    genes_all = expression.shape[1]
    own_count = genes_all // row_count
    half_samples = eigvecs.shape[1]
    samples = half_samples * lax.axis_size("col")
    owner_order = owner_listing(gene_owner)
    my_genes = lax.dynamic_slice_in_dim(owner_order, row_index * own_count, own_count)
    expr_panel, dose_panel = (
        lax.all_to_all(expression, "row", split_axis=1, concat_axis=0, tiled=True),
        lax.all_to_all(dosage, "row", split_axis=1, concat_axis=0, tiled=True),
    )
    panel_data = jnp.concatenate([expr_panel, dose_panel], axis=1)
    rotated = lax.dot_general(
        panel_data,
        lax.all_gather(eigvecs, "row", axis=0, tiled=True),
        (((0,), (0,)), ((), ())),
        preferred_element_type=jnp.float32,
    ).astype(jnp.bfloat16)
    rot_expr = rotated[:own_count]
    rot_dose = rotated[own_count:]
    dose_all = lax.all_gather(rot_dose, "row", axis=0, tiled=True)
    capacity = max(2, own_count // row_count)
    destination = lax.dynamic_slice_in_dim(gene_owner, row_index * own_count, own_count)
    position = destination * capacity + earlier_equal(destination)
    slot_ids = jnp.arange(row_count * capacity, dtype=jnp.int32)
    placement_map = (slot_ids[:, None] == position[None, :]).astype(jnp.bfloat16)
    buckets = jnp.dot(placement_map, rot_expr, preferred_element_type=jnp.float32).astype(
        jnp.bfloat16
    )
    received = lax.all_to_all(buckets, "row", split_axis=0, concat_axis=0, tiled=True)
    source = my_genes // own_count
    owned_expr = jnp.take(received, source * capacity + earlier_equal(source), axis=0)
    own_delta = jnp.take(delta, my_genes)
    own_start = jnp.take(window_start, my_genes)
    own_valid = jnp.take(window_valid, my_genes)
    weight = 1.0 / (eigvals[None, :] + own_delta[:, None])
    expr_float = owned_expr.astype(jnp.float32)
    expr_power = jnp.sum(weight * expr_float * expr_float, axis=1)
    weighted = (weight * expr_float).astype(jnp.bfloat16)
    weight_low = weight.astype(jnp.bfloat16)
    dose_sq = jnp.square(dose_all.astype(jnp.float32)).astype(jnp.bfloat16)
    slot_index = jnp.arange(W, dtype=jnp.int32)
    contract = (((1,), (1,)), ((), ()))
    cross_all = lax.dot_general(weighted, dose_all, contract, preferred_element_type=jnp.float32)
    power_all = lax.dot_general(weight_low, dose_sq, contract, preferred_element_type=jnp.float32)
    stacked = jnp.stack([cross_all, power_all], axis=0)
    variants = dose_all.shape[0]
    shifted = shift_windows(stacked, own_start, variants - W)
    cross_sum = shifted[0, :, :W]
    dose_power = shifted[1, :, :W]
    cross_sum, dose_power, expr_power = lax.psum((cross_sum, dose_power, expr_power), "col")
    scale = jnp.sqrt(jnp.float32(samples))
    zscore = jnp.where(
        slot_index[None, :] < own_valid[:, None],
        scale * cross_sum / jnp.sqrt(dose_power * expr_power[:, None]),
        0.0,
    )
    width_part = W // lax.axis_size("col")
    return lax.dynamic_slice_in_dim(zscore, lax.axis_index("col") * width_part, width_part, 1)


def route_kernel(place_ref, owner_ref, delta_ref, start_ref, valid_ref, vecs_ref, expr_ref, far_ref, e2_ref, e1_ref, e0_ref, gene_ref):
    slices = owner_ref.shape[0]
    capacity = LANES // slices
    half = vecs_ref.shape[1]
    part = expr_ref.shape[0] // 2
    row, core = place_ref[0], place_ref[1]
    owner = owner_ref[...]
    before = lax.broadcasted_iota(jnp.int32, (LANES, LANES), 0) < lax.broadcasted_iota(
        jnp.int32, (LANES, LANES), 1
    )
    before = before.astype(bf16)
    rank = jnp.zeros(owner.shape, f32)
    for o in range(slices):
        same = (owner == o).astype(f32)
        rank += same * jnp.dot(same.astype(bf16), before, preferred_element_type=f32)
    bucket = (owner ^ row) * capacity + rank.astype(jnp.int32)
    slot = lax.broadcasted_iota(jnp.int32, (LANES, LANES), 0)
    own_slot = lax.broadcasted_iota(jnp.int32, (capacity, LANES), 0)
    lane = lax.broadcasted_iota(jnp.int32, (capacity, LANES), 1)
    rows = pl.ds(pl.multiple_of(core * part, part), part)
    sorted_slices = []
    for s in range(slices):
        here = bucket[s : s + 1, :]
        pick = (slot == here).astype(bf16)
        sorted_slices.append(
            lax.dot_general(pick, expr_ref[rows, s * LANES : (s + 1) * LANES], NT, preferred_element_type=f32)
        )
        mine = (own_slot == here).astype(f32)
        figures = jnp.zeros((capacity, LANES), f32)
        for i, ref in enumerate((delta_ref, start_ref, valid_ref)):
            line = ref[s : s + 1, :].astype(f32)
            figures = jnp.where(lane == i, jnp.sum(mine * line, axis=1, keepdims=True), figures)
        gene_ref[s * capacity : (s + 1) * capacity, :] = figures
    far_ref[:, :half] = vecs_ref[...]
    for m in range(slices):
        block = jnp.concatenate([x[m * capacity : (m + 1) * capacity, :] for x in sorted_slices], axis=0)
        block = block.T.astype(bf16)
        side = slice(half + m % 2 * LANES, half + (m % 2 + 1) * LANES)
        if m >= 4:
            far_ref[(m - 4) // 2 * part : ((m - 4) // 2 + 1) * part, side] = block
        elif m >= 2:
            e2_ref[:, m % 2 * LANES : (m % 2 + 1) * LANES] = block
        elif m == 1:
            e1_ref[...] = block
        else:
            e0_ref[...] = block


def weight_kernel(place_ref, kept_ref, near_ref, kept2_ref, near2_ref, vals_ref, gene_ref, turned_ref, weighted_ref, low_ref, power_ref, data_scr):
    samples = kept_ref.shape[0]
    half = vals_ref.shape[1] // 2
    part = samples // 2
    core = place_ref[1]
    sources = ((kept_ref, kept2_ref), (near_ref, near2_ref))
    for n, pair in enumerate(sources):
        for c, ref in enumerate(pair):
            side = core if c == 0 else 1 - core
            for i in range(4):
                first = (n * 4 + i) * samples
                turned_ref[c * half : (c + 1) * half, first : first + samples] = (
                    ref[:, i * half : (i + 1) * half].astype(f32).T.astype(bf16)
                )
                at = 4 * half + i % 2 * LANES
                data_scr[pl.ds(pl.multiple_of(first + side * part, part), part), :] = ref[
                    i // 2 * part : (i // 2 + 1) * part, at : at + LANES
                ]
    data = data_scr[...].astype(f32).T.astype(bf16)
    delta = gene_ref[:, 0:1]
    total = jnp.zeros((data.shape[0], 1), f32)
    for c in range(2):
        vecs = jnp.concatenate(
            [pair[c][:, i * half : (i + 1) * half] for pair in sources for i in range(4)], axis=0
        )
        cols = slice(c * half, (c + 1) * half)
        rotated = jnp.dot(data, vecs, preferred_element_type=f32).astype(bf16).astype(f32)
        weight = 1.0 / (vals_ref[:, cols] + delta)
        total += jnp.sum(weight * rotated * rotated, axis=1, keepdims=True)
        weighted_ref[:, cols] = (weight * rotated).astype(bf16)
        low_ref[:, cols] = weight.astype(bf16)
    power_ref[...] = jnp.broadcast_to(total, power_ref.shape)


def score_kernel(place_ref, gene_ref, power_ref, turned_ref, weighted_ref, low_ref, *refs):
    *dose_refs, keep_ref, pass_ref, dose_scr = refs
    samples, variants = dose_refs[0].shape
    for m, ref in enumerate(dose_refs):
        dose_scr[m * samples : (m + 1) * samples, :] = ref[...]
    rotated = jnp.dot(turned_ref[...], dose_scr[...], preferred_element_type=f32).astype(bf16)
    squared = jnp.square(rotated.astype(f32)).astype(bf16)
    cross = jnp.dot(weighted_ref[...], rotated, preferred_element_type=f32)
    power = jnp.dot(low_ref[...], squared, preferred_element_type=f32)
    core = place_ref[1]
    start = gene_ref[:, 1:2].astype(jnp.int32)
    valid = gene_ref[:, 2:3].astype(jnp.int32)
    genes = cross.shape[0]
    lane = lax.broadcasted_iota(jnp.int32, (genes, LANES), 1)
    own_power = power_ref[...]
    scale = jnp.sqrt(f32(samples * len(dose_refs)))
    blocks = variants // LANES
    for out_ref, half in ((keep_ref, core), (pass_ref, 1 - core)):
        offset = start + half * LANES - core * variants
        block = offset >> 7
        shift = offset & (LANES - 1)
        at = lane + shift
        wrapped = at >= LANES
        at = at & (LANES - 1)
        here = block + wrapped.astype(jnp.int32)
        picked = []
        for array in (cross, power):
            low = jnp.zeros((genes, LANES), f32)
            high = low
            for b in range(blocks):
                part = array[:, b * LANES : (b + 1) * LANES]
                low = jnp.where(block == b, part, low)
                high = jnp.where(block + 1 == b, part, high)
            low = jnp.take_along_axis(low, at, axis=1)
            high = jnp.take_along_axis(high, at, axis=1)
            picked.append(jnp.where(wrapped, high, low))
        live = (here >= 0) & (here < blocks) & (lane + half * LANES < valid)
        score = scale * picked[0] / jnp.sqrt(picked[1] * own_power)
        out_ref[...] = jnp.where(live, score, 0.0)


def call(kernel, outs, scratch=(), smem=1, count=0):
    vmem = pl.BlockSpec(memory_space=pltpu.VMEM)
    return pl.pallas_call(
        kernel,
        out_shape=[jax.ShapeDtypeStruct(*o) for o in outs],
        in_specs=[pl.BlockSpec(memory_space=pltpu.SMEM)] * smem + [vmem] * (count - smem),
        out_specs=[vmem] * len(outs),
        scratch_shapes=list(scratch),
        compiler_params=pltpu.CompilerParams(vmem_limit_bytes=VMEM_LIMIT),
    )


def near_body(eigvecs, eigvals, expression, dosage, delta, window_start, window_valid, gene_owner):
    rows = lax.axis_size("row")
    row = lax.axis_index("row")
    core = lax.axis_index("col")
    panel, half = eigvecs.shape
    part = panel // 2
    samples = panel * rows
    variants = dosage.shape[1] // 2
    place = jnp.stack([row, core]).astype(jnp.int32)

    def swap(x, m):
        return lax.ppermute(x, "row", [(i, i ^ m) for i in range(rows)])

    def other_core(x):
        return lax.ppermute(x, "col", [(0, 1), (1, 0)])

    dose = {0: lax.dynamic_slice_in_dim(dosage, core * variants, variants, 1)}
    dose[4] = swap(dose[0], 4)
    dose[1] = swap(dose[0], 1)
    dose[2] = swap(dose[0], 2)
    vals = jnp.concatenate([eigvals, other_core(eigvals)])[None, :]
    far, e2, e1, e0, gene = call(
        route_kernel,
        [
            ((panel, half + 2 * LANES), bf16),
            ((part, 2 * LANES), bf16),
            ((part, LANES), bf16),
            ((part, LANES), bf16),
            ((LANES, LANES), f32),
        ],
        count=7,
    )(
        place,
        gene_owner.reshape(rows, LANES),
        delta.reshape(rows, LANES),
        window_start.reshape(rows, LANES),
        window_valid.reshape(rows, LANES),
        eigvecs,
        expression,
    )
    r4 = swap(far, 4)
    mid = jnp.concatenate([e2, r4[part:, half:]], axis=0)
    r2 = swap(jnp.concatenate([eigvecs, r4[:, :half], mid], axis=1), 2)
    vecs = [eigvecs, r4[:, :half], r2[:, :half], r2[:, half : 2 * half]]

    def joined(mine, at):
        upper = jnp.concatenate([mine, r4[:part, half + at : half + at + LANES]], axis=1)
        right = r2[:, 2 * half + at : 2 * half + at + LANES]
        lower = jnp.concatenate([right[:part], right[part:]], axis=1)
        return jnp.concatenate(vecs + [jnp.concatenate([upper, lower], axis=0)], axis=1)

    near = swap(joined(e1, LANES), 1)
    kept = joined(e0, 0)
    dose[6] = swap(dose[4], 2)
    for m in (4, 2, 6):
        dose[m + 1] = swap(dose[m], 1)
    turned, weighted, low, power = call(
        weight_kernel,
        [((2 * half, samples), bf16), ((LANES, 2 * half), bf16), ((LANES, 2 * half), bf16), ((LANES, LANES), f32)],
        scratch=[pltpu.VMEM((samples, LANES), bf16)],
        count=7,
    )(place, kept, near, other_core(kept), other_core(near), vals, gene)
    keep, passed = call(
        score_kernel,
        [((LANES, LANES), f32)] * 2,
        scratch=[pltpu.VMEM((samples, variants), bf16)],
        count=6 + rows,
    )(place, gene, power, turned, weighted, low, *[dose[m] for m in (0, 4, 2, 6, 1, 5, 3, 7)])
    return keep + other_core(passed)


def body(eigvecs, eigvals, expression, dosage, delta, window_start, window_valid, gene_owner):
    rows = lax.axis_size("row")
    samples = eigvecs.shape[0] * rows
    own = expression.shape[1] // rows
    fits = (
        lax.axis_size("col") == 2
        and own == LANES
        and W == 2 * LANES
        and rows == 8
        and dosage.shape[1] % (2 * LANES) == 0
        and samples * (samples + dosage.shape[1]) <= VMEM_LIMIT // 16
    )
    run = near_body if fits else wide_body
    return run(eigvecs, eigvals, expression, dosage, delta, window_start, window_valid, gene_owner)


def solution(mesh):
    placed = (
        P(("groups", "row"), "col"),
        P(("groups", "col")),
        P(("groups", "row"), None),
        P(("groups", "row"), None),
        P("groups"),
        P("groups"),
        P("groups"),
        P("groups"),
    )
    return jax.shard_map(
        body, mesh=mesh, in_specs=placed, out_specs=P(("groups", "row"), "col"), check_vma=False
    )
```

```python
import jax
import jax.numpy as jnp
from jax import lax
from jax.experimental import pallas as pl
from jax.experimental.pallas import tpu as pltpu
from jax.sharding import PartitionSpec as P

W = 256
LANES = 128
VMEM_LIMIT = 32 * 1024 * 1024
NT = (((1,), (1,)), ((), ()))
f32 = jnp.float32
bf16 = jnp.bfloat16


def owner_listing(gene_owner):
    total = gene_owner.shape[0]
    return jnp.argsort(gene_owner * total + jnp.arange(total, dtype=jnp.int32))


def earlier_equal(labels):
    places = jnp.arange(labels.shape[0], dtype=jnp.int32)
    same = labels[:, None] == labels[None, :]
    before = places[:, None] > places[None, :]
    return jnp.sum((same & before).astype(jnp.int32), axis=1)


def shift_windows(tables, starts, largest):
    moved_tables = tables
    step_size = 1
    while step_size <= largest:
        bit_set = starts // step_size % 2 == 1
        filler = jnp.zeros(moved_tables.shape[:-1] + (step_size,), moved_tables.dtype)
        moved = jnp.concatenate([moved_tables[..., step_size:], filler], axis=-1)
        moved_tables = jnp.where(bit_set[None, :, None], moved, moved_tables)
        step_size = step_size * 2
    return moved_tables


def wide_body(eigvecs, eigvals, expression, dosage, delta, window_start, window_valid, gene_owner):
    row_count = lax.axis_size("row")
    row_index = lax.axis_index("row")
    genes_all = expression.shape[1]
    own_count = genes_all // row_count
    half_samples = eigvecs.shape[1]
    samples = half_samples * lax.axis_size("col")
    owner_order = owner_listing(gene_owner)
    my_genes = lax.dynamic_slice_in_dim(owner_order, row_index * own_count, own_count)
    expr_panel, dose_panel = (
        lax.all_to_all(expression, "row", split_axis=1, concat_axis=0, tiled=True),
        lax.all_to_all(dosage, "row", split_axis=1, concat_axis=0, tiled=True),
    )
    panel_data = jnp.concatenate([expr_panel, dose_panel], axis=1)
    rotated = lax.dot_general(
        panel_data,
        lax.all_gather(eigvecs, "row", axis=0, tiled=True),
        (((0,), (0,)), ((), ())),
        preferred_element_type=jnp.float32,
    ).astype(jnp.bfloat16)
    rot_expr = rotated[:own_count]
    rot_dose = rotated[own_count:]
    dose_all = lax.all_gather(rot_dose, "row", axis=0, tiled=True)
    capacity = max(2, own_count // row_count)
    destination = lax.dynamic_slice_in_dim(gene_owner, row_index * own_count, own_count)
    position = destination * capacity + earlier_equal(destination)
    slot_ids = jnp.arange(row_count * capacity, dtype=jnp.int32)
    placement_map = (slot_ids[:, None] == position[None, :]).astype(jnp.bfloat16)
    buckets = jnp.dot(placement_map, rot_expr, preferred_element_type=jnp.float32).astype(
        jnp.bfloat16
    )
    received = lax.all_to_all(buckets, "row", split_axis=0, concat_axis=0, tiled=True)
    source = my_genes // own_count
    owned_expr = jnp.take(received, source * capacity + earlier_equal(source), axis=0)
    own_delta = jnp.take(delta, my_genes)
    own_start = jnp.take(window_start, my_genes)
    own_valid = jnp.take(window_valid, my_genes)
    weight = 1.0 / (eigvals[None, :] + own_delta[:, None])
    expr_float = owned_expr.astype(jnp.float32)
    expr_power = jnp.sum(weight * expr_float * expr_float, axis=1)
    weighted = (weight * expr_float).astype(jnp.bfloat16)
    weight_low = weight.astype(jnp.bfloat16)
    dose_sq = jnp.square(dose_all.astype(jnp.float32)).astype(jnp.bfloat16)
    slot_index = jnp.arange(W, dtype=jnp.int32)
    contract = (((1,), (1,)), ((), ()))
    cross_all = lax.dot_general(weighted, dose_all, contract, preferred_element_type=jnp.float32)
    power_all = lax.dot_general(weight_low, dose_sq, contract, preferred_element_type=jnp.float32)
    stacked = jnp.stack([cross_all, power_all], axis=0)
    variants = dose_all.shape[0]
    shifted = shift_windows(stacked, own_start, variants - W)
    cross_sum = shifted[0, :, :W]
    dose_power = shifted[1, :, :W]
    cross_sum, dose_power, expr_power = lax.psum((cross_sum, dose_power, expr_power), "col")
    scale = jnp.sqrt(jnp.float32(samples))
    zscore = jnp.where(
        slot_index[None, :] < own_valid[:, None],
        scale * cross_sum / jnp.sqrt(dose_power * expr_power[:, None]),
        0.0,
    )
    width_part = W // lax.axis_size("col")
    return lax.dynamic_slice_in_dim(zscore, lax.axis_index("col") * width_part, width_part, 1)


def route_kernel(
    place_ref, owner_any, delta_any, start_any, valid_any, expr_any,
    e4_ref, e2_ref, e1_ref, e0_ref, gene_ref,
    owner_ref, delta_ref, start_ref, valid_ref, expr_ref, sems,
):
    row, core = place_ref[0], place_ref[1]
    part = expr_ref.shape[0]
    rows = pl.ds(pl.multiple_of(core * part, part), part)
    pairs = (
        (owner_any, owner_ref),
        (expr_any.at[rows], expr_ref),
        (delta_any, delta_ref),
        (start_any, start_ref),
        (valid_any, valid_ref),
    )
    copies = [pltpu.make_async_copy(a, b, sems.at[i]) for i, (a, b) in enumerate(pairs)]
    for copy in copies:
        copy.start()
    slices = owner_ref.shape[0]
    capacity = LANES // slices
    before = lax.broadcasted_iota(jnp.int32, (LANES, LANES), 0) < lax.broadcasted_iota(
        jnp.int32, (LANES, LANES), 1
    )
    before = before.astype(bf16)
    slot = lax.broadcasted_iota(jnp.int32, (LANES, LANES), 0)
    own_slot = lax.broadcasted_iota(jnp.int32, (capacity, LANES), 0)
    lane = lax.broadcasted_iota(jnp.int32, (capacity, LANES), 1)
    copies[0].wait()
    owner = owner_ref[...]
    rank = jnp.zeros(owner.shape, f32)
    for o in range(slices):
        same = (owner == o).astype(f32)
        rank += same * jnp.dot(same.astype(bf16), before, preferred_element_type=f32)
    bucket = (owner ^ row) * capacity + rank.astype(jnp.int32)
    for copy in copies[1:]:
        copy.wait()
    sorted_slices = []
    for s in range(slices):
        here = bucket[s : s + 1, :]
        pick = (slot == here).astype(bf16)
        sorted_slices.append(
            lax.dot_general(pick, expr_ref[:, s * LANES : (s + 1) * LANES], NT, preferred_element_type=f32)
        )
        mine = (own_slot == here).astype(f32)
        figures = jnp.zeros((capacity, LANES), f32)
        for i, ref in enumerate((delta_ref, start_ref, valid_ref)):
            line = ref[s : s + 1, :].astype(f32)
            figures = jnp.where(lane == i, jnp.sum(mine * line, axis=1, keepdims=True), figures)
        gene_ref[s * capacity : (s + 1) * capacity, :] = figures
    for m in range(slices):
        block = jnp.concatenate([x[m * capacity : (m + 1) * capacity, :] for x in sorted_slices], axis=0)
        block = block.T.astype(bf16)
        side = slice(m % 2 * LANES, (m % 2 + 1) * LANES)
        if m >= 4:
            e4_ref[(m - 4) // 2 * part : ((m - 4) // 2 + 1) * part, side] = block
        elif m >= 2:
            e2_ref[:, side] = block
        elif m == 1:
            e1_ref[...] = block
        else:
            e0_ref[...] = block


def turn(refs, out_ref):
    samples = refs[0].shape[0]
    half = refs[0].shape[1] // 4
    for c, ref in enumerate(refs):
        for i in range(4):
            out_ref[c * half : (c + 1) * half, i * samples : (i + 1) * samples] = (
                ref[:, i * half : (i + 1) * half].astype(f32).T.astype(bf16)
            )


def line_kernel(vecs_ref, vecs2_ref, *refs):
    *dose_refs, part_ref, turned_scr, dose_scr = refs
    turn((vecs_ref, vecs2_ref), turned_scr)
    samples = dose_refs[0].shape[0]
    for m, ref in enumerate(dose_refs):
        dose_scr[m * samples : (m + 1) * samples, :] = ref[...]
    part_ref[...] = jnp.dot(turned_scr[...], dose_scr[...], preferred_element_type=f32)


def weight_kernel(
    place_ref, kept_ref, kept2_ref, near_ref, near2_ref, expr_ref, expr2_ref, vals_ref, vals2_ref, gene_ref,
    turned_ref, weighted_ref, low_ref, power_ref, data_scr,
):
    samples = kept_ref.shape[0]
    half = vals_ref.shape[1]
    part = samples // 2
    core = place_ref[1]
    turn((near_ref, near2_ref), turned_ref)
    for ref, side in ((expr_ref, core), (expr2_ref, 1 - core)):
        for i in range(8):
            at = i // 4 * 2 * LANES + i % 2 * LANES
            data_scr[pl.ds(pl.multiple_of(i * samples + side * part, part), part), :] = ref[
                i // 2 % 2 * part : (i // 2 % 2 + 1) * part, at : at + LANES
            ]
    data = data_scr[...].astype(f32).T.astype(bf16)
    delta = gene_ref[:, 0:1]
    total = jnp.zeros((data.shape[0], 1), f32)
    sources = ((kept_ref, near_ref, vals_ref), (kept2_ref, near2_ref, vals2_ref))
    for c, (first, second, vals) in enumerate(sources):
        vecs = jnp.concatenate(
            [ref[:, i * half : (i + 1) * half] for ref in (first, second) for i in range(4)], axis=0
        )
        cols = slice(c * half, (c + 1) * half)
        rotated = jnp.dot(data, vecs, preferred_element_type=f32).astype(bf16).astype(f32)
        weight = 1.0 / (vals[...] + delta)
        total += jnp.sum(weight * rotated * rotated, axis=1, keepdims=True)
        weighted_ref[:, cols] = (weight * rotated).astype(bf16)
        low_ref[:, cols] = weight.astype(bf16)
    power_ref[...] = jnp.broadcast_to(total, power_ref.shape)


def score_kernel(place_ref, gene_ref, power_ref, part_ref, turned_ref, weighted_ref, low_ref, *refs):
    *dose_refs, keep_ref, pass_ref, dose_scr = refs
    samples, variants = dose_refs[0].shape
    for m, ref in enumerate(dose_refs):
        dose_scr[m * samples : (m + 1) * samples, :] = ref[...]
    rotated = part_ref[...] + jnp.dot(turned_ref[...], dose_scr[...], preferred_element_type=f32)
    rotated = rotated.astype(bf16)
    squared = jnp.square(rotated.astype(f32)).astype(bf16)
    cross = jnp.dot(weighted_ref[...], rotated, preferred_element_type=f32)
    power = jnp.dot(low_ref[...], squared, preferred_element_type=f32)
    core = place_ref[1]
    start = gene_ref[:, 1:2].astype(jnp.int32)
    valid = gene_ref[:, 2:3].astype(jnp.int32)
    genes = cross.shape[0]
    lane = lax.broadcasted_iota(jnp.int32, (genes, LANES), 1)
    own_power = power_ref[...]
    scale = jnp.sqrt(f32(part_ref.shape[0]))
    blocks = variants // LANES
    for out_ref, half in ((keep_ref, core), (pass_ref, 1 - core)):
        offset = start + half * LANES - core * variants
        block = offset >> 7
        shift = offset & (LANES - 1)
        at = lane + shift
        wrapped = at >= LANES
        at = at & (LANES - 1)
        here = block + wrapped.astype(jnp.int32)
        picked = []
        for array in (cross, power):
            low = jnp.zeros((genes, LANES), f32)
            high = low
            for b in range(blocks):
                part = array[:, b * LANES : (b + 1) * LANES]
                low = jnp.where(block == b, part, low)
                high = jnp.where(block + 1 == b, part, high)
            low = jnp.take_along_axis(low, at, axis=1)
            high = jnp.take_along_axis(high, at, axis=1)
            picked.append(jnp.where(wrapped, high, low))
        live = (here >= 0) & (here < blocks) & (lane + half * LANES < valid)
        score = scale * picked[0] / jnp.sqrt(picked[1] * own_power)
        out_ref[...] = jnp.where(live, score, 0.0)


def call(kernel, outs, count, scratch=(), smem=1, anywhere=0, flops=0):
    vmem = pl.BlockSpec(memory_space=pltpu.VMEM)
    inputs = [pl.BlockSpec(memory_space=pltpu.SMEM)] * smem + [pl.BlockSpec(memory_space=pltpu.HBM)] * anywhere
    return pl.pallas_call(
        kernel,
        out_shape=[jax.ShapeDtypeStruct(*o) for o in outs],
        in_specs=inputs + [vmem] * (count - len(inputs)),
        out_specs=[vmem] * len(outs),
        scratch_shapes=list(scratch),
        compiler_params=pltpu.CompilerParams(vmem_limit_bytes=VMEM_LIMIT),
        cost_estimate=pl.CostEstimate(flops=flops, bytes_accessed=1 << 20, transcendentals=0),
    )


def near_body(eigvecs, eigvals, expression, dosage, delta, window_start, window_valid, gene_owner):
    rows = lax.axis_size("row")
    row = lax.axis_index("row")
    core = lax.axis_index("col")
    panel, half = eigvecs.shape
    part = panel // 2
    line = panel * rows // 2
    vectors = 2 * half
    variants = dosage.shape[1] // 2
    place = jnp.stack([row, core]).astype(jnp.int32)
    ints = (rows, LANES)

    def swap(x, m):
        return lax.ppermute(x, "row", [(i, i ^ m) for i in range(rows)])

    def other_core(x):
        return lax.ppermute(x, "col", [(0, 1), (1, 0)])

    def beside(*xs):
        return jnp.concatenate(xs, axis=1)

    def below(*xs):
        return jnp.concatenate(xs, axis=0)

    dose = {0: lax.dynamic_slice_in_dim(dosage, core * variants, variants, 1)}
    dose[4] = swap(dose[0], 4)
    dose[1] = swap(dose[0], 1)
    dose[2] = swap(dose[0], 2)
    dose[6] = swap(dose[4], 2)
    for m in (4, 2, 6):
        dose[m + 1] = swap(dose[m], 1)
    vals = eigvals[None, :]
    u4 = swap(eigvecs, 4)
    u2 = swap(beside(eigvecs, u4), 2)
    kept = beside(eigvecs, u4, u2)
    near = swap(kept, 1)
    kept2 = other_core(kept)
    near2 = other_core(near)
    e4, e2, e1, e0, gene = call(
        route_kernel,
        [
            ((panel, 2 * LANES), bf16),
            ((part, 2 * LANES), bf16),
            ((part, LANES), bf16),
            ((part, LANES), bf16),
            ((LANES, LANES), f32),
        ],
        6,
        scratch=[
            pltpu.VMEM(ints, jnp.int32),
            pltpu.VMEM(ints, f32),
            pltpu.VMEM(ints, jnp.int32),
            pltpu.VMEM(ints, jnp.int32),
            pltpu.VMEM((part, expression.shape[1]), bf16),
            pltpu.SemaphoreType.DMA((5,)),
        ],
        anywhere=5,
    )(
        place,
        gene_owner.reshape(ints),
        delta.reshape(ints),
        window_start.reshape(ints),
        window_valid.reshape(ints),
        expression,
    )
    r4 = swap(e4, 4)
    r2 = swap(below(e2, r4[part:]), 2)

    def joined(mine, at):
        return below(beside(mine, r4[:part, at : at + LANES]), beside(r2[:part, at : at + LANES], r2[part:, at : at + LANES]))

    data = beside(joined(e0, 0), swap(joined(e1, LANES), 1))
    first = call(
        line_kernel,
        [((vectors, variants), f32)],
        6,
        scratch=[pltpu.VMEM((vectors, line), bf16), pltpu.VMEM((line, variants), bf16)],
        smem=0,
        flops=2 * vectors * line * variants,
    )(kept, kept2, *[dose[m] for m in (0, 4, 2, 6)])[0]
    turned, weighted, low, power = call(
        weight_kernel,
        [((vectors, line), bf16), ((LANES, vectors), bf16), ((LANES, vectors), bf16), ((LANES, LANES), f32)],
        10,
        scratch=[pltpu.VMEM((2 * line, LANES), bf16)],
    )(place, kept, kept2, near, near2, data, other_core(data), vals, other_core(vals), gene)
    keep, passed = call(
        score_kernel,
        [((LANES, LANES), f32)] * 2,
        11,
        scratch=[pltpu.VMEM((line, variants), bf16)],
    )(place, gene, power, first, turned, weighted, low, *[dose[m] for m in (1, 5, 3, 7)])
    return keep + other_core(passed)


def body(eigvecs, eigvals, expression, dosage, delta, window_start, window_valid, gene_owner):
    rows = lax.axis_size("row")
    samples = eigvecs.shape[0] * rows
    own = expression.shape[1] // rows
    fits = (
        lax.axis_size("col") == 2
        and own == LANES
        and W == 2 * LANES
        and rows == 8
        and dosage.shape[1] % (2 * LANES) == 0
        and samples * (samples + dosage.shape[1]) <= VMEM_LIMIT // 16
    )
    run = near_body if fits else wide_body
    return run(eigvecs, eigvals, expression, dosage, delta, window_start, window_valid, gene_owner)


def solution(mesh):
    placed = (
        P(("groups", "row"), "col"),
        P(("groups", "col")),
        P(("groups", "row"), None),
        P(("groups", "row"), None),
        P("groups"),
        P("groups"),
        P("groups"),
        P("groups"),
    )
    return jax.shard_map(
        body, mesh=mesh, in_specs=placed, out_specs=P(("groups", "row"), "col"), check_vma=False
    )
```

```python
import jax
import jax.numpy as jnp
from jax import lax
from jax.experimental import pallas as pl
from jax.experimental.pallas import tpu as pltpu
from jax.sharding import PartitionSpec as P

W = 256
LANES = 128
VMEM_LIMIT = 32 * 1024 * 1024
NT = (((1,), (1,)), ((), ()))
f32 = jnp.float32
bf16 = jnp.bfloat16


def owner_listing(gene_owner):
    total = gene_owner.shape[0]
    return jnp.argsort(gene_owner * total + jnp.arange(total, dtype=jnp.int32))


def earlier_equal(labels):
    places = jnp.arange(labels.shape[0], dtype=jnp.int32)
    same = labels[:, None] == labels[None, :]
    before = places[:, None] > places[None, :]
    return jnp.sum((same & before).astype(jnp.int32), axis=1)


def shift_windows(tables, starts, largest):
    moved_tables = tables
    step_size = 1
    while step_size <= largest:
        bit_set = starts // step_size % 2 == 1
        filler = jnp.zeros(moved_tables.shape[:-1] + (step_size,), moved_tables.dtype)
        moved = jnp.concatenate([moved_tables[..., step_size:], filler], axis=-1)
        moved_tables = jnp.where(bit_set[None, :, None], moved, moved_tables)
        step_size = step_size * 2
    return moved_tables


def wide_body(eigvecs, eigvals, expression, dosage, delta, window_start, window_valid, gene_owner):
    row_count = lax.axis_size("row")
    row_index = lax.axis_index("row")
    genes_all = expression.shape[1]
    own_count = genes_all // row_count
    half_samples = eigvecs.shape[1]
    samples = half_samples * lax.axis_size("col")
    owner_order = owner_listing(gene_owner)
    my_genes = lax.dynamic_slice_in_dim(owner_order, row_index * own_count, own_count)
    expr_panel, dose_panel = (
        lax.all_to_all(expression, "row", split_axis=1, concat_axis=0, tiled=True),
        lax.all_to_all(dosage, "row", split_axis=1, concat_axis=0, tiled=True),
    )
    panel_data = jnp.concatenate([expr_panel, dose_panel], axis=1)
    rotated = lax.dot_general(
        panel_data,
        lax.all_gather(eigvecs, "row", axis=0, tiled=True),
        (((0,), (0,)), ((), ())),
        preferred_element_type=jnp.float32,
    ).astype(jnp.bfloat16)
    rot_expr = rotated[:own_count]
    rot_dose = rotated[own_count:]
    dose_all = lax.all_gather(rot_dose, "row", axis=0, tiled=True)
    capacity = max(2, own_count // row_count)
    destination = lax.dynamic_slice_in_dim(gene_owner, row_index * own_count, own_count)
    position = destination * capacity + earlier_equal(destination)
    slot_ids = jnp.arange(row_count * capacity, dtype=jnp.int32)
    placement_map = (slot_ids[:, None] == position[None, :]).astype(jnp.bfloat16)
    buckets = jnp.dot(placement_map, rot_expr, preferred_element_type=jnp.float32).astype(
        jnp.bfloat16
    )
    received = lax.all_to_all(buckets, "row", split_axis=0, concat_axis=0, tiled=True)
    source = my_genes // own_count
    owned_expr = jnp.take(received, source * capacity + earlier_equal(source), axis=0)
    own_delta = jnp.take(delta, my_genes)
    own_start = jnp.take(window_start, my_genes)
    own_valid = jnp.take(window_valid, my_genes)
    weight = 1.0 / (eigvals[None, :] + own_delta[:, None])
    expr_float = owned_expr.astype(jnp.float32)
    expr_power = jnp.sum(weight * expr_float * expr_float, axis=1)
    weighted = (weight * expr_float).astype(jnp.bfloat16)
    weight_low = weight.astype(jnp.bfloat16)
    dose_sq = jnp.square(dose_all.astype(jnp.float32)).astype(jnp.bfloat16)
    slot_index = jnp.arange(W, dtype=jnp.int32)
    contract = (((1,), (1,)), ((), ()))
    cross_all = lax.dot_general(weighted, dose_all, contract, preferred_element_type=jnp.float32)
    power_all = lax.dot_general(weight_low, dose_sq, contract, preferred_element_type=jnp.float32)
    stacked = jnp.stack([cross_all, power_all], axis=0)
    variants = dose_all.shape[0]
    shifted = shift_windows(stacked, own_start, variants - W)
    cross_sum = shifted[0, :, :W]
    dose_power = shifted[1, :, :W]
    cross_sum, dose_power, expr_power = lax.psum((cross_sum, dose_power, expr_power), "col")
    scale = jnp.sqrt(jnp.float32(samples))
    zscore = jnp.where(
        slot_index[None, :] < own_valid[:, None],
        scale * cross_sum / jnp.sqrt(dose_power * expr_power[:, None]),
        0.0,
    )
    width_part = W // lax.axis_size("col")
    return lax.dynamic_slice_in_dim(zscore, lax.axis_index("col") * width_part, width_part, 1)


def route_kernel(
    place_ref, owner_ref, delta_ref, start_ref, valid_ref, vecs_ref, expr_ref, ahead_ref, e46_ref, e2_ref, e0_ref, gene_ref
):
    slices = owner_ref.shape[0]
    capacity = LANES // slices
    half = vecs_ref.shape[1]
    part = expr_ref.shape[0] // 2
    row, core = place_ref[0], place_ref[1]
    owner = owner_ref[...]
    before = lax.broadcasted_iota(jnp.int32, (LANES, LANES), 0) < lax.broadcasted_iota(
        jnp.int32, (LANES, LANES), 1
    )
    before = before.astype(bf16)
    rank = jnp.zeros(owner.shape, f32)
    for o in range(slices):
        same = (owner == o).astype(f32)
        rank += same * jnp.dot(same.astype(bf16), before, preferred_element_type=f32)
    bucket = (owner ^ row) * capacity + rank.astype(jnp.int32)
    slot = lax.broadcasted_iota(jnp.int32, (LANES, LANES), 0)
    own_slot = lax.broadcasted_iota(jnp.int32, (capacity, LANES), 0)
    lane = lax.broadcasted_iota(jnp.int32, (capacity, LANES), 1)
    rows = pl.ds(pl.multiple_of(core * part, part), part)
    sorted_slices = []
    for s in range(slices):
        here = bucket[s : s + 1, :]
        pick = (slot == here).astype(bf16)
        sorted_slices.append(
            lax.dot_general(pick, expr_ref[rows, s * LANES : (s + 1) * LANES], NT, preferred_element_type=f32)
        )
        mine = (own_slot == here).astype(f32)
        figures = jnp.zeros((capacity, LANES), f32)
        for i, ref in enumerate((delta_ref, start_ref, valid_ref)):
            line = ref[s : s + 1, :].astype(f32)
            figures = jnp.where(lane == i, jnp.sum(mine * line, axis=1, keepdims=True), figures)
        gene_ref[s * capacity : (s + 1) * capacity, :] = figures
    ahead_ref[:, :half] = vecs_ref[...]
    left, right = slice(0, LANES), slice(LANES, 2 * LANES)
    upper, lower = slice(0, part), slice(part, 2 * part)
    targets = {
        0: (e0_ref, upper, left),
        1: (ahead_ref, upper, slice(half, half + LANES)),
        2: (e2_ref, upper, left),
        3: (ahead_ref, upper, slice(half + LANES, half + 2 * LANES)),
        4: (e46_ref, upper, left),
        5: (ahead_ref, lower, slice(half, half + LANES)),
        6: (e46_ref, upper, right),
        7: (ahead_ref, lower, slice(half + LANES, half + 2 * LANES)),
    }
    for m, (ref, down, side) in targets.items():
        block = jnp.concatenate([x[m * capacity : (m + 1) * capacity, :] for x in sorted_slices], axis=0)
        ref[down, side] = block.T.astype(bf16)


def second_kernel(vecs_ref, r1_ref, e46_ref, d4_any, d1_any, out_ref):
    half = vecs_ref.shape[1]
    part = e46_ref.shape[0]
    out_ref[:, :half] = vecs_ref[...]
    out_ref[:, half : 2 * half] = r1_ref[:, :half]
    out_ref[:part, 2 * half :] = e46_ref[...]
    out_ref[part:, 2 * half :] = r1_ref[part:, half:]


def third_kernel(vecs_ref, r1_ref, r4_ref, e2_ref, e0_ref, out_ref, kept_ref):
    half = vecs_ref.shape[1]
    part = e0_ref.shape[0]
    for ref, own, at in ((out_ref, e2_ref, LANES), (kept_ref, e0_ref, 0)):
        ref[:, :half] = vecs_ref[...]
        ref[:, half : 2 * half] = r1_ref[:, :half]
        ref[:, 2 * half : 4 * half] = r4_ref[:, : 2 * half]
        side = slice(2 * half + at, 2 * half + at + LANES)
        left, right = slice(4 * half, 4 * half + LANES), slice(4 * half + LANES, 4 * half + 2 * LANES)
        ref[:part, left] = own[...]
        ref[:part, right] = r1_ref[:part, half + at : half + at + LANES]
        ref[part:, left] = r4_ref[:part, side]
        ref[part:, right] = r4_ref[part:, side]


def pack_kernel(kept_ref, far_ref, vals_ref, out_ref):
    width = kept_ref.shape[1]
    out_ref[:, :width] = kept_ref[...]
    out_ref[:, width : 2 * width] = far_ref[...]
    vals = vals_ref[...]
    high = vals.astype(bf16).astype(f32)
    middle = (vals - high).astype(bf16).astype(f32)
    low = vals - high - middle
    row = lax.broadcasted_iota(jnp.int32, (out_ref.shape[0], vals.shape[1]), 0)
    terms = jnp.where(row == 0, high, jnp.where(row == 1, middle, jnp.where(row == 2, low, 0.0)))
    out_ref[:, 2 * width :] = terms.astype(bf16)


def weight_kernel(place_ref, mine_ref, other_ref, gene_ref, turned_ref, weighted_ref, low_ref, power_ref, data_scr):
    samples = mine_ref.shape[0]
    half = turned_ref.shape[0] // 2
    part = samples // 2
    core = place_ref[1]
    width = 4 * half + 2 * LANES
    panels = [n * width + i * half for n in range(2) for i in range(4)]
    for c, ref in enumerate((mine_ref, other_ref)):
        side = core if c == 0 else 1 - core
        for m, at in enumerate(panels):
            turned_ref[c * half : (c + 1) * half, m * samples : (m + 1) * samples] = (
                ref[:, at : at + half].astype(f32).T.astype(bf16)
            )
            n, i = divmod(m, 4)
            at = n * width + 4 * half + i % 2 * LANES
            data_scr[pl.ds(pl.multiple_of(m * samples + side * part, part), part), :] = ref[
                i // 2 * part : (i // 2 + 1) * part, at : at + LANES
            ]
    data = data_scr[...].astype(f32).T.astype(bf16)
    delta = gene_ref[:, 0:1]
    total = jnp.zeros((data.shape[0], 1), f32)
    for c, ref in enumerate((mine_ref, other_ref)):
        vecs = jnp.concatenate([ref[:, at : at + half] for at in panels], axis=0)
        cols = slice(c * half, (c + 1) * half)
        terms = ref[0:16, 2 * width :].astype(f32)
        vals = terms[0:1] + terms[1:2] + terms[2:3]
        rotated = jnp.dot(data, vecs, preferred_element_type=f32).astype(bf16).astype(f32)
        weight = 1.0 / (vals + delta)
        total += jnp.sum(weight * rotated * rotated, axis=1, keepdims=True)
        weighted_ref[:, cols] = (weight * rotated).astype(bf16)
        low_ref[:, cols] = weight.astype(bf16)
    power_ref[...] = jnp.broadcast_to(total, power_ref.shape)


def score_kernel(place_ref, gene_ref, power_ref, turned_ref, weighted_ref, low_ref, *refs):
    *dose_refs, keep_ref, pass_ref, dose_scr = refs
    samples, variants = dose_refs[0].shape
    chunks = [(ref, at) for ref in dose_refs for at in range(0, ref.shape[1], variants)]
    order = [0, 1, 2, 5, 3, 6, 4, 7]
    for m, (ref, at) in enumerate(chunks[i] for i in order):
        dose_scr[m * samples : (m + 1) * samples, :] = ref[:, at : at + variants]
    rotated = jnp.dot(turned_ref[...], dose_scr[...], preferred_element_type=f32).astype(bf16)
    squared = jnp.square(rotated.astype(f32)).astype(bf16)
    cross = jnp.dot(weighted_ref[...], rotated, preferred_element_type=f32)
    power = jnp.dot(low_ref[...], squared, preferred_element_type=f32)
    core = place_ref[1]
    start = gene_ref[:, 1:2].astype(jnp.int32)
    valid = gene_ref[:, 2:3].astype(jnp.int32)
    genes = cross.shape[0]
    lane = lax.broadcasted_iota(jnp.int32, (genes, LANES), 1)
    own_power = power_ref[...]
    scale = jnp.sqrt(f32(dose_scr.shape[0]))
    blocks = variants // LANES
    for out_ref, half in ((keep_ref, core), (pass_ref, 1 - core)):
        offset = start + half * LANES - core * variants
        block = offset >> 7
        shift = offset & (LANES - 1)
        at = lane + shift
        wrapped = at >= LANES
        at = at & (LANES - 1)
        here = block + wrapped.astype(jnp.int32)
        picked = []
        for array in (cross, power):
            low = jnp.zeros((genes, LANES), f32)
            high = low
            for b in range(blocks):
                part = array[:, b * LANES : (b + 1) * LANES]
                low = jnp.where(block == b, part, low)
                high = jnp.where(block + 1 == b, part, high)
            low = jnp.take_along_axis(low, at, axis=1)
            high = jnp.take_along_axis(high, at, axis=1)
            picked.append(jnp.where(wrapped, high, low))
        live = (here >= 0) & (here < blocks) & (lane + half * LANES < valid)
        score = scale * picked[0] / jnp.sqrt(picked[1] * own_power)
        out_ref[...] = jnp.where(live, score, 0.0)


def call(kernel, outs, count, scratch=(), smem=1, anywhere=0):
    vmem = pl.BlockSpec(memory_space=pltpu.VMEM)
    return pl.pallas_call(
        kernel,
        out_shape=[jax.ShapeDtypeStruct(*o) for o in outs],
        in_specs=[pl.BlockSpec(memory_space=pltpu.SMEM)] * smem + [vmem] * (count - smem - anywhere) + [pl.BlockSpec(memory_space=pl.ANY)] * anywhere,
        out_specs=[vmem] * len(outs),
        scratch_shapes=list(scratch),
        compiler_params=pltpu.CompilerParams(vmem_limit_bytes=VMEM_LIMIT),
    )


def near_body(eigvecs, eigvals, expression, dosage, delta, window_start, window_valid, gene_owner):
    rows = lax.axis_size("row")
    row = lax.axis_index("row")
    core = lax.axis_index("col")
    panel, half = eigvecs.shape
    part = panel // 2
    samples = panel * rows
    variants = dosage.shape[1] // 2
    place = jnp.stack([row, core]).astype(jnp.int32)

    def swap(x, m):
        return lax.ppermute(x, "row", [(i, i ^ m) for i in range(rows)])

    def other_core(x):
        return lax.ppermute(x, "col", [(0, 1), (1, 0)])

    d0 = lax.dynamic_slice_in_dim(dosage, core * variants, variants, 1)
    d4 = swap(d0, 4)
    d1 = swap(d0, 1)
    d26 = swap(jnp.concatenate([d0, d4], axis=1), 2)
    d537 = swap(jnp.concatenate([d4, d26], axis=1), 1)
    ahead, e46, e2, e0, gene = call(
        route_kernel,
        [
            ((panel, half + 2 * LANES), bf16),
            ((part, 2 * LANES), bf16),
            ((part, LANES), bf16),
            ((part, LANES), bf16),
            ((LANES, LANES), f32),
        ],
        7,
    )(
        place,
        gene_owner.reshape(rows, LANES),
        delta.reshape(rows, LANES),
        window_start.reshape(rows, LANES),
        window_valid.reshape(rows, LANES),
        eigvecs,
        expression,
    )
    r1 = swap(ahead, 1)
    r4 = swap(
        call(second_kernel, [((panel, 2 * half + 2 * LANES), bf16)], 5, smem=0, anywhere=2)(eigvecs, r1, e46, d4, d1)[0], 4
    )
    width = 4 * half + 2 * LANES
    out, kept = call(third_kernel, [((panel, width), bf16)] * 2, 5, smem=0)(eigvecs, r1, r4, e2, e0)
    mine = call(pack_kernel, [((panel, 2 * width + half), bf16)], 3, smem=0)(kept, swap(out, 2), eigvals[None, :])[0]
    turned, weighted, low, power = call(
        weight_kernel,
        [((2 * half, samples), bf16), ((LANES, 2 * half), bf16), ((LANES, 2 * half), bf16), ((LANES, LANES), f32)],
        4,
        scratch=[pltpu.VMEM((samples, LANES), bf16)],
    )(place, mine, other_core(mine), gene)
    keep, passed = call(
        score_kernel,
        [((LANES, LANES), f32)] * 2,
        11,
        scratch=[pltpu.VMEM((samples, variants), bf16)],
    )(place, gene, power, turned, weighted, low, d0, d1, d4, d26, d537)
    return keep + other_core(passed)


def body(eigvecs, eigvals, expression, dosage, delta, window_start, window_valid, gene_owner):
    rows = lax.axis_size("row")
    samples = eigvecs.shape[0] * rows
    own = expression.shape[1] // rows
    fits = (
        lax.axis_size("col") == 2
        and own == LANES
        and W == 2 * LANES
        and rows == 8
        and dosage.shape[1] % (2 * LANES) == 0
        and samples * (samples + dosage.shape[1]) <= VMEM_LIMIT // 16
    )
    run = near_body if fits else wide_body
    return run(eigvecs, eigvals, expression, dosage, delta, window_start, window_valid, gene_owner)


def solution(mesh):
    placed = (
        P(("groups", "row"), "col"),
        P(("groups", "col")),
        P(("groups", "row"), None),
        P(("groups", "row"), None),
        P("groups"),
        P("groups"),
        P("groups"),
        P("groups"),
    )
    return jax.shard_map(
        body, mesh=mesh, in_specs=placed, out_specs=P(("groups", "row"), "col"), check_vma=False
    )
```

```python
import jax
import jax.numpy as jnp
from jax import lax
from jax.experimental import pallas as pl
from jax.experimental.pallas import tpu as pltpu
from jax.sharding import PartitionSpec as P

W = 256
LANES = 128
VMEM_LIMIT = 32 * 1024 * 1024
NT = (((1,), (1,)), ((), ()))
f32 = jnp.float32
bf16 = jnp.bfloat16


def owner_listing(gene_owner):
    total = gene_owner.shape[0]
    return jnp.argsort(gene_owner * total + jnp.arange(total, dtype=jnp.int32))


def earlier_equal(labels):
    places = jnp.arange(labels.shape[0], dtype=jnp.int32)
    same = labels[:, None] == labels[None, :]
    before = places[:, None] > places[None, :]
    return jnp.sum((same & before).astype(jnp.int32), axis=1)


def shift_windows(tables, starts, largest):
    moved_tables = tables
    step_size = 1
    while step_size <= largest:
        bit_set = starts // step_size % 2 == 1
        filler = jnp.zeros(moved_tables.shape[:-1] + (step_size,), moved_tables.dtype)
        moved = jnp.concatenate([moved_tables[..., step_size:], filler], axis=-1)
        moved_tables = jnp.where(bit_set[None, :, None], moved, moved_tables)
        step_size = step_size * 2
    return moved_tables


def wide_body(eigvecs, eigvals, expression, dosage, delta, window_start, window_valid, gene_owner):
    row_count = lax.axis_size("row")
    row_index = lax.axis_index("row")
    genes_all = expression.shape[1]
    own_count = genes_all // row_count
    half_samples = eigvecs.shape[1]
    samples = half_samples * lax.axis_size("col")
    owner_order = owner_listing(gene_owner)
    my_genes = lax.dynamic_slice_in_dim(owner_order, row_index * own_count, own_count)
    expr_panel, dose_panel = (
        lax.all_to_all(expression, "row", split_axis=1, concat_axis=0, tiled=True),
        lax.all_to_all(dosage, "row", split_axis=1, concat_axis=0, tiled=True),
    )
    panel_data = jnp.concatenate([expr_panel, dose_panel], axis=1)
    rotated = lax.dot_general(
        panel_data,
        lax.all_gather(eigvecs, "row", axis=0, tiled=True),
        (((0,), (0,)), ((), ())),
        preferred_element_type=jnp.float32,
    ).astype(jnp.bfloat16)
    rot_expr = rotated[:own_count]
    rot_dose = rotated[own_count:]
    dose_all = lax.all_gather(rot_dose, "row", axis=0, tiled=True)
    capacity = max(2, own_count // row_count)
    destination = lax.dynamic_slice_in_dim(gene_owner, row_index * own_count, own_count)
    position = destination * capacity + earlier_equal(destination)
    slot_ids = jnp.arange(row_count * capacity, dtype=jnp.int32)
    placement_map = (slot_ids[:, None] == position[None, :]).astype(jnp.bfloat16)
    buckets = jnp.dot(placement_map, rot_expr, preferred_element_type=jnp.float32).astype(
        jnp.bfloat16
    )
    received = lax.all_to_all(buckets, "row", split_axis=0, concat_axis=0, tiled=True)
    source = my_genes // own_count
    owned_expr = jnp.take(received, source * capacity + earlier_equal(source), axis=0)
    own_delta = jnp.take(delta, my_genes)
    own_start = jnp.take(window_start, my_genes)
    own_valid = jnp.take(window_valid, my_genes)
    weight = 1.0 / (eigvals[None, :] + own_delta[:, None])
    expr_float = owned_expr.astype(jnp.float32)
    expr_power = jnp.sum(weight * expr_float * expr_float, axis=1)
    weighted = (weight * expr_float).astype(jnp.bfloat16)
    weight_low = weight.astype(jnp.bfloat16)
    dose_sq = jnp.square(dose_all.astype(jnp.float32)).astype(jnp.bfloat16)
    slot_index = jnp.arange(W, dtype=jnp.int32)
    contract = (((1,), (1,)), ((), ()))
    cross_all = lax.dot_general(weighted, dose_all, contract, preferred_element_type=jnp.float32)
    power_all = lax.dot_general(weight_low, dose_sq, contract, preferred_element_type=jnp.float32)
    stacked = jnp.stack([cross_all, power_all], axis=0)
    variants = dose_all.shape[0]
    shifted = shift_windows(stacked, own_start, variants - W)
    cross_sum = shifted[0, :, :W]
    dose_power = shifted[1, :, :W]
    cross_sum, dose_power, expr_power = lax.psum((cross_sum, dose_power, expr_power), "col")
    scale = jnp.sqrt(jnp.float32(samples))
    zscore = jnp.where(
        slot_index[None, :] < own_valid[:, None],
        scale * cross_sum / jnp.sqrt(dose_power * expr_power[:, None]),
        0.0,
    )
    width_part = W // lax.axis_size("col")
    return lax.dynamic_slice_in_dim(zscore, lax.axis_index("col") * width_part, width_part, 1)


def route_kernel(
    place_ref, owner_ref, delta_ref, start_ref, valid_ref, vals_ref, vecs_ref, expr_ref,
    ahead_ref, e46_ref, e2_ref, e0_ref, gene_ref, terms_ref,
):
    slices = owner_ref.shape[0]
    capacity = LANES // slices
    half = vecs_ref.shape[1]
    part = expr_ref.shape[0] // 2
    row, core = place_ref[0], place_ref[1]
    owner = owner_ref[...]
    before = lax.broadcasted_iota(jnp.int32, (LANES, LANES), 0) < lax.broadcasted_iota(
        jnp.int32, (LANES, LANES), 1
    )
    before = before.astype(bf16)
    rank = jnp.zeros(owner.shape, f32)
    for o in range(slices):
        same = (owner == o).astype(f32)
        rank += same * jnp.dot(same.astype(bf16), before, preferred_element_type=f32)
    bucket = (owner ^ row) * capacity + rank.astype(jnp.int32)
    slot = lax.broadcasted_iota(jnp.int32, (LANES, LANES), 0)
    own_slot = lax.broadcasted_iota(jnp.int32, (capacity, LANES), 0)
    lane = lax.broadcasted_iota(jnp.int32, (capacity, LANES), 1)
    rows = pl.ds(pl.multiple_of(core * part, part), part)
    sorted_slices = []
    for s in range(slices):
        here = bucket[s : s + 1, :]
        pick = (slot == here).astype(bf16)
        sorted_slices.append(
            lax.dot_general(pick, expr_ref[rows, s * LANES : (s + 1) * LANES], NT, preferred_element_type=f32)
        )
        mine = (own_slot == here).astype(f32)
        figures = jnp.zeros((capacity, LANES), f32)
        for i, ref in enumerate((delta_ref, start_ref, valid_ref)):
            line = ref[s : s + 1, :].astype(f32)
            figures = jnp.where(lane == i, jnp.sum(mine * line, axis=1, keepdims=True), figures)
        gene_ref[s * capacity : (s + 1) * capacity, :] = figures
    vals = vals_ref[...]
    high = vals.astype(bf16).astype(f32)
    middle = (vals - high).astype(bf16).astype(f32)
    term = lax.broadcasted_iota(jnp.int32, terms_ref.shape, 0)
    terms = jnp.where(term == 0, high, jnp.where(term == 1, middle, jnp.where(term == 2, vals - high - middle, 0.0)))
    terms_ref[...] = terms.astype(bf16)
    ahead_ref[:, :half] = vecs_ref[...]
    left, right = slice(0, LANES), slice(LANES, 2 * LANES)
    upper, lower = slice(0, part), slice(part, 2 * part)
    targets = {
        0: (e0_ref, upper, left),
        1: (ahead_ref, upper, slice(half, half + LANES)),
        2: (e2_ref, upper, left),
        3: (ahead_ref, upper, slice(half + LANES, half + 2 * LANES)),
        4: (e46_ref, upper, left),
        5: (ahead_ref, lower, slice(half, half + LANES)),
        6: (e46_ref, upper, right),
        7: (ahead_ref, lower, slice(half + LANES, half + 2 * LANES)),
    }
    for m, (ref, down, side) in targets.items():
        block = jnp.concatenate([x[m * capacity : (m + 1) * capacity, :] for x in sorted_slices], axis=0)
        ref[down, side] = block.T.astype(bf16)


def second_kernel(vecs_ref, r1_ref, e46_ref, d4_any, d1_any, d2_any, out_ref):
    half = vecs_ref.shape[1]
    part = e46_ref.shape[0]
    out_ref[:, :half] = vecs_ref[...]
    out_ref[:, half : 2 * half] = r1_ref[:, :half]
    out_ref[:part, 2 * half :] = e46_ref[...]
    out_ref[part:, 2 * half :] = r1_ref[part:, half:]


def third_kernel(vecs_ref, r1_ref, r4_ref, e2_ref, e0_ref, d6_any, d5_any, d3_any, out_ref, kept_ref):
    half = vecs_ref.shape[1]
    part = e0_ref.shape[0]
    for ref, own, at in ((out_ref, e2_ref, LANES), (kept_ref, e0_ref, 0)):
        ref[:, :half] = vecs_ref[...]
        ref[:, half : 2 * half] = r1_ref[:, :half]
        ref[:, 2 * half : 4 * half] = r4_ref[:, : 2 * half]
        side = slice(2 * half + at, 2 * half + at + LANES)
        left, right = slice(4 * half, 4 * half + LANES), slice(4 * half + LANES, 4 * half + 2 * LANES)
        ref[:part, left] = own[...]
        ref[:part, right] = r1_ref[:part, half + at : half + at + LANES]
        ref[part:, left] = r4_ref[:part, side]
        ref[part:, right] = r4_ref[part:, side]


def pack_kernel(kept_ref, far_ref, terms_ref, d7_any, out_ref):
    width = kept_ref.shape[1]
    out_ref[:, :width] = kept_ref[...]
    out_ref[:, width : 2 * width] = far_ref[...]
    out_ref[: terms_ref.shape[0], 2 * width :] = terms_ref[...]
    out_ref[terms_ref.shape[0] :, 2 * width :] = jnp.zeros_like(out_ref[terms_ref.shape[0] :, 2 * width :])


def weight_kernel(place_ref, mine_ref, other_ref, gene_ref, turned_ref, weighted_ref, low_ref, power_ref, data_scr):
    samples = mine_ref.shape[0]
    half = turned_ref.shape[0] // 2
    part = samples // 2
    core = place_ref[1]
    width = 4 * half + 2 * LANES
    panels = [n * width + i * half for n in range(2) for i in range(4)]
    for c, ref in enumerate((mine_ref, other_ref)):
        side = core if c == 0 else 1 - core
        for m, at in enumerate(panels):
            turned_ref[c * half : (c + 1) * half, m * samples : (m + 1) * samples] = (
                ref[:, at : at + half].astype(f32).T.astype(bf16)
            )
            n, i = divmod(m, 4)
            at = n * width + 4 * half + i % 2 * LANES
            data_scr[pl.ds(pl.multiple_of(m * samples + side * part, part), part), :] = ref[
                i // 2 * part : (i // 2 + 1) * part, at : at + LANES
            ]
    data = data_scr[...].astype(f32).T.astype(bf16)
    delta = gene_ref[:, 0:1]
    total = jnp.zeros((data.shape[0], 1), f32)
    for c, ref in enumerate((mine_ref, other_ref)):
        vecs = jnp.concatenate([ref[:, at : at + half] for at in panels], axis=0)
        cols = slice(c * half, (c + 1) * half)
        terms = ref[0:16, 2 * width :].astype(f32)
        vals = terms[0:1] + terms[1:2] + terms[2:3]
        rotated = jnp.dot(data, vecs, preferred_element_type=f32).astype(bf16).astype(f32)
        weight = 1.0 / (vals + delta)
        total += jnp.sum(weight * rotated * rotated, axis=1, keepdims=True)
        weighted_ref[:, cols] = (weight * rotated).astype(bf16)
        low_ref[:, cols] = weight.astype(bf16)
    power_ref[...] = jnp.broadcast_to(total, power_ref.shape)


def score_kernel(place_ref, gene_ref, power_ref, turned_ref, weighted_ref, low_ref, *refs):
    *dose_refs, keep_ref, pass_ref, dose_scr = refs
    samples, variants = dose_refs[0].shape
    chunks = [(ref, at) for ref in dose_refs for at in range(0, ref.shape[1], variants)]
    order = range(8)
    for m, (ref, at) in enumerate(chunks[i] for i in order):
        dose_scr[m * samples : (m + 1) * samples, :] = ref[:, at : at + variants]
    rotated = jnp.dot(turned_ref[...], dose_scr[...], preferred_element_type=f32).astype(bf16)
    squared = jnp.square(rotated.astype(f32)).astype(bf16)
    cross = jnp.dot(weighted_ref[...], rotated, preferred_element_type=f32)
    power = jnp.dot(low_ref[...], squared, preferred_element_type=f32)
    core = place_ref[1]
    start = gene_ref[:, 1:2].astype(jnp.int32)
    valid = gene_ref[:, 2:3].astype(jnp.int32)
    genes = cross.shape[0]
    lane = lax.broadcasted_iota(jnp.int32, (genes, LANES), 1)
    own_power = power_ref[...]
    scale = jnp.sqrt(f32(dose_scr.shape[0]))
    blocks = variants // LANES
    for out_ref, half in ((keep_ref, core), (pass_ref, 1 - core)):
        offset = start + half * LANES - core * variants
        block = offset >> 7
        shift = offset & (LANES - 1)
        at = lane + shift
        wrapped = at >= LANES
        at = at & (LANES - 1)
        here = block + wrapped.astype(jnp.int32)
        picked = []
        for array in (cross, power):
            low = jnp.zeros((genes, LANES), f32)
            high = low
            for b in range(blocks):
                part = array[:, b * LANES : (b + 1) * LANES]
                low = jnp.where(block == b, part, low)
                high = jnp.where(block + 1 == b, part, high)
            low = jnp.take_along_axis(low, at, axis=1)
            high = jnp.take_along_axis(high, at, axis=1)
            picked.append(jnp.where(wrapped, high, low))
        live = (here >= 0) & (here < blocks) & (lane + half * LANES < valid)
        score = scale * picked[0] / jnp.sqrt(picked[1] * own_power)
        out_ref[...] = jnp.where(live, score, 0.0)


def call(kernel, outs, count, scratch=(), smem=1, anywhere=0):
    vmem = pl.BlockSpec(memory_space=pltpu.VMEM)
    return pl.pallas_call(
        kernel,
        out_shape=[jax.ShapeDtypeStruct(*o) for o in outs],
        in_specs=[pl.BlockSpec(memory_space=pltpu.SMEM)] * smem + [vmem] * (count - smem - anywhere) + [pl.BlockSpec(memory_space=pl.ANY)] * anywhere,
        out_specs=[vmem] * len(outs),
        scratch_shapes=list(scratch),
        compiler_params=pltpu.CompilerParams(vmem_limit_bytes=VMEM_LIMIT),
    )


def near_body(eigvecs, eigvals, expression, dosage, delta, window_start, window_valid, gene_owner):
    rows = lax.axis_size("row")
    row = lax.axis_index("row")
    core = lax.axis_index("col")
    panel, half = eigvecs.shape
    part = panel // 2
    samples = panel * rows
    variants = dosage.shape[1] // 2
    place = jnp.stack([row, core]).astype(jnp.int32)

    def swap(x, m):
        return lax.ppermute(x, "row", [(i, i ^ m) for i in range(rows)])

    def other_core(x):
        return lax.ppermute(x, "col", [(0, 1), (1, 0)])

    d0 = lax.dynamic_slice_in_dim(dosage, core * variants, variants, 1)
    d4 = swap(d0, 4)
    d1 = swap(d0, 1)
    d2 = swap(d0, 2)
    ahead, e46, e2, e0, gene, terms = call(
        route_kernel,
        [
            ((panel, half + 2 * LANES), bf16),
            ((part, 2 * LANES), bf16),
            ((part, LANES), bf16),
            ((part, LANES), bf16),
            ((LANES, LANES), f32),
            ((16, half), bf16),
        ],
        8,
    )(
        place,
        gene_owner.reshape(rows, LANES),
        delta.reshape(rows, LANES),
        window_start.reshape(rows, LANES),
        window_valid.reshape(rows, LANES),
        eigvals[None, :],
        eigvecs,
        expression,
    )
    r1 = swap(ahead, 1)
    r4 = swap(
        call(second_kernel, [((panel, 2 * half + 2 * LANES), bf16)], 6, smem=0, anywhere=3)(
            eigvecs, r1, e46, d4, d1, d2
        )[0],
        4,
    )
    d6 = swap(d4, 2)
    d5 = swap(d4, 1)
    d3 = swap(d2, 1)
    d7 = swap(d6, 1)
    width = 4 * half + 2 * LANES
    out, kept = call(third_kernel, [((panel, width), bf16)] * 2, 8, smem=0, anywhere=3)(
        eigvecs, r1, r4, e2, e0, d6, d5, d3
    )
    mine = call(pack_kernel, [((panel, 2 * width + half), bf16)], 4, smem=0, anywhere=1)(kept, swap(out, 2), terms, d7)[0]
    turned, weighted, low, power = call(
        weight_kernel,
        [((2 * half, samples), bf16), ((LANES, 2 * half), bf16), ((LANES, 2 * half), bf16), ((LANES, LANES), f32)],
        4,
        scratch=[pltpu.VMEM((samples, LANES), bf16)],
    )(place, mine, other_core(mine), gene)
    keep, passed = call(
        score_kernel,
        [((LANES, LANES), f32)] * 2,
        14,
        scratch=[pltpu.VMEM((samples, variants), bf16)],
    )(place, gene, power, turned, weighted, low, d0, d1, d4, d5, d2, d3, d6, d7)
    return keep + other_core(passed)


def body(eigvecs, eigvals, expression, dosage, delta, window_start, window_valid, gene_owner):
    rows = lax.axis_size("row")
    samples = eigvecs.shape[0] * rows
    own = expression.shape[1] // rows
    fits = (
        lax.axis_size("col") == 2
        and own == LANES
        and W == 2 * LANES
        and rows == 8
        and dosage.shape[1] % (2 * LANES) == 0
        and samples * (samples + dosage.shape[1]) <= VMEM_LIMIT // 16
    )
    run = near_body if fits else wide_body
    return run(eigvecs, eigvals, expression, dosage, delta, window_start, window_valid, gene_owner)


def solution(mesh):
    placed = (
        P(("groups", "row"), "col"),
        P(("groups", "col")),
        P(("groups", "row"), None),
        P(("groups", "row"), None),
        P("groups"),
        P("groups"),
        P("groups"),
        P("groups"),
    )
    return jax.shard_map(
        body, mesh=mesh, in_specs=placed, out_specs=P(("groups", "row"), "col"), check_vma=False
    )
```

```python
import jax
import jax.numpy as jnp
from jax import lax
from jax.experimental import pallas as pl
from jax.experimental.pallas import tpu as pltpu
from jax.sharding import PartitionSpec as P

W = 256
LANES = 128
VMEM_LIMIT = 32 * 1024 * 1024
NT = (((1,), (1,)), ((), ()))
f32 = jnp.float32
bf16 = jnp.bfloat16


def owner_listing(gene_owner):
    total = gene_owner.shape[0]
    return jnp.argsort(gene_owner * total + jnp.arange(total, dtype=jnp.int32))


def earlier_equal(labels):
    places = jnp.arange(labels.shape[0], dtype=jnp.int32)
    same = labels[:, None] == labels[None, :]
    before = places[:, None] > places[None, :]
    return jnp.sum((same & before).astype(jnp.int32), axis=1)


def shift_windows(tables, starts, largest):
    moved_tables = tables
    step_size = 1
    while step_size <= largest:
        bit_set = starts // step_size % 2 == 1
        filler = jnp.zeros(moved_tables.shape[:-1] + (step_size,), moved_tables.dtype)
        moved = jnp.concatenate([moved_tables[..., step_size:], filler], axis=-1)
        moved_tables = jnp.where(bit_set[None, :, None], moved, moved_tables)
        step_size = step_size * 2
    return moved_tables


def wide_body(eigvecs, eigvals, expression, dosage, delta, window_start, window_valid, gene_owner):
    row_count = lax.axis_size("row")
    row_index = lax.axis_index("row")
    genes_all = expression.shape[1]
    own_count = genes_all // row_count
    half_samples = eigvecs.shape[1]
    samples = half_samples * lax.axis_size("col")
    owner_order = owner_listing(gene_owner)
    my_genes = lax.dynamic_slice_in_dim(owner_order, row_index * own_count, own_count)
    expr_panel, dose_panel = (
        lax.all_to_all(expression, "row", split_axis=1, concat_axis=0, tiled=True),
        lax.all_to_all(dosage, "row", split_axis=1, concat_axis=0, tiled=True),
    )
    panel_data = jnp.concatenate([expr_panel, dose_panel], axis=1)
    rotated = lax.dot_general(
        panel_data,
        lax.all_gather(eigvecs, "row", axis=0, tiled=True),
        (((0,), (0,)), ((), ())),
        preferred_element_type=jnp.float32,
    ).astype(jnp.bfloat16)
    rot_expr = rotated[:own_count]
    rot_dose = rotated[own_count:]
    dose_all = lax.all_gather(rot_dose, "row", axis=0, tiled=True)
    capacity = max(2, own_count // row_count)
    destination = lax.dynamic_slice_in_dim(gene_owner, row_index * own_count, own_count)
    position = destination * capacity + earlier_equal(destination)
    slot_ids = jnp.arange(row_count * capacity, dtype=jnp.int32)
    placement_map = (slot_ids[:, None] == position[None, :]).astype(jnp.bfloat16)
    buckets = jnp.dot(placement_map, rot_expr, preferred_element_type=jnp.float32).astype(
        jnp.bfloat16
    )
    received = lax.all_to_all(buckets, "row", split_axis=0, concat_axis=0, tiled=True)
    source = my_genes // own_count
    owned_expr = jnp.take(received, source * capacity + earlier_equal(source), axis=0)
    own_delta = jnp.take(delta, my_genes)
    own_start = jnp.take(window_start, my_genes)
    own_valid = jnp.take(window_valid, my_genes)
    weight = 1.0 / (eigvals[None, :] + own_delta[:, None])
    expr_float = owned_expr.astype(jnp.float32)
    expr_power = jnp.sum(weight * expr_float * expr_float, axis=1)
    weighted = (weight * expr_float).astype(jnp.bfloat16)
    weight_low = weight.astype(jnp.bfloat16)
    dose_sq = jnp.square(dose_all.astype(jnp.float32)).astype(jnp.bfloat16)
    slot_index = jnp.arange(W, dtype=jnp.int32)
    contract = (((1,), (1,)), ((), ()))
    cross_all = lax.dot_general(weighted, dose_all, contract, preferred_element_type=jnp.float32)
    power_all = lax.dot_general(weight_low, dose_sq, contract, preferred_element_type=jnp.float32)
    stacked = jnp.stack([cross_all, power_all], axis=0)
    variants = dose_all.shape[0]
    shifted = shift_windows(stacked, own_start, variants - W)
    cross_sum = shifted[0, :, :W]
    dose_power = shifted[1, :, :W]
    cross_sum, dose_power, expr_power = lax.psum((cross_sum, dose_power, expr_power), "col")
    scale = jnp.sqrt(jnp.float32(samples))
    zscore = jnp.where(
        slot_index[None, :] < own_valid[:, None],
        scale * cross_sum / jnp.sqrt(dose_power * expr_power[:, None]),
        0.0,
    )
    width_part = W // lax.axis_size("col")
    return lax.dynamic_slice_in_dim(zscore, lax.axis_index("col") * width_part, width_part, 1)


def route_kernel(
    place_ref, owner_ref, delta_ref, start_ref, valid_ref, vals_ref, vecs_ref, expr_ref, dose_ref,
    ahead_ref, e46_ref, e2_ref, e0_ref, gene_ref, terms_ref, again_ref,
):
    slices = owner_ref.shape[0]
    capacity = LANES // slices
    half = vecs_ref.shape[1]
    part = expr_ref.shape[0] // 2
    row, core = place_ref[0], place_ref[1]
    owner = owner_ref[...]
    before = lax.broadcasted_iota(jnp.int32, (LANES, LANES), 0) < lax.broadcasted_iota(
        jnp.int32, (LANES, LANES), 1
    )
    before = before.astype(bf16)
    rank = jnp.zeros(owner.shape, f32)
    for o in range(slices):
        same = (owner == o).astype(f32)
        rank += same * jnp.dot(same.astype(bf16), before, preferred_element_type=f32)
    bucket = (owner ^ row) * capacity + rank.astype(jnp.int32)
    slot = lax.broadcasted_iota(jnp.int32, (LANES, LANES), 0)
    own_slot = lax.broadcasted_iota(jnp.int32, (capacity, LANES), 0)
    lane = lax.broadcasted_iota(jnp.int32, (capacity, LANES), 1)
    rows = pl.ds(pl.multiple_of(core * part, part), part)
    sorted_slices = []
    for s in range(slices):
        here = bucket[s : s + 1, :]
        pick = (slot == here).astype(bf16)
        sorted_slices.append(
            lax.dot_general(pick, expr_ref[rows, s * LANES : (s + 1) * LANES], NT, preferred_element_type=f32)
        )
        mine = (own_slot == here).astype(f32)
        figures = jnp.zeros((capacity, LANES), f32)
        for i, ref in enumerate((delta_ref, start_ref, valid_ref)):
            line = ref[s : s + 1, :].astype(f32)
            figures = jnp.where(lane == i, jnp.sum(mine * line, axis=1, keepdims=True), figures)
        gene_ref[s * capacity : (s + 1) * capacity, :] = figures
    vals = vals_ref[...]
    high = vals.astype(bf16).astype(f32)
    middle = (vals - high).astype(bf16).astype(f32)
    term = lax.broadcasted_iota(jnp.int32, terms_ref.shape, 0)
    terms = jnp.where(term == 0, high, jnp.where(term == 1, middle, jnp.where(term == 2, vals - high - middle, 0.0)))
    terms_ref[...] = terms.astype(bf16)
    again_ref[...] = dose_ref[...]
    ahead_ref[:, :half] = vecs_ref[...]
    left, right = slice(0, LANES), slice(LANES, 2 * LANES)
    upper, lower = slice(0, part), slice(part, 2 * part)
    targets = {
        0: (e0_ref, upper, left),
        1: (ahead_ref, upper, slice(half, half + LANES)),
        2: (e2_ref, upper, left),
        3: (ahead_ref, upper, slice(half + LANES, half + 2 * LANES)),
        4: (e46_ref, upper, left),
        5: (ahead_ref, lower, slice(half, half + LANES)),
        6: (e46_ref, upper, right),
        7: (ahead_ref, lower, slice(half + LANES, half + 2 * LANES)),
    }
    for m, (ref, down, side) in targets.items():
        block = jnp.concatenate([x[m * capacity : (m + 1) * capacity, :] for x in sorted_slices], axis=0)
        ref[down, side] = block.T.astype(bf16)


def second_kernel(vecs_ref, r1_ref, e46_ref, d0_ref, d4_ref, d2_ref, out_ref, dose_ref, again_ref):
    half = vecs_ref.shape[1]
    part = e46_ref.shape[0]
    variants = d0_ref.shape[1]
    out_ref[:, :half] = vecs_ref[...]
    out_ref[:, half : 2 * half] = r1_ref[:, :half]
    out_ref[:part, 2 * half :] = e46_ref[...]
    out_ref[part:, 2 * half :] = r1_ref[part:, half:]
    for i, ref in enumerate((d0_ref, d4_ref, d2_ref)):
        dose_ref[:, i * variants : (i + 1) * variants] = ref[...]
    again_ref[...] = d4_ref[...]


def third_kernel(vecs_ref, r1_ref, r4_ref, e2_ref, e0_ref, out_ref, kept_ref):
    half = vecs_ref.shape[1]
    part = e0_ref.shape[0]
    for ref, own, at in ((out_ref, e2_ref, LANES), (kept_ref, e0_ref, 0)):
        ref[:, :half] = vecs_ref[...]
        ref[:, half : 2 * half] = r1_ref[:, :half]
        ref[:, 2 * half : 4 * half] = r4_ref[:, : 2 * half]
        side = slice(2 * half + at, 2 * half + at + LANES)
        left, right = slice(4 * half, 4 * half + LANES), slice(4 * half + LANES, 4 * half + 2 * LANES)
        ref[:part, left] = own[...]
        ref[:part, right] = r1_ref[:part, half + at : half + at + LANES]
        ref[part:, left] = r4_ref[:part, side]
        ref[part:, right] = r4_ref[part:, side]


def pack_kernel(kept_ref, far_ref, terms_ref, d153_any, d7_any, out_ref):
    width = kept_ref.shape[1]
    out_ref[:, :width] = kept_ref[...]
    out_ref[:, width : 2 * width] = far_ref[...]
    out_ref[: terms_ref.shape[0], 2 * width :] = terms_ref[...]
    out_ref[terms_ref.shape[0] :, 2 * width :] = jnp.zeros_like(out_ref[terms_ref.shape[0] :, 2 * width :])


def weight_kernel(place_ref, mine_ref, other_ref, gene_ref, turned_ref, weighted_ref, low_ref, power_ref, data_scr):
    samples = mine_ref.shape[0]
    half = turned_ref.shape[0] // 2
    part = samples // 2
    core = place_ref[1]
    width = 4 * half + 2 * LANES
    panels = [n * width + i * half for n in range(2) for i in range(4)]
    for c, ref in enumerate((mine_ref, other_ref)):
        side = core if c == 0 else 1 - core
        for m, at in enumerate(panels):
            turned_ref[c * half : (c + 1) * half, m * samples : (m + 1) * samples] = (
                ref[:, at : at + half].astype(f32).T.astype(bf16)
            )
            n, i = divmod(m, 4)
            at = n * width + 4 * half + i % 2 * LANES
            data_scr[pl.ds(pl.multiple_of(m * samples + side * part, part), part), :] = ref[
                i // 2 * part : (i // 2 + 1) * part, at : at + LANES
            ]
    data = data_scr[...].astype(f32).T.astype(bf16)
    delta = gene_ref[:, 0:1]
    total = jnp.zeros((data.shape[0], 1), f32)
    for c, ref in enumerate((mine_ref, other_ref)):
        vecs = jnp.concatenate([ref[:, at : at + half] for at in panels], axis=0)
        cols = slice(c * half, (c + 1) * half)
        terms = ref[0:16, 2 * width :].astype(f32)
        vals = terms[0:1] + terms[1:2] + terms[2:3]
        rotated = jnp.dot(data, vecs, preferred_element_type=f32).astype(bf16).astype(f32)
        weight = 1.0 / (vals + delta)
        total += jnp.sum(weight * rotated * rotated, axis=1, keepdims=True)
        weighted_ref[:, cols] = (weight * rotated).astype(bf16)
        low_ref[:, cols] = weight.astype(bf16)
    power_ref[...] = jnp.broadcast_to(total, power_ref.shape)


def score_kernel(place_ref, gene_ref, power_ref, turned_ref, weighted_ref, low_ref, *refs):
    *dose_refs, keep_ref, pass_ref, dose_scr = refs
    samples, variants = dose_refs[0].shape
    chunks = [(ref, at) for ref in dose_refs for at in range(0, ref.shape[1], variants)]
    order = [0, 3, 1, 4, 2, 5, 6, 7]
    for m, (ref, at) in enumerate(chunks[i] for i in order):
        dose_scr[m * samples : (m + 1) * samples, :] = ref[:, at : at + variants]
    rotated = jnp.dot(turned_ref[...], dose_scr[...], preferred_element_type=f32).astype(bf16)
    squared = jnp.square(rotated.astype(f32)).astype(bf16)
    cross = jnp.dot(weighted_ref[...], rotated, preferred_element_type=f32)
    power = jnp.dot(low_ref[...], squared, preferred_element_type=f32)
    core = place_ref[1]
    start = gene_ref[:, 1:2].astype(jnp.int32)
    valid = gene_ref[:, 2:3].astype(jnp.int32)
    genes = cross.shape[0]
    lane = lax.broadcasted_iota(jnp.int32, (genes, LANES), 1)
    own_power = power_ref[...]
    scale = jnp.sqrt(f32(dose_scr.shape[0]))
    blocks = variants // LANES
    for out_ref, half in ((keep_ref, core), (pass_ref, 1 - core)):
        offset = start + half * LANES - core * variants
        block = offset >> 7
        shift = offset & (LANES - 1)
        at = lane + shift
        wrapped = at >= LANES
        at = at & (LANES - 1)
        here = block + wrapped.astype(jnp.int32)
        picked = []
        for array in (cross, power):
            low = jnp.zeros((genes, LANES), f32)
            high = low
            for b in range(blocks):
                part = array[:, b * LANES : (b + 1) * LANES]
                low = jnp.where(block == b, part, low)
                high = jnp.where(block + 1 == b, part, high)
            low = jnp.take_along_axis(low, at, axis=1)
            high = jnp.take_along_axis(high, at, axis=1)
            picked.append(jnp.where(wrapped, high, low))
        live = (here >= 0) & (here < blocks) & (lane + half * LANES < valid)
        score = scale * picked[0] / jnp.sqrt(picked[1] * own_power)
        out_ref[...] = jnp.where(live, score, 0.0)


def call(kernel, outs, count, scratch=(), smem=1, anywhere=0):
    vmem = pl.BlockSpec(memory_space=pltpu.VMEM)
    return pl.pallas_call(
        kernel,
        out_shape=[jax.ShapeDtypeStruct(*o) for o in outs],
        in_specs=[pl.BlockSpec(memory_space=pltpu.SMEM)] * smem + [vmem] * (count - smem - anywhere) + [pl.BlockSpec(memory_space=pl.ANY)] * anywhere,
        out_specs=[vmem] * len(outs),
        scratch_shapes=list(scratch),
        compiler_params=pltpu.CompilerParams(vmem_limit_bytes=VMEM_LIMIT),
    )


def near_body(eigvecs, eigvals, expression, dosage, delta, window_start, window_valid, gene_owner):
    rows = lax.axis_size("row")
    row = lax.axis_index("row")
    core = lax.axis_index("col")
    panel, half = eigvecs.shape
    part = panel // 2
    samples = panel * rows
    variants = dosage.shape[1] // 2
    place = jnp.stack([row, core]).astype(jnp.int32)

    def swap(x, m):
        return lax.ppermute(x, "row", [(i, i ^ m) for i in range(rows)])

    def other_core(x):
        return lax.ppermute(x, "col", [(0, 1), (1, 0)])

    d0 = lax.dynamic_slice_in_dim(dosage, core * variants, variants, 1)
    d4 = swap(d0, 4)
    ahead, e46, e2, e0, gene, terms, again = call(
        route_kernel,
        [
            ((panel, half + 2 * LANES), bf16),
            ((part, 2 * LANES), bf16),
            ((part, LANES), bf16),
            ((part, LANES), bf16),
            ((LANES, LANES), f32),
            ((16, half), bf16),
            ((panel, variants), bf16),
        ],
        9,
    )(
        place,
        gene_owner.reshape(rows, LANES),
        delta.reshape(rows, LANES),
        window_start.reshape(rows, LANES),
        window_valid.reshape(rows, LANES),
        eigvals[None, :],
        eigvecs,
        expression,
        d0,
    )
    r1 = swap(ahead, 1)
    d2 = swap(again, 2)
    to4, three, again4 = call(
        second_kernel,
        [((panel, 2 * half + 2 * LANES), bf16), ((panel, 3 * variants), bf16), ((panel, variants), bf16)],
        6,
        smem=0,
    )(eigvecs, r1, e46, d0, d4, d2)
    r4 = swap(to4, 4)
    d6 = swap(again4, 2)
    d153 = swap(three, 1)
    d7 = swap(d6, 1)
    width = 4 * half + 2 * LANES
    out, kept = call(third_kernel, [((panel, width), bf16)] * 2, 5, smem=0)(eigvecs, r1, r4, e2, e0)
    mine = call(pack_kernel, [((panel, 2 * width + half), bf16)], 5, smem=0, anywhere=2)(
        kept, swap(out, 2), terms, d153, d7
    )[0]
    turned, weighted, low, power = call(
        weight_kernel,
        [((2 * half, samples), bf16), ((LANES, 2 * half), bf16), ((LANES, 2 * half), bf16), ((LANES, LANES), f32)],
        4,
        scratch=[pltpu.VMEM((samples, LANES), bf16)],
    )(place, mine, other_core(mine), gene)
    keep, passed = call(
        score_kernel,
        [((LANES, LANES), f32)] * 2,
        12,
        scratch=[pltpu.VMEM((samples, variants), bf16)],
    )(place, gene, power, turned, weighted, low, d0, d4, d2, d153, d6, d7)
    return keep + other_core(passed)


def body(eigvecs, eigvals, expression, dosage, delta, window_start, window_valid, gene_owner):
    rows = lax.axis_size("row")
    samples = eigvecs.shape[0] * rows
    own = expression.shape[1] // rows
    fits = (
        lax.axis_size("col") == 2
        and own == LANES
        and W == 2 * LANES
        and rows == 8
        and dosage.shape[1] % (2 * LANES) == 0
        and samples * (samples + dosage.shape[1]) <= VMEM_LIMIT // 16
    )
    run = near_body if fits else wide_body
    return run(eigvecs, eigvals, expression, dosage, delta, window_start, window_valid, gene_owner)


def solution(mesh):
    placed = (
        P(("groups", "row"), "col"),
        P(("groups", "col")),
        P(("groups", "row"), None),
        P(("groups", "row"), None),
        P("groups"),
        P("groups"),
        P("groups"),
        P("groups"),
    )
    return jax.shard_map(
        body, mesh=mesh, in_specs=placed, out_specs=P(("groups", "row"), "col"), check_vma=False
    )
```

```python
import jax
import jax.numpy as jnp
from jax import lax
from jax.experimental import pallas as pl
from jax.experimental.pallas import tpu as pltpu
from jax.sharding import PartitionSpec as P

W = 256
LANES = 128
VMEM_LIMIT = 32 * 1024 * 1024
NT = (((1,), (1,)), ((), ()))
f32 = jnp.float32
bf16 = jnp.bfloat16


def owner_listing(gene_owner):
    total = gene_owner.shape[0]
    return jnp.argsort(gene_owner * total + jnp.arange(total, dtype=jnp.int32))


def earlier_equal(labels):
    places = jnp.arange(labels.shape[0], dtype=jnp.int32)
    same = labels[:, None] == labels[None, :]
    before = places[:, None] > places[None, :]
    return jnp.sum((same & before).astype(jnp.int32), axis=1)


def shift_windows(tables, starts, largest):
    moved_tables = tables
    step_size = 1
    while step_size <= largest:
        bit_set = starts // step_size % 2 == 1
        filler = jnp.zeros(moved_tables.shape[:-1] + (step_size,), moved_tables.dtype)
        moved = jnp.concatenate([moved_tables[..., step_size:], filler], axis=-1)
        moved_tables = jnp.where(bit_set[None, :, None], moved, moved_tables)
        step_size = step_size * 2
    return moved_tables


def wide_body(eigvecs, eigvals, expression, dosage, delta, window_start, window_valid, gene_owner):
    row_count = lax.axis_size("row")
    row_index = lax.axis_index("row")
    genes_all = expression.shape[1]
    own_count = genes_all // row_count
    half_samples = eigvecs.shape[1]
    samples = half_samples * lax.axis_size("col")
    owner_order = owner_listing(gene_owner)
    my_genes = lax.dynamic_slice_in_dim(owner_order, row_index * own_count, own_count)
    expr_panel, dose_panel = (
        lax.all_to_all(expression, "row", split_axis=1, concat_axis=0, tiled=True),
        lax.all_to_all(dosage, "row", split_axis=1, concat_axis=0, tiled=True),
    )
    panel_data = jnp.concatenate([expr_panel, dose_panel], axis=1)
    rotated = lax.dot_general(
        panel_data,
        lax.all_gather(eigvecs, "row", axis=0, tiled=True),
        (((0,), (0,)), ((), ())),
        preferred_element_type=jnp.float32,
    ).astype(jnp.bfloat16)
    rot_expr = rotated[:own_count]
    rot_dose = rotated[own_count:]
    dose_all = lax.all_gather(rot_dose, "row", axis=0, tiled=True)
    capacity = max(2, own_count // row_count)
    destination = lax.dynamic_slice_in_dim(gene_owner, row_index * own_count, own_count)
    position = destination * capacity + earlier_equal(destination)
    slot_ids = jnp.arange(row_count * capacity, dtype=jnp.int32)
    placement_map = (slot_ids[:, None] == position[None, :]).astype(jnp.bfloat16)
    buckets = jnp.dot(placement_map, rot_expr, preferred_element_type=jnp.float32).astype(
        jnp.bfloat16
    )
    received = lax.all_to_all(buckets, "row", split_axis=0, concat_axis=0, tiled=True)
    source = my_genes // own_count
    owned_expr = jnp.take(received, source * capacity + earlier_equal(source), axis=0)
    own_delta = jnp.take(delta, my_genes)
    own_start = jnp.take(window_start, my_genes)
    own_valid = jnp.take(window_valid, my_genes)
    weight = 1.0 / (eigvals[None, :] + own_delta[:, None])
    expr_float = owned_expr.astype(jnp.float32)
    expr_power = jnp.sum(weight * expr_float * expr_float, axis=1)
    weighted = (weight * expr_float).astype(jnp.bfloat16)
    weight_low = weight.astype(jnp.bfloat16)
    dose_sq = jnp.square(dose_all.astype(jnp.float32)).astype(jnp.bfloat16)
    slot_index = jnp.arange(W, dtype=jnp.int32)
    contract = (((1,), (1,)), ((), ()))
    cross_all = lax.dot_general(weighted, dose_all, contract, preferred_element_type=jnp.float32)
    power_all = lax.dot_general(weight_low, dose_sq, contract, preferred_element_type=jnp.float32)
    stacked = jnp.stack([cross_all, power_all], axis=0)
    variants = dose_all.shape[0]
    shifted = shift_windows(stacked, own_start, variants - W)
    cross_sum = shifted[0, :, :W]
    dose_power = shifted[1, :, :W]
    cross_sum, dose_power, expr_power = lax.psum((cross_sum, dose_power, expr_power), "col")
    scale = jnp.sqrt(jnp.float32(samples))
    zscore = jnp.where(
        slot_index[None, :] < own_valid[:, None],
        scale * cross_sum / jnp.sqrt(dose_power * expr_power[:, None]),
        0.0,
    )
    width_part = W // lax.axis_size("col")
    return lax.dynamic_slice_in_dim(zscore, lax.axis_index("col") * width_part, width_part, 1)


def route_kernel(
    place_ref, owner_ref, delta_ref, start_ref, valid_ref, vals_ref, vecs_ref, expr_ref, dose_ref,
    ahead_ref, e46_ref, e2_ref, e0_ref, gene_ref, terms_ref, again_ref,
):
    slices = owner_ref.shape[0]
    capacity = LANES // slices
    half = vecs_ref.shape[1]
    part = expr_ref.shape[0] // 2
    row, core = place_ref[0], place_ref[1]
    owner = owner_ref[...]
    before = lax.broadcasted_iota(jnp.int32, (LANES, LANES), 0) < lax.broadcasted_iota(
        jnp.int32, (LANES, LANES), 1
    )
    before = before.astype(bf16)
    rank = jnp.zeros(owner.shape, f32)
    for o in range(slices):
        same = (owner == o).astype(f32)
        rank += same * jnp.dot(same.astype(bf16), before, preferred_element_type=f32)
    bucket = (owner ^ row) * capacity + rank.astype(jnp.int32)
    slot = lax.broadcasted_iota(jnp.int32, (LANES, LANES), 0)
    own_slot = lax.broadcasted_iota(jnp.int32, (capacity, LANES), 0)
    lane = lax.broadcasted_iota(jnp.int32, (capacity, LANES), 1)
    rows = pl.ds(pl.multiple_of(core * part, part), part)
    sorted_slices = []
    for s in range(slices):
        here = bucket[s : s + 1, :]
        pick = (slot == here).astype(bf16)
        sorted_slices.append(
            lax.dot_general(pick, expr_ref[rows, s * LANES : (s + 1) * LANES], NT, preferred_element_type=f32)
        )
        mine = (own_slot == here).astype(f32)
        figures = jnp.zeros((capacity, LANES), f32)
        for i, ref in enumerate((delta_ref, start_ref, valid_ref)):
            line = ref[s : s + 1, :].astype(f32)
            figures = jnp.where(lane == i, jnp.sum(mine * line, axis=1, keepdims=True), figures)
        gene_ref[s * capacity : (s + 1) * capacity, :] = figures
    vals = vals_ref[...]
    high = vals.astype(bf16).astype(f32)
    middle = (vals - high).astype(bf16).astype(f32)
    term = lax.broadcasted_iota(jnp.int32, terms_ref.shape, 0)
    terms = jnp.where(term == 0, high, jnp.where(term == 1, middle, jnp.where(term == 2, vals - high - middle, 0.0)))
    terms_ref[...] = terms.astype(bf16)
    again_ref[...] = dose_ref[...]
    ahead_ref[:, :half] = vecs_ref[...]
    left, right = slice(0, LANES), slice(LANES, 2 * LANES)
    upper, lower = slice(0, part), slice(part, 2 * part)
    targets = {
        0: (e0_ref, upper, left),
        1: (ahead_ref, upper, slice(half, half + LANES)),
        2: (e2_ref, upper, left),
        3: (ahead_ref, upper, slice(half + LANES, half + 2 * LANES)),
        4: (e46_ref, upper, left),
        5: (ahead_ref, lower, slice(half, half + LANES)),
        6: (e46_ref, upper, right),
        7: (ahead_ref, lower, slice(half + LANES, half + 2 * LANES)),
    }
    for m, (ref, down, side) in targets.items():
        block = jnp.concatenate([x[m * capacity : (m + 1) * capacity, :] for x in sorted_slices], axis=0)
        ref[down, side] = block.T.astype(bf16)


def second_kernel(vecs_ref, r1_ref, e46_ref, out_ref):
    half = vecs_ref.shape[1]
    part = e46_ref.shape[0]
    out_ref[:, :half] = vecs_ref[...]
    out_ref[:, half : 2 * half] = r1_ref[:, :half]
    out_ref[:part, 2 * half :] = e46_ref[...]
    out_ref[part:, 2 * half :] = r1_ref[part:, half:]


def copy_kernel(dose_ref, after_any, out_ref):
    out_ref[...] = dose_ref[...]


def third_kernel(
    vecs_ref, r1_ref, r4_ref, e2_ref, e0_ref, terms_ref, d4_ref, d2_ref, d6_ref, d1_any, out_ref, kept_ref, dose_ref
):
    half = vecs_ref.shape[1]
    part = e0_ref.shape[0]
    for ref, own, at in ((out_ref, e2_ref, LANES), (kept_ref, e0_ref, 0)):
        ref[:, :half] = vecs_ref[...]
        ref[:, half : 2 * half] = r1_ref[:, :half]
        ref[:, 2 * half : 4 * half] = r4_ref[:, : 2 * half]
        side = slice(2 * half + at, 2 * half + at + LANES)
        left, right = slice(4 * half, 4 * half + LANES), slice(4 * half + LANES, 4 * half + 2 * LANES)
        ref[:part, left] = own[...]
        ref[:part, right] = r1_ref[:part, half + at : half + at + LANES]
        ref[part:, left] = r4_ref[:part, side]
        ref[part:, right] = r4_ref[part:, side]
    width = out_ref.shape[1]
    terms = terms_ref.shape[0]
    kept_ref[:terms, width:] = terms_ref[...]
    kept_ref[terms:, width:] = jnp.zeros((kept_ref.shape[0] - terms, half), bf16)
    variants = d4_ref.shape[1]
    for i, ref in enumerate((d4_ref, d2_ref, d6_ref)):
        dose_ref[:, i * variants : (i + 1) * variants] = ref[...]


def rotate(place_ref, refs, turned_ref, data_scr):
    samples = refs[0].shape[0]
    half = turned_ref.shape[0] // 2
    part = samples // 2
    core = place_ref[1]
    for c, ref in enumerate(refs):
        side = core if c == 0 else 1 - core
        for i in range(4):
            turned_ref[c * half : (c + 1) * half, i * samples : (i + 1) * samples] = (
                ref[:, i * half : (i + 1) * half].astype(f32).T.astype(bf16)
            )
            at = 4 * half + i % 2 * LANES
            data_scr[pl.ds(pl.multiple_of(i * samples + side * part, part), part), :] = ref[
                i // 2 * part : (i // 2 + 1) * part, at : at + LANES
            ]
    data = data_scr[...].astype(f32).T.astype(bf16)
    shares = []
    for ref in refs:
        vecs = jnp.concatenate([ref[:, i * half : (i + 1) * half] for i in range(4)], axis=0)
        shares.append(jnp.dot(data, vecs, preferred_element_type=f32))
    return shares


def half_kernel(place_ref, mine_ref, other_ref, turned_ref, share_ref, data_scr):
    half = turned_ref.shape[0] // 2
    for c, share in enumerate(rotate(place_ref, (mine_ref, other_ref), turned_ref, data_scr)):
        share_ref[:, c * half : (c + 1) * half] = share


def weight_kernel(
    place_ref, kept_ref, kept2_ref, mine_ref, other_ref, share_ref, gene_ref, d537_any,
    turned_ref, weighted_ref, low_ref, power_ref, data_scr,
):
    half = turned_ref.shape[0] // 2
    delta = gene_ref[:, 0:1]
    total = jnp.zeros((delta.shape[0], 1), f32)
    shares = rotate(place_ref, (mine_ref, other_ref), turned_ref, data_scr)
    width = mine_ref.shape[1]
    for c, (share, ref) in enumerate(zip(shares, (kept_ref, kept2_ref))):
        cols = slice(c * half, (c + 1) * half)
        terms = ref[0:16, width:].astype(f32)
        vals = terms[0:1] + terms[1:2] + terms[2:3]
        rotated = (share_ref[:, cols] + share).astype(bf16).astype(f32)
        weight = 1.0 / (vals + delta)
        total += jnp.sum(weight * rotated * rotated, axis=1, keepdims=True)
        weighted_ref[:, cols] = (weight * rotated).astype(bf16)
        low_ref[:, cols] = weight.astype(bf16)
    power_ref[...] = jnp.broadcast_to(total, power_ref.shape)


def score_kernel(place_ref, gene_ref, power_ref, turned_ref, turned2_ref, weighted_ref, low_ref, *refs):
    *dose_refs, keep_ref, pass_ref, dose_scr = refs
    samples, variants = dose_refs[0].shape
    chunks = [(ref, at) for ref in dose_refs for at in range(0, ref.shape[1], variants)]
    order = [0, 1, 2, 3, 6, 4, 7, 5]
    for m, (ref, at) in enumerate(chunks[i] for i in order):
        dose_scr[m * samples : (m + 1) * samples, :] = ref[:, at : at + variants]
    line = turned_ref.shape[1]
    rotated = jnp.dot(turned_ref[...], dose_scr[:line], preferred_element_type=f32)
    rotated += jnp.dot(turned2_ref[...], dose_scr[line:], preferred_element_type=f32)
    rotated = rotated.astype(bf16)
    squared = jnp.square(rotated.astype(f32)).astype(bf16)
    cross = jnp.dot(weighted_ref[...], rotated, preferred_element_type=f32)
    power = jnp.dot(low_ref[...], squared, preferred_element_type=f32)
    core = place_ref[1]
    start = gene_ref[:, 1:2].astype(jnp.int32)
    valid = gene_ref[:, 2:3].astype(jnp.int32)
    genes = cross.shape[0]
    lane = lax.broadcasted_iota(jnp.int32, (genes, LANES), 1)
    own_power = power_ref[...]
    scale = jnp.sqrt(f32(dose_scr.shape[0]))
    blocks = variants // LANES
    for out_ref, half in ((keep_ref, core), (pass_ref, 1 - core)):
        offset = start + half * LANES - core * variants
        block = offset >> 7
        shift = offset & (LANES - 1)
        at = lane + shift
        wrapped = at >= LANES
        at = at & (LANES - 1)
        here = block + wrapped.astype(jnp.int32)
        picked = []
        for array in (cross, power):
            low = jnp.zeros((genes, LANES), f32)
            high = low
            for b in range(blocks):
                part = array[:, b * LANES : (b + 1) * LANES]
                low = jnp.where(block == b, part, low)
                high = jnp.where(block + 1 == b, part, high)
            low = jnp.take_along_axis(low, at, axis=1)
            high = jnp.take_along_axis(high, at, axis=1)
            picked.append(jnp.where(wrapped, high, low))
        live = (here >= 0) & (here < blocks) & (lane + half * LANES < valid)
        score = scale * picked[0] / jnp.sqrt(picked[1] * own_power)
        out_ref[...] = jnp.where(live, score, 0.0)


def call(kernel, outs, count, scratch=(), smem=1, anywhere=0):
    vmem = pl.BlockSpec(memory_space=pltpu.VMEM)
    return pl.pallas_call(
        kernel,
        out_shape=[jax.ShapeDtypeStruct(*o) for o in outs],
        in_specs=[pl.BlockSpec(memory_space=pltpu.SMEM)] * smem + [vmem] * (count - smem - anywhere) + [pl.BlockSpec(memory_space=pl.ANY)] * anywhere,
        out_specs=[vmem] * len(outs),
        scratch_shapes=list(scratch),
        compiler_params=pltpu.CompilerParams(vmem_limit_bytes=VMEM_LIMIT),
    )


def near_body(eigvecs, eigvals, expression, dosage, delta, window_start, window_valid, gene_owner):
    rows = lax.axis_size("row")
    row = lax.axis_index("row")
    core = lax.axis_index("col")
    panel, half = eigvecs.shape
    part = panel // 2
    samples = panel * rows
    variants = dosage.shape[1] // 2
    place = jnp.stack([row, core]).astype(jnp.int32)

    def swap(x, m):
        return lax.ppermute(x, "row", [(i, i ^ m) for i in range(rows)])

    def other_core(x):
        return lax.ppermute(x, "col", [(0, 1), (1, 0)])

    d0 = lax.dynamic_slice_in_dim(dosage, core * variants, variants, 1)
    d4 = swap(d0, 4)
    ahead, e46, e2, e0, gene, terms, again = call(
        route_kernel,
        [
            ((panel, half + 2 * LANES), bf16),
            ((part, 2 * LANES), bf16),
            ((part, LANES), bf16),
            ((part, LANES), bf16),
            ((LANES, LANES), f32),
            ((16, half), bf16),
            ((panel, variants), bf16),
        ],
        9,
    )(
        place,
        gene_owner.reshape(rows, LANES),
        delta.reshape(rows, LANES),
        window_start.reshape(rows, LANES),
        window_valid.reshape(rows, LANES),
        eigvals[None, :],
        eigvecs,
        expression,
        d0,
    )
    r1 = swap(ahead, 1)
    d2 = swap(again, 2)
    d1 = swap(again, 1)
    to4 = call(second_kernel, [((panel, 2 * half + 2 * LANES), bf16)], 3, smem=0)(eigvecs, r1, e46)[0]
    r4 = swap(to4, 4)
    d6 = swap(call(copy_kernel, [((panel, variants), bf16)], 2, smem=0, anywhere=1)(d4, to4)[0], 2)
    width = 4 * half + 2 * LANES
    out, kept, three = call(
        third_kernel,
        [((panel, width), bf16), ((panel, width + half), bf16), ((panel, 3 * variants), bf16)],
        10,
        smem=0,
        anywhere=1,
    )(eigvecs, r1, r4, e2, e0, terms, d4, d2, d6, d1)
    d537 = swap(three, 1)
    kept2 = other_core(kept)
    near = swap(out, 2)
    near2 = other_core(near)
    shape = ((2 * half, samples // 2), bf16)
    turned, share = call(
        half_kernel,
        [shape, ((LANES, 2 * half), f32)],
        3,
        scratch=[pltpu.VMEM((samples // 2, LANES), bf16)],
    )(place, kept, kept2)
    turned2, weighted, low, power = call(
        weight_kernel,
        [shape, ((LANES, 2 * half), bf16), ((LANES, 2 * half), bf16), ((LANES, LANES), f32)],
        8,
        scratch=[pltpu.VMEM((samples // 2, LANES), bf16)],
        anywhere=1,
    )(place, kept, kept2, near, near2, share, gene, d537)
    keep, passed = call(
        score_kernel,
        [((LANES, LANES), f32)] * 2,
        13,
        scratch=[pltpu.VMEM((samples, variants), bf16)],
    )(place, gene, power, turned, turned2, weighted, low, d0, d1, d4, d537, d2, d6)
    return keep + other_core(passed)


def body(eigvecs, eigvals, expression, dosage, delta, window_start, window_valid, gene_owner):
    rows = lax.axis_size("row")
    samples = eigvecs.shape[0] * rows
    own = expression.shape[1] // rows
    fits = (
        lax.axis_size("col") == 2
        and own == LANES
        and W == 2 * LANES
        and rows == 8
        and dosage.shape[1] % (2 * LANES) == 0
        and samples * (samples + dosage.shape[1]) <= VMEM_LIMIT // 16
    )
    run = near_body if fits else wide_body
    return run(eigvecs, eigvals, expression, dosage, delta, window_start, window_valid, gene_owner)


def solution(mesh):
    placed = (
        P(("groups", "row"), "col"),
        P(("groups", "col")),
        P(("groups", "row"), None),
        P(("groups", "row"), None),
        P("groups"),
        P("groups"),
        P("groups"),
        P("groups"),
    )
    return jax.shard_map(
        body, mesh=mesh, in_specs=placed, out_specs=P(("groups", "row"), "col"), check_vma=False
    )
```

```python
import jax
import jax.numpy as jnp
from jax import lax
from jax.experimental import pallas as pl
from jax.experimental.pallas import tpu as pltpu
from jax.sharding import PartitionSpec as P

W = 256
LANES = 128
VMEM_LIMIT = 32 * 1024 * 1024
NT = (((1,), (1,)), ((), ()))
f32 = jnp.float32
bf16 = jnp.bfloat16


def owner_listing(gene_owner):
    total = gene_owner.shape[0]
    return jnp.argsort(gene_owner * total + jnp.arange(total, dtype=jnp.int32))


def earlier_equal(labels):
    places = jnp.arange(labels.shape[0], dtype=jnp.int32)
    same = labels[:, None] == labels[None, :]
    before = places[:, None] > places[None, :]
    return jnp.sum((same & before).astype(jnp.int32), axis=1)


def shift_windows(tables, starts, largest):
    moved_tables = tables
    step_size = 1
    while step_size <= largest:
        bit_set = starts // step_size % 2 == 1
        filler = jnp.zeros(moved_tables.shape[:-1] + (step_size,), moved_tables.dtype)
        moved = jnp.concatenate([moved_tables[..., step_size:], filler], axis=-1)
        moved_tables = jnp.where(bit_set[None, :, None], moved, moved_tables)
        step_size = step_size * 2
    return moved_tables


def wide_body(eigvecs, eigvals, expression, dosage, delta, window_start, window_valid, gene_owner):
    row_count = lax.axis_size("row")
    row_index = lax.axis_index("row")
    genes_all = expression.shape[1]
    own_count = genes_all // row_count
    half_samples = eigvecs.shape[1]
    samples = half_samples * lax.axis_size("col")
    owner_order = owner_listing(gene_owner)
    my_genes = lax.dynamic_slice_in_dim(owner_order, row_index * own_count, own_count)
    expr_panel, dose_panel = (
        lax.all_to_all(expression, "row", split_axis=1, concat_axis=0, tiled=True),
        lax.all_to_all(dosage, "row", split_axis=1, concat_axis=0, tiled=True),
    )
    panel_data = jnp.concatenate([expr_panel, dose_panel], axis=1)
    rotated = lax.dot_general(
        panel_data,
        lax.all_gather(eigvecs, "row", axis=0, tiled=True),
        (((0,), (0,)), ((), ())),
        preferred_element_type=jnp.float32,
    ).astype(jnp.bfloat16)
    rot_expr = rotated[:own_count]
    rot_dose = rotated[own_count:]
    dose_all = lax.all_gather(rot_dose, "row", axis=0, tiled=True)
    capacity = max(2, own_count // row_count)
    destination = lax.dynamic_slice_in_dim(gene_owner, row_index * own_count, own_count)
    position = destination * capacity + earlier_equal(destination)
    slot_ids = jnp.arange(row_count * capacity, dtype=jnp.int32)
    placement_map = (slot_ids[:, None] == position[None, :]).astype(jnp.bfloat16)
    buckets = jnp.dot(placement_map, rot_expr, preferred_element_type=jnp.float32).astype(
        jnp.bfloat16
    )
    received = lax.all_to_all(buckets, "row", split_axis=0, concat_axis=0, tiled=True)
    source = my_genes // own_count
    owned_expr = jnp.take(received, source * capacity + earlier_equal(source), axis=0)
    own_delta = jnp.take(delta, my_genes)
    own_start = jnp.take(window_start, my_genes)
    own_valid = jnp.take(window_valid, my_genes)
    weight = 1.0 / (eigvals[None, :] + own_delta[:, None])
    expr_float = owned_expr.astype(jnp.float32)
    expr_power = jnp.sum(weight * expr_float * expr_float, axis=1)
    weighted = (weight * expr_float).astype(jnp.bfloat16)
    weight_low = weight.astype(jnp.bfloat16)
    dose_sq = jnp.square(dose_all.astype(jnp.float32)).astype(jnp.bfloat16)
    slot_index = jnp.arange(W, dtype=jnp.int32)
    contract = (((1,), (1,)), ((), ()))
    cross_all = lax.dot_general(weighted, dose_all, contract, preferred_element_type=jnp.float32)
    power_all = lax.dot_general(weight_low, dose_sq, contract, preferred_element_type=jnp.float32)
    stacked = jnp.stack([cross_all, power_all], axis=0)
    variants = dose_all.shape[0]
    shifted = shift_windows(stacked, own_start, variants - W)
    cross_sum = shifted[0, :, :W]
    dose_power = shifted[1, :, :W]
    cross_sum, dose_power, expr_power = lax.psum((cross_sum, dose_power, expr_power), "col")
    scale = jnp.sqrt(jnp.float32(samples))
    zscore = jnp.where(
        slot_index[None, :] < own_valid[:, None],
        scale * cross_sum / jnp.sqrt(dose_power * expr_power[:, None]),
        0.0,
    )
    width_part = W // lax.axis_size("col")
    return lax.dynamic_slice_in_dim(zscore, lax.axis_index("col") * width_part, width_part, 1)


def route_kernel(
    place_ref, owner_ref, delta_ref, start_ref, valid_ref, vals_ref, vecs_ref, expr_ref, dose_ref,
    ahead_ref, e46_ref, e2_ref, e0_ref, gene_ref, terms_ref, again_ref,
):
    slices = owner_ref.shape[0]
    capacity = LANES // slices
    half = vecs_ref.shape[1]
    part = expr_ref.shape[0] // 2
    row, core = place_ref[0], place_ref[1]
    owner = owner_ref[...]
    before = lax.broadcasted_iota(jnp.int32, (LANES, LANES), 0) < lax.broadcasted_iota(
        jnp.int32, (LANES, LANES), 1
    )
    before = before.astype(bf16)
    rank = jnp.zeros(owner.shape, f32)
    for o in range(slices):
        same = (owner == o).astype(f32)
        rank += same * jnp.dot(same.astype(bf16), before, preferred_element_type=f32)
    bucket = (owner ^ row) * capacity + rank.astype(jnp.int32)
    slot = lax.broadcasted_iota(jnp.int32, (LANES, LANES), 0)
    own_slot = lax.broadcasted_iota(jnp.int32, (capacity, LANES), 0)
    lane = lax.broadcasted_iota(jnp.int32, (capacity, LANES), 1)
    rows = pl.ds(pl.multiple_of(core * part, part), part)
    sorted_slices = []
    for s in range(slices):
        here = bucket[s : s + 1, :]
        pick = (slot == here).astype(bf16)
        sorted_slices.append(
            lax.dot_general(pick, expr_ref[rows, s * LANES : (s + 1) * LANES], NT, preferred_element_type=f32)
        )
        mine = (own_slot == here).astype(f32)
        figures = jnp.zeros((capacity, LANES), f32)
        for i, ref in enumerate((delta_ref, start_ref, valid_ref)):
            line = ref[s : s + 1, :].astype(f32)
            figures = jnp.where(lane == i, jnp.sum(mine * line, axis=1, keepdims=True), figures)
        gene_ref[s * capacity : (s + 1) * capacity, :] = figures
    vals = vals_ref[...]
    high = vals.astype(bf16).astype(f32)
    middle = (vals - high).astype(bf16).astype(f32)
    term = lax.broadcasted_iota(jnp.int32, terms_ref.shape, 0)
    terms = jnp.where(term == 0, high, jnp.where(term == 1, middle, jnp.where(term == 2, vals - high - middle, 0.0)))
    terms_ref[...] = terms.astype(bf16)
    again_ref[...] = dose_ref[...]
    ahead_ref[:, :half] = vecs_ref[...]
    left, right = slice(0, LANES), slice(LANES, 2 * LANES)
    upper, lower = slice(0, part), slice(part, 2 * part)
    targets = {
        0: (e0_ref, upper, left),
        1: (ahead_ref, upper, slice(half, half + LANES)),
        2: (e2_ref, upper, left),
        3: (ahead_ref, upper, slice(half + LANES, half + 2 * LANES)),
        4: (e46_ref, upper, left),
        5: (ahead_ref, lower, slice(half, half + LANES)),
        6: (e46_ref, upper, right),
        7: (ahead_ref, lower, slice(half + LANES, half + 2 * LANES)),
    }
    for m, (ref, down, side) in targets.items():
        block = jnp.concatenate([x[m * capacity : (m + 1) * capacity, :] for x in sorted_slices], axis=0)
        ref[down, side] = block.T.astype(bf16)


def second_kernel(vecs_ref, r1_ref, e46_ref, out_ref):
    half = vecs_ref.shape[1]
    part = e46_ref.shape[0]
    out_ref[:, :half] = vecs_ref[...]
    out_ref[:, half : 2 * half] = r1_ref[:, :half]
    out_ref[:part, 2 * half :] = e46_ref[...]
    out_ref[part:, 2 * half :] = r1_ref[part:, half:]


def copy_kernel(d0_ref, d4_ref, after_any, own_ref, far_ref):
    own_ref[...] = d0_ref[...]
    far_ref[...] = d4_ref[...]


def third_kernel(
    vecs_ref, r1_ref, r4_ref, e2_ref, e0_ref, terms_ref, d4_ref, d2_ref, d6_ref, d1_any, out_ref, kept_ref, dose_ref
):
    half = vecs_ref.shape[1]
    part = e0_ref.shape[0]
    for ref, own, at in ((out_ref, e2_ref, LANES), (kept_ref, e0_ref, 0)):
        ref[:, :half] = vecs_ref[...]
        ref[:, half : 2 * half] = r1_ref[:, :half]
        ref[:, 2 * half : 4 * half] = r4_ref[:, : 2 * half]
        side = slice(2 * half + at, 2 * half + at + LANES)
        left, right = slice(4 * half, 4 * half + LANES), slice(4 * half + LANES, 4 * half + 2 * LANES)
        ref[:part, left] = own[...]
        ref[:part, right] = r1_ref[:part, half + at : half + at + LANES]
        ref[part:, left] = r4_ref[:part, side]
        ref[part:, right] = r4_ref[part:, side]
    width = out_ref.shape[1]
    terms = terms_ref.shape[0]
    kept_ref[:terms, width:] = terms_ref[...]
    kept_ref[terms:, width:] = jnp.zeros((kept_ref.shape[0] - terms, half), bf16)
    variants = d4_ref.shape[1]
    for i, ref in enumerate((d4_ref, d2_ref, d6_ref)):
        dose_ref[:, i * variants : (i + 1) * variants] = ref[...]


def rotate(place_ref, refs, turned_ref, data_scr):
    samples = refs[0].shape[0]
    half = turned_ref.shape[0] // 2
    part = samples // 2
    core = place_ref[1]
    for c, ref in enumerate(refs):
        side = core if c == 0 else 1 - core
        for i in range(4):
            turned_ref[c * half : (c + 1) * half, i * samples : (i + 1) * samples] = (
                ref[:, i * half : (i + 1) * half].astype(f32).T.astype(bf16)
            )
            at = 4 * half + i % 2 * LANES
            data_scr[pl.ds(pl.multiple_of(i * samples + side * part, part), part), :] = ref[
                i // 2 * part : (i // 2 + 1) * part, at : at + LANES
            ]
    data = data_scr[...].astype(f32).T.astype(bf16)
    shares = []
    for ref in refs:
        vecs = jnp.concatenate([ref[:, i * half : (i + 1) * half] for i in range(4)], axis=0)
        shares.append(jnp.dot(data, vecs, preferred_element_type=f32))
    return shares


def half_kernel(place_ref, mine_ref, other_ref, turned_ref, share_ref, data_scr):
    half = turned_ref.shape[0] // 2
    for c, share in enumerate(rotate(place_ref, (mine_ref, other_ref), turned_ref, data_scr)):
        share_ref[:, c * half : (c + 1) * half] = share


def weight_kernel(
    place_ref, kept_ref, kept2_ref, mine_ref, other_ref, share_ref, gene_ref,
    turned_ref, weighted_ref, low_ref, power_ref, data_scr,
):
    half = turned_ref.shape[0] // 2
    delta = gene_ref[:, 0:1]
    total = jnp.zeros((delta.shape[0], 1), f32)
    shares = rotate(place_ref, (mine_ref, other_ref), turned_ref, data_scr)
    width = mine_ref.shape[1]
    for c, (share, ref) in enumerate(zip(shares, (kept_ref, kept2_ref))):
        cols = slice(c * half, (c + 1) * half)
        terms = ref[0:16, width:].astype(f32)
        vals = terms[0:1] + terms[1:2] + terms[2:3]
        rotated = (share_ref[:, cols] + share).astype(bf16).astype(f32)
        weight = 1.0 / (vals + delta)
        total += jnp.sum(weight * rotated * rotated, axis=1, keepdims=True)
        weighted_ref[:, cols] = (weight * rotated).astype(bf16)
        low_ref[:, cols] = weight.astype(bf16)
    power_ref[...] = jnp.broadcast_to(total, power_ref.shape)


def score_kernel(place_ref, gene_ref, power_ref, turned_ref, turned2_ref, weighted_ref, low_ref, *refs):
    *dose_refs, keep_ref, pass_ref, dose_scr = refs
    samples, variants = dose_refs[0].shape
    chunks = [(ref, at) for ref in dose_refs for at in range(0, ref.shape[1], variants)]
    order = [0, 1, 2, 3, 6, 4, 7, 5]
    for m, (ref, at) in enumerate(chunks[i] for i in order):
        dose_scr[m * samples : (m + 1) * samples, :] = ref[:, at : at + variants]
    line = turned_ref.shape[1]
    rotated = jnp.dot(turned_ref[...], dose_scr[:line], preferred_element_type=f32)
    rotated += jnp.dot(turned2_ref[...], dose_scr[line:], preferred_element_type=f32)
    rotated = rotated.astype(bf16)
    squared = jnp.square(rotated.astype(f32)).astype(bf16)
    cross = jnp.dot(weighted_ref[...], rotated, preferred_element_type=f32)
    power = jnp.dot(low_ref[...], squared, preferred_element_type=f32)
    core = place_ref[1]
    start = gene_ref[:, 1:2].astype(jnp.int32)
    valid = gene_ref[:, 2:3].astype(jnp.int32)
    genes = cross.shape[0]
    lane = lax.broadcasted_iota(jnp.int32, (genes, LANES), 1)
    own_power = power_ref[...]
    scale = jnp.sqrt(f32(dose_scr.shape[0]))
    blocks = variants // LANES
    for out_ref, half in ((keep_ref, core), (pass_ref, 1 - core)):
        offset = start + half * LANES - core * variants
        block = offset >> 7
        shift = offset & (LANES - 1)
        need = block + (lane < shift).astype(jnp.int32)
        products = [jnp.zeros((genes, LANES), f32)] * 2
        for b in range(blocks):
            here = need == b
            parts = [array[:, b * LANES : (b + 1) * LANES] for array in (cross, power)]
            products = [jnp.where(here, part, product) for part, product in zip(parts, products)]
        inside = (need >= 0) & (need < blocks)
        score = jnp.where(inside, scale * products[0] / jnp.sqrt(products[1] * own_power), 0.0)
        score = jnp.take_along_axis(score, (lane + shift) & (LANES - 1), axis=1)
        out_ref[...] = jnp.where(lane + half * LANES < valid, score, 0.0)


def call(kernel, outs, count, scratch=(), smem=1, anywhere=0):
    vmem = pl.BlockSpec(memory_space=pltpu.VMEM)
    return pl.pallas_call(
        kernel,
        out_shape=[jax.ShapeDtypeStruct(*o) for o in outs],
        in_specs=[pl.BlockSpec(memory_space=pltpu.SMEM)] * smem + [vmem] * (count - smem - anywhere) + [pl.BlockSpec(memory_space=pl.ANY)] * anywhere,
        out_specs=[vmem] * len(outs),
        scratch_shapes=list(scratch),
        compiler_params=pltpu.CompilerParams(vmem_limit_bytes=VMEM_LIMIT),
    )


def near_body(eigvecs, eigvals, expression, dosage, delta, window_start, window_valid, gene_owner):
    rows = lax.axis_size("row")
    row = lax.axis_index("row")
    core = lax.axis_index("col")
    panel, half = eigvecs.shape
    part = panel // 2
    samples = panel * rows
    variants = dosage.shape[1] // 2
    place = jnp.stack([row, core]).astype(jnp.int32)

    def swap(x, m):
        return lax.ppermute(x, "row", [(i, i ^ m) for i in range(rows)])

    def other_core(x):
        return lax.ppermute(x, "col", [(0, 1), (1, 0)])

    d0 = lax.dynamic_slice_in_dim(dosage, core * variants, variants, 1)
    d4 = swap(d0, 4)
    ahead, e46, e2, e0, gene, terms, again = call(
        route_kernel,
        [
            ((panel, half + 2 * LANES), bf16),
            ((part, 2 * LANES), bf16),
            ((part, LANES), bf16),
            ((part, LANES), bf16),
            ((LANES, LANES), f32),
            ((16, half), bf16),
            ((panel, variants), bf16),
        ],
        9,
    )(
        place,
        gene_owner.reshape(rows, LANES),
        delta.reshape(rows, LANES),
        window_start.reshape(rows, LANES),
        window_valid.reshape(rows, LANES),
        eigvals[None, :],
        eigvecs,
        expression,
        d0,
    )
    r1 = swap(ahead, 1)
    d2 = swap(again, 2)
    to4 = call(second_kernel, [((panel, 2 * half + 2 * LANES), bf16)], 3, smem=0)(eigvecs, r1, e46)[0]
    r4 = swap(to4, 4)
    own, far = call(copy_kernel, [((panel, variants), bf16)] * 2, 3, smem=0, anywhere=1)(d0, d4, to4)
    d6 = swap(far, 2)
    d1 = swap(own, 1)
    width = 4 * half + 2 * LANES
    out, kept, three = call(
        third_kernel,
        [((panel, width), bf16), ((panel, width + half), bf16), ((panel, 3 * variants), bf16)],
        10,
        smem=0,
        anywhere=1,
    )(eigvecs, r1, r4, e2, e0, terms, d4, d2, d6, d1)
    d537 = swap(three, 1)
    kept2 = other_core(kept)
    near = swap(out, 2)
    near2 = other_core(near)
    shape = ((2 * half, samples // 2), bf16)
    turned, share = call(
        half_kernel,
        [shape, ((LANES, 2 * half), f32)],
        3,
        scratch=[pltpu.VMEM((samples // 2, LANES), bf16)],
    )(place, kept, kept2)
    turned2, weighted, low, power = call(
        weight_kernel,
        [shape, ((LANES, 2 * half), bf16), ((LANES, 2 * half), bf16), ((LANES, LANES), f32)],
        7,
        scratch=[pltpu.VMEM((samples // 2, LANES), bf16)],
    )(place, kept, kept2, near, near2, share, gene)
    keep, passed = call(
        score_kernel,
        [((LANES, LANES), f32)] * 2,
        13,
        scratch=[pltpu.VMEM((samples, variants), bf16)],
    )(place, gene, power, turned, turned2, weighted, low, d0, d1, d4, d537, d2, d6)
    return keep + other_core(passed)


def body(eigvecs, eigvals, expression, dosage, delta, window_start, window_valid, gene_owner):
    rows = lax.axis_size("row")
    samples = eigvecs.shape[0] * rows
    own = expression.shape[1] // rows
    fits = (
        lax.axis_size("col") == 2
        and own == LANES
        and W == 2 * LANES
        and rows == 8
        and dosage.shape[1] % (2 * LANES) == 0
        and samples * (samples + dosage.shape[1]) <= VMEM_LIMIT // 16
    )
    run = near_body if fits else wide_body
    return run(eigvecs, eigvals, expression, dosage, delta, window_start, window_valid, gene_owner)


def solution(mesh):
    placed = (
        P(("groups", "row"), "col"),
        P(("groups", "col")),
        P(("groups", "row"), None),
        P(("groups", "row"), None),
        P("groups"),
        P("groups"),
        P("groups"),
        P("groups"),
    )
    return jax.shard_map(
        body, mesh=mesh, in_specs=placed, out_specs=P(("groups", "row"), "col"), check_vma=False
    )
```

```python
import jax
import jax.numpy as jnp
from jax import lax
from jax.experimental import pallas as pl
from jax.experimental.pallas import tpu as pltpu
from jax.sharding import PartitionSpec as P

W = 256
LANES = 128
VMEM_LIMIT = 32 * 1024 * 1024
ROUTE_LIMIT = 32 * 1024 * 1024
NT = (((1,), (1,)), ((), ()))
f32 = jnp.float32
bf16 = jnp.bfloat16


def owner_listing(gene_owner):
    total = gene_owner.shape[0]
    return jnp.argsort(gene_owner * total + jnp.arange(total, dtype=jnp.int32))


def earlier_equal(labels):
    places = jnp.arange(labels.shape[0], dtype=jnp.int32)
    same = labels[:, None] == labels[None, :]
    before = places[:, None] > places[None, :]
    return jnp.sum((same & before).astype(jnp.int32), axis=1)


def shift_windows(tables, starts, largest):
    moved_tables = tables
    step_size = 1
    while step_size <= largest:
        bit_set = starts // step_size % 2 == 1
        filler = jnp.zeros(moved_tables.shape[:-1] + (step_size,), moved_tables.dtype)
        moved = jnp.concatenate([moved_tables[..., step_size:], filler], axis=-1)
        moved_tables = jnp.where(bit_set[None, :, None], moved, moved_tables)
        step_size = step_size * 2
    return moved_tables


def wide_body(eigvecs, eigvals, expression, dosage, delta, window_start, window_valid, gene_owner):
    row_count = lax.axis_size("row")
    row_index = lax.axis_index("row")
    genes_all = expression.shape[1]
    own_count = genes_all // row_count
    half_samples = eigvecs.shape[1]
    samples = half_samples * lax.axis_size("col")
    owner_order = owner_listing(gene_owner)
    my_genes = lax.dynamic_slice_in_dim(owner_order, row_index * own_count, own_count)
    expr_panel, dose_panel = (
        lax.all_to_all(expression, "row", split_axis=1, concat_axis=0, tiled=True),
        lax.all_to_all(dosage, "row", split_axis=1, concat_axis=0, tiled=True),
    )
    panel_data = jnp.concatenate([expr_panel, dose_panel], axis=1)
    rotated = lax.dot_general(
        panel_data,
        lax.all_gather(eigvecs, "row", axis=0, tiled=True),
        (((0,), (0,)), ((), ())),
        preferred_element_type=jnp.float32,
    ).astype(jnp.bfloat16)
    rot_expr = rotated[:own_count]
    rot_dose = rotated[own_count:]
    dose_all = lax.all_gather(rot_dose, "row", axis=0, tiled=True)
    capacity = max(2, own_count // row_count)
    destination = lax.dynamic_slice_in_dim(gene_owner, row_index * own_count, own_count)
    position = destination * capacity + earlier_equal(destination)
    slot_ids = jnp.arange(row_count * capacity, dtype=jnp.int32)
    placement_map = (slot_ids[:, None] == position[None, :]).astype(jnp.bfloat16)
    buckets = jnp.dot(placement_map, rot_expr, preferred_element_type=jnp.float32).astype(
        jnp.bfloat16
    )
    received = lax.all_to_all(buckets, "row", split_axis=0, concat_axis=0, tiled=True)
    source = my_genes // own_count
    owned_expr = jnp.take(received, source * capacity + earlier_equal(source), axis=0)
    own_delta = jnp.take(delta, my_genes)
    own_start = jnp.take(window_start, my_genes)
    own_valid = jnp.take(window_valid, my_genes)
    weight = 1.0 / (eigvals[None, :] + own_delta[:, None])
    expr_float = owned_expr.astype(jnp.float32)
    expr_power = jnp.sum(weight * expr_float * expr_float, axis=1)
    weighted = (weight * expr_float).astype(jnp.bfloat16)
    weight_low = weight.astype(jnp.bfloat16)
    dose_sq = jnp.square(dose_all.astype(jnp.float32)).astype(jnp.bfloat16)
    slot_index = jnp.arange(W, dtype=jnp.int32)
    contract = (((1,), (1,)), ((), ()))
    cross_all = lax.dot_general(weighted, dose_all, contract, preferred_element_type=jnp.float32)
    power_all = lax.dot_general(weight_low, dose_sq, contract, preferred_element_type=jnp.float32)
    stacked = jnp.stack([cross_all, power_all], axis=0)
    variants = dose_all.shape[0]
    shifted = shift_windows(stacked, own_start, variants - W)
    cross_sum = shifted[0, :, :W]
    dose_power = shifted[1, :, :W]
    cross_sum, dose_power, expr_power = lax.psum((cross_sum, dose_power, expr_power), "col")
    scale = jnp.sqrt(jnp.float32(samples))
    zscore = jnp.where(
        slot_index[None, :] < own_valid[:, None],
        scale * cross_sum / jnp.sqrt(dose_power * expr_power[:, None]),
        0.0,
    )
    width_part = W // lax.axis_size("col")
    return lax.dynamic_slice_in_dim(zscore, lax.axis_index("col") * width_part, width_part, 1)


def route_kernel(
    place_ref, owner_any, delta_any, start_any, valid_any, vals_any, vecs_any, expr_any, dose_any,
    ahead_ref, e46_ref, e2_ref, e0_ref, gene_ref, terms_ref, half_ref,
    owner_ref, delta_ref, start_ref, valid_ref, vals_ref, expr_ref, sems,
):
    row, core = place_ref[0], place_ref[1]
    half = vecs_any.shape[1]
    part = expr_ref.shape[0]
    variants = half_ref.shape[1]
    pairs = (
        (owner_any, owner_ref),
        (expr_any.at[pl.ds(pl.multiple_of(core * part, part), part)], expr_ref),
        (delta_any, delta_ref),
        (start_any, start_ref),
        (valid_any, valid_ref),
        (vals_any, vals_ref),
        (vecs_any, ahead_ref.at[:, pl.ds(0, half)]),
        (dose_any.at[:, pl.ds(pl.multiple_of(core * variants, LANES), variants)], half_ref),
    )
    copies = [pltpu.make_async_copy(a, b, sems.at[i]) for i, (a, b) in enumerate(pairs)]
    for copy in copies:
        copy.start()
    slices = owner_ref.shape[0]
    capacity = LANES // slices
    before = lax.broadcasted_iota(jnp.int32, (LANES, LANES), 0) < lax.broadcasted_iota(
        jnp.int32, (LANES, LANES), 1
    )
    before = before.astype(bf16)
    slot = lax.broadcasted_iota(jnp.int32, (LANES, LANES), 0)
    own_slot = lax.broadcasted_iota(jnp.int32, (capacity, LANES), 0)
    lane = lax.broadcasted_iota(jnp.int32, (capacity, LANES), 1)
    copies[0].wait()
    owner = owner_ref[...]
    rank = jnp.zeros(owner.shape, f32)
    for o in range(slices):
        same = (owner == o).astype(f32)
        rank += same * jnp.dot(same.astype(bf16), before, preferred_element_type=f32)
    bucket = (owner ^ row) * capacity + rank.astype(jnp.int32)
    for copy in copies[1:]:
        copy.wait()
    sorted_slices = []
    for s in range(slices):
        here = bucket[s : s + 1, :]
        pick = (slot == here).astype(bf16)
        sorted_slices.append(
            lax.dot_general(pick, expr_ref[:, s * LANES : (s + 1) * LANES], NT, preferred_element_type=f32)
        )
        mine = (own_slot == here).astype(f32)
        figures = jnp.zeros((capacity, LANES), f32)
        for i, ref in enumerate((delta_ref, start_ref, valid_ref)):
            line = ref[s : s + 1, :].astype(f32)
            figures = jnp.where(lane == i, jnp.sum(mine * line, axis=1, keepdims=True), figures)
        gene_ref[s * capacity : (s + 1) * capacity, :] = figures
    vals = vals_ref[...]
    high = vals.astype(bf16).astype(f32)
    middle = (vals - high).astype(bf16).astype(f32)
    term = lax.broadcasted_iota(jnp.int32, terms_ref.shape, 0)
    terms = jnp.where(term == 0, high, jnp.where(term == 1, middle, jnp.where(term == 2, vals - high - middle, 0.0)))
    terms_ref[...] = terms.astype(bf16)
    left, right = slice(0, LANES), slice(LANES, 2 * LANES)
    upper, lower = slice(0, part), slice(part, 2 * part)
    targets = {
        0: (e0_ref, upper, left),
        1: (ahead_ref, upper, slice(half, half + LANES)),
        2: (e2_ref, upper, left),
        3: (ahead_ref, upper, slice(half + LANES, half + 2 * LANES)),
        4: (e46_ref, upper, left),
        5: (ahead_ref, lower, slice(half, half + LANES)),
        6: (e46_ref, upper, right),
        7: (ahead_ref, lower, slice(half + LANES, half + 2 * LANES)),
    }
    for m, (ref, down, side) in targets.items():
        block = jnp.concatenate([x[m * capacity : (m + 1) * capacity, :] for x in sorted_slices], axis=0)
        ref[down, side] = block.T.astype(bf16)


def second_kernel(ahead_ref, r1_ref, e46_ref, out_ref):
    half = out_ref.shape[1] // 2 - LANES
    part = e46_ref.shape[0]
    out_ref[:, :half] = ahead_ref[:, :half]
    out_ref[:, half : 2 * half] = r1_ref[:, :half]
    out_ref[:part, 2 * half :] = e46_ref[...]
    out_ref[part:, 2 * half :] = r1_ref[part:, half:]


def copy_kernel(d0_ref, d4_ref, after_any, own_ref, far_ref):
    own_ref[...] = d0_ref[...]
    far_ref[...] = d4_ref[...]


def third_kernel(
    ahead_ref, r1_ref, r4_ref, e2_ref, e0_ref, terms_ref, d4_ref, d2_ref, d6_ref, d1_any, out_ref, kept_ref, dose_ref
):
    half = terms_ref.shape[1]
    part = e0_ref.shape[0]
    for ref, own, at in ((out_ref, e2_ref, LANES), (kept_ref, e0_ref, 0)):
        ref[:, :half] = ahead_ref[:, :half]
        ref[:, half : 2 * half] = r1_ref[:, :half]
        ref[:, 2 * half : 4 * half] = r4_ref[:, : 2 * half]
        side = slice(2 * half + at, 2 * half + at + LANES)
        left, right = slice(4 * half, 4 * half + LANES), slice(4 * half + LANES, 4 * half + 2 * LANES)
        ref[:part, left] = own[...]
        ref[:part, right] = r1_ref[:part, half + at : half + at + LANES]
        ref[part:, left] = r4_ref[:part, side]
        ref[part:, right] = r4_ref[part:, side]
    width = out_ref.shape[1]
    terms = terms_ref.shape[0]
    kept_ref[:terms, width:] = terms_ref[...]
    kept_ref[terms:, width:] = jnp.zeros((kept_ref.shape[0] - terms, half), bf16)
    variants = d4_ref.shape[1]
    for i, ref in enumerate((d4_ref, d2_ref, d6_ref)):
        dose_ref[:, i * variants : (i + 1) * variants] = ref[...]


def rotate(place_ref, refs, turned_ref, data_scr):
    samples = refs[0].shape[0]
    half = turned_ref.shape[0] // 2
    part = samples // 2
    core = place_ref[1]
    for c, ref in enumerate(refs):
        side = core if c == 0 else 1 - core
        for i in range(4):
            turned_ref[c * half : (c + 1) * half, i * samples : (i + 1) * samples] = (
                ref[:, i * half : (i + 1) * half].astype(f32).T.astype(bf16)
            )
            at = 4 * half + i % 2 * LANES
            data_scr[pl.ds(pl.multiple_of(i * samples + side * part, part), part), :] = ref[
                i // 2 * part : (i // 2 + 1) * part, at : at + LANES
            ]
    data = data_scr[...].astype(f32).T.astype(bf16)
    shares = []
    for ref in refs:
        vecs = jnp.concatenate([ref[:, i * half : (i + 1) * half] for i in range(4)], axis=0)
        shares.append(jnp.dot(data, vecs, preferred_element_type=f32))
    return shares


def half_kernel(place_ref, mine_ref, other_ref, turned_ref, share_ref, data_scr):
    half = turned_ref.shape[0] // 2
    for c, share in enumerate(rotate(place_ref, (mine_ref, other_ref), turned_ref, data_scr)):
        share_ref[:, c * half : (c + 1) * half] = share


def weight_kernel(
    place_ref, kept_ref, kept2_ref, mine_ref, other_ref, share_ref, gene_ref,
    turned_ref, weighted_ref, low_ref, power_ref, data_scr,
):
    half = turned_ref.shape[0] // 2
    delta = gene_ref[:, 0:1]
    total = jnp.zeros((delta.shape[0], 1), f32)
    shares = rotate(place_ref, (mine_ref, other_ref), turned_ref, data_scr)
    width = mine_ref.shape[1]
    for c, (share, ref) in enumerate(zip(shares, (kept_ref, kept2_ref))):
        cols = slice(c * half, (c + 1) * half)
        terms = ref[0:16, width:].astype(f32)
        vals = terms[0:1] + terms[1:2] + terms[2:3]
        rotated = (share_ref[:, cols] + share).astype(bf16).astype(f32)
        weight = 1.0 / (vals + delta)
        total += jnp.sum(weight * rotated * rotated, axis=1, keepdims=True)
        weighted_ref[:, cols] = (weight * rotated).astype(bf16)
        low_ref[:, cols] = weight.astype(bf16)
    power_ref[...] = jnp.broadcast_to(total, power_ref.shape)


def score_kernel(place_ref, gene_ref, power_ref, turned_ref, turned2_ref, weighted_ref, low_ref, *refs):
    *dose_refs, keep_ref, pass_ref, dose_scr = refs
    samples, variants = dose_refs[0].shape
    chunks = [(ref, at) for ref in dose_refs for at in range(0, ref.shape[1], variants)]
    order = [0, 1, 2, 3, 6, 4, 7, 5]
    for m, (ref, at) in enumerate(chunks[i] for i in order):
        dose_scr[m * samples : (m + 1) * samples, :] = ref[:, at : at + variants]
    line = turned_ref.shape[1]
    rotated = jnp.dot(turned_ref[...], dose_scr[:line], preferred_element_type=f32)
    rotated += jnp.dot(turned2_ref[...], dose_scr[line:], preferred_element_type=f32)
    rotated = rotated.astype(bf16)
    squared = jnp.square(rotated.astype(f32)).astype(bf16)
    cross = jnp.dot(weighted_ref[...], rotated, preferred_element_type=f32)
    power = jnp.dot(low_ref[...], squared, preferred_element_type=f32)
    core = place_ref[1]
    start = gene_ref[:, 1:2].astype(jnp.int32)
    valid = gene_ref[:, 2:3].astype(jnp.int32)
    genes = cross.shape[0]
    lane = lax.broadcasted_iota(jnp.int32, (genes, LANES), 1)
    own_power = power_ref[...]
    scale = jnp.sqrt(f32(dose_scr.shape[0]))
    blocks = variants // LANES
    for out_ref, half in ((keep_ref, core), (pass_ref, 1 - core)):
        offset = start + half * LANES - core * variants
        block = offset >> 7
        shift = offset & (LANES - 1)
        need = block + (lane < shift).astype(jnp.int32)
        products = [jnp.zeros((genes, LANES), f32)] * 2
        for b in range(blocks):
            here = need == b
            parts = [array[:, b * LANES : (b + 1) * LANES] for array in (cross, power)]
            products = [jnp.where(here, part, product) for part, product in zip(parts, products)]
        inside = (need >= 0) & (need < blocks)
        score = jnp.where(inside, scale * products[0] / jnp.sqrt(products[1] * own_power), 0.0)
        score = jnp.take_along_axis(score, (lane + shift) & (LANES - 1), axis=1)
        out_ref[...] = jnp.where(lane + half * LANES < valid, score, 0.0)


def call(kernel, outs, count, scratch=(), smem=1, anywhere=0, limit=VMEM_LIMIT):
    vmem = pl.BlockSpec(memory_space=pltpu.VMEM)
    return pl.pallas_call(
        kernel,
        out_shape=[jax.ShapeDtypeStruct(*o) for o in outs],
        in_specs=[pl.BlockSpec(memory_space=pltpu.SMEM)] * smem + [vmem] * (count - smem - anywhere) + [pl.BlockSpec(memory_space=pl.ANY)] * anywhere,
        out_specs=[vmem] * len(outs),
        scratch_shapes=list(scratch),
        compiler_params=pltpu.CompilerParams(vmem_limit_bytes=limit),
    )


def near_body(eigvecs, eigvals, expression, dosage, delta, window_start, window_valid, gene_owner):
    rows = lax.axis_size("row")
    row = lax.axis_index("row")
    core = lax.axis_index("col")
    panel, half = eigvecs.shape
    part = panel // 2
    samples = panel * rows
    variants = dosage.shape[1] // 2
    place = jnp.stack([row, core]).astype(jnp.int32)

    def swap(x, m):
        return lax.ppermute(x, "row", [(i, i ^ m) for i in range(rows)])

    def other_core(x):
        return lax.ppermute(x, "col", [(0, 1), (1, 0)])

    ahead, e46, e2, e0, gene, terms, d0 = call(
        route_kernel,
        [
            ((panel, half + 2 * LANES), bf16),
            ((part, 2 * LANES), bf16),
            ((part, LANES), bf16),
            ((part, LANES), bf16),
            ((LANES, LANES), f32),
            ((16, half), bf16),
            ((panel, variants), bf16),
        ],
        9,
        scratch=[pltpu.VMEM((rows, LANES), kind) for kind in (jnp.int32, f32, jnp.int32, jnp.int32)]
        + [pltpu.VMEM((1, half), f32), pltpu.VMEM((part, expression.shape[1]), bf16), pltpu.SemaphoreType.DMA((8,))],
        anywhere=8,
        limit=ROUTE_LIMIT,
    )(
        place,
        *[
            pltpu.with_memory_space_constraint(x, pltpu.HBM)
            for x in (
                gene_owner.reshape(rows, LANES),
                delta.reshape(rows, LANES),
                window_start.reshape(rows, LANES),
                window_valid.reshape(rows, LANES),
                eigvals[None, :],
                eigvecs,
                expression,
                dosage,
            )
        ],
    )
    r1 = swap(ahead, 1)
    d4 = swap(d0, 4)
    d2 = swap(d0, 2)
    to4 = call(second_kernel, [((panel, 2 * half + 2 * LANES), bf16)], 3, smem=0)(ahead, r1, e46)[0]
    r4 = swap(to4, 4)
    own, far = call(copy_kernel, [((panel, variants), bf16)] * 2, 3, smem=0, anywhere=1)(d0, d4, to4)
    d6 = swap(far, 2)
    d1 = swap(own, 1)
    width = 4 * half + 2 * LANES
    out, kept, three = call(
        third_kernel,
        [((panel, width), bf16), ((panel, width + half), bf16), ((panel, 3 * variants), bf16)],
        10,
        smem=0,
        anywhere=1,
    )(ahead, r1, r4, e2, e0, terms, d4, d2, d6, d1)
    d537 = swap(three, 1)
    kept2 = other_core(kept)
    near = swap(out, 2)
    near2 = other_core(near)
    shape = ((2 * half, samples // 2), bf16)
    turned, share = call(
        half_kernel,
        [shape, ((LANES, 2 * half), f32)],
        3,
        scratch=[pltpu.VMEM((samples // 2, LANES), bf16)],
    )(place, kept, kept2)
    turned2, weighted, low, power = call(
        weight_kernel,
        [shape, ((LANES, 2 * half), bf16), ((LANES, 2 * half), bf16), ((LANES, LANES), f32)],
        7,
        scratch=[pltpu.VMEM((samples // 2, LANES), bf16)],
    )(place, kept, kept2, near, near2, share, gene)
    keep, passed = call(
        score_kernel,
        [((LANES, LANES), f32)] * 2,
        13,
        scratch=[pltpu.VMEM((samples, variants), bf16)],
    )(place, gene, power, turned, turned2, weighted, low, d0, d1, d4, d537, d2, d6)
    return keep + other_core(passed)


def body(eigvecs, eigvals, expression, dosage, delta, window_start, window_valid, gene_owner):
    rows = lax.axis_size("row")
    samples = eigvecs.shape[0] * rows
    own = expression.shape[1] // rows
    fits = (
        lax.axis_size("col") == 2
        and own == LANES
        and W == 2 * LANES
        and rows == 8
        and dosage.shape[1] % (2 * LANES) == 0
        and samples * (samples + dosage.shape[1]) <= VMEM_LIMIT // 16
    )
    run = near_body if fits else wide_body
    return run(eigvecs, eigvals, expression, dosage, delta, window_start, window_valid, gene_owner)


def solution(mesh):
    placed = (
        P(("groups", "row"), "col"),
        P(("groups", "col")),
        P(("groups", "row"), None),
        P(("groups", "row"), None),
        P("groups"),
        P("groups"),
        P("groups"),
        P("groups"),
    )
    return jax.shard_map(
        body, mesh=mesh, in_specs=placed, out_specs=P(("groups", "row"), "col"), check_vma=False
    )
```

```python
import jax
import jax.numpy as jnp
from jax import lax
from jax.experimental import pallas as pl
from jax.experimental.pallas import tpu as pltpu
from jax.sharding import PartitionSpec as P

W = 256
LANES = 128
VMEM_LIMIT = 32 * 1024 * 1024
ROUTE_LIMIT = 32 * 1024 * 1024
NT = (((1,), (1,)), ((), ()))
f32 = jnp.float32
bf16 = jnp.bfloat16


def owner_listing(gene_owner):
    total = gene_owner.shape[0]
    return jnp.argsort(gene_owner * total + jnp.arange(total, dtype=jnp.int32))


def earlier_equal(labels):
    places = jnp.arange(labels.shape[0], dtype=jnp.int32)
    same = labels[:, None] == labels[None, :]
    before = places[:, None] > places[None, :]
    return jnp.sum((same & before).astype(jnp.int32), axis=1)


def shift_windows(tables, starts, largest):
    moved_tables = tables
    step_size = 1
    while step_size <= largest:
        bit_set = starts // step_size % 2 == 1
        filler = jnp.zeros(moved_tables.shape[:-1] + (step_size,), moved_tables.dtype)
        moved = jnp.concatenate([moved_tables[..., step_size:], filler], axis=-1)
        moved_tables = jnp.where(bit_set[None, :, None], moved, moved_tables)
        step_size = step_size * 2
    return moved_tables


def wide_body(eigvecs, eigvals, expression, dosage, delta, window_start, window_valid, gene_owner):
    row_count = lax.axis_size("row")
    row_index = lax.axis_index("row")
    genes_all = expression.shape[1]
    own_count = genes_all // row_count
    half_samples = eigvecs.shape[1]
    samples = half_samples * lax.axis_size("col")
    owner_order = owner_listing(gene_owner)
    my_genes = lax.dynamic_slice_in_dim(owner_order, row_index * own_count, own_count)
    expr_panel, dose_panel = (
        lax.all_to_all(expression, "row", split_axis=1, concat_axis=0, tiled=True),
        lax.all_to_all(dosage, "row", split_axis=1, concat_axis=0, tiled=True),
    )
    panel_data = jnp.concatenate([expr_panel, dose_panel], axis=1)
    rotated = lax.dot_general(
        panel_data,
        lax.all_gather(eigvecs, "row", axis=0, tiled=True),
        (((0,), (0,)), ((), ())),
        preferred_element_type=jnp.float32,
    ).astype(jnp.bfloat16)
    rot_expr = rotated[:own_count]
    rot_dose = rotated[own_count:]
    dose_all = lax.all_gather(rot_dose, "row", axis=0, tiled=True)
    capacity = max(2, own_count // row_count)
    destination = lax.dynamic_slice_in_dim(gene_owner, row_index * own_count, own_count)
    position = destination * capacity + earlier_equal(destination)
    slot_ids = jnp.arange(row_count * capacity, dtype=jnp.int32)
    placement_map = (slot_ids[:, None] == position[None, :]).astype(jnp.bfloat16)
    buckets = jnp.dot(placement_map, rot_expr, preferred_element_type=jnp.float32).astype(
        jnp.bfloat16
    )
    received = lax.all_to_all(buckets, "row", split_axis=0, concat_axis=0, tiled=True)
    source = my_genes // own_count
    owned_expr = jnp.take(received, source * capacity + earlier_equal(source), axis=0)
    own_delta = jnp.take(delta, my_genes)
    own_start = jnp.take(window_start, my_genes)
    own_valid = jnp.take(window_valid, my_genes)
    weight = 1.0 / (eigvals[None, :] + own_delta[:, None])
    expr_float = owned_expr.astype(jnp.float32)
    expr_power = jnp.sum(weight * expr_float * expr_float, axis=1)
    weighted = (weight * expr_float).astype(jnp.bfloat16)
    weight_low = weight.astype(jnp.bfloat16)
    dose_sq = jnp.square(dose_all.astype(jnp.float32)).astype(jnp.bfloat16)
    slot_index = jnp.arange(W, dtype=jnp.int32)
    contract = (((1,), (1,)), ((), ()))
    cross_all = lax.dot_general(weighted, dose_all, contract, preferred_element_type=jnp.float32)
    power_all = lax.dot_general(weight_low, dose_sq, contract, preferred_element_type=jnp.float32)
    stacked = jnp.stack([cross_all, power_all], axis=0)
    variants = dose_all.shape[0]
    shifted = shift_windows(stacked, own_start, variants - W)
    cross_sum = shifted[0, :, :W]
    dose_power = shifted[1, :, :W]
    cross_sum, dose_power, expr_power = lax.psum((cross_sum, dose_power, expr_power), "col")
    scale = jnp.sqrt(jnp.float32(samples))
    zscore = jnp.where(
        slot_index[None, :] < own_valid[:, None],
        scale * cross_sum / jnp.sqrt(dose_power * expr_power[:, None]),
        0.0,
    )
    width_part = W // lax.axis_size("col")
    return lax.dynamic_slice_in_dim(zscore, lax.axis_index("col") * width_part, width_part, 1)


def route_kernel(
    place_ref, owner_any, delta_any, start_any, valid_any, vals_any, vecs_any, expr_any, dose_any,
    ahead_ref, e46_ref, e2_ref, e0_ref, gene_ref, terms_ref, half_ref,
    owner_ref, delta_ref, start_ref, valid_ref, vals_ref, expr_ref, sems,
):
    row, core = place_ref[0], place_ref[1]
    half = vecs_any.shape[1]
    part = expr_ref.shape[0]
    variants = half_ref.shape[1]
    pairs = (
        (owner_any, owner_ref),
        (expr_any.at[pl.ds(pl.multiple_of(core * part, part), part)], expr_ref),
        (delta_any, delta_ref),
        (start_any, start_ref),
        (valid_any, valid_ref),
        (vals_any, vals_ref),
        (vecs_any, ahead_ref.at[:, pl.ds(0, half)]),
        (dose_any.at[:, pl.ds(pl.multiple_of(core * variants, LANES), variants)], half_ref),
    )
    copies = [pltpu.make_async_copy(a, b, sems.at[i]) for i, (a, b) in enumerate(pairs)]
    for copy in copies:
        copy.start()
    slices = owner_ref.shape[0]
    capacity = LANES // slices
    before = lax.broadcasted_iota(jnp.int32, (LANES, LANES), 0) < lax.broadcasted_iota(
        jnp.int32, (LANES, LANES), 1
    )
    before = before.astype(bf16)
    slot = lax.broadcasted_iota(jnp.int32, (LANES, LANES), 0)
    own_slot = lax.broadcasted_iota(jnp.int32, (capacity, LANES), 0)
    lane = lax.broadcasted_iota(jnp.int32, (capacity, LANES), 1)
    copies[0].wait()
    owner = owner_ref[...]
    rank = jnp.zeros(owner.shape, f32)
    for o in range(slices):
        same = (owner == o).astype(f32)
        rank += same * jnp.dot(same.astype(bf16), before, preferred_element_type=f32)
    bucket = (owner ^ row) * capacity + rank.astype(jnp.int32)
    for copy in copies[1:]:
        copy.wait()
    sorted_slices = []
    for s in range(slices):
        here = bucket[s : s + 1, :]
        pick = (slot == here).astype(bf16)
        sorted_slices.append(
            lax.dot_general(pick, expr_ref[:, s * LANES : (s + 1) * LANES], NT, preferred_element_type=f32)
        )
        mine = (own_slot == here).astype(f32)
        figures = jnp.zeros((capacity, LANES), f32)
        for i, ref in enumerate((delta_ref, start_ref, valid_ref)):
            line = ref[s : s + 1, :].astype(f32)
            figures = jnp.where(lane == i, jnp.sum(mine * line, axis=1, keepdims=True), figures)
        gene_ref[s * capacity : (s + 1) * capacity, :] = figures
    vals = vals_ref[...]
    high = vals.astype(bf16).astype(f32)
    middle = (vals - high).astype(bf16).astype(f32)
    term = lax.broadcasted_iota(jnp.int32, terms_ref.shape, 0)
    terms = jnp.where(term == 0, high, jnp.where(term == 1, middle, jnp.where(term == 2, vals - high - middle, 0.0)))
    terms_ref[...] = terms.astype(bf16)
    left, right = slice(0, LANES), slice(LANES, 2 * LANES)
    upper, lower = slice(0, part), slice(part, 2 * part)
    targets = {
        0: (e0_ref, upper, left),
        1: (ahead_ref, upper, slice(half, half + LANES)),
        2: (e2_ref, upper, left),
        3: (ahead_ref, upper, slice(half + LANES, half + 2 * LANES)),
        4: (e46_ref, upper, left),
        5: (ahead_ref, lower, slice(half, half + LANES)),
        6: (e46_ref, upper, right),
        7: (ahead_ref, lower, slice(half + LANES, half + 2 * LANES)),
    }
    for m, (ref, down, side) in targets.items():
        block = jnp.concatenate([x[m * capacity : (m + 1) * capacity, :] for x in sorted_slices], axis=0)
        ref[down, side] = block.T.astype(bf16)


def second_kernel(ahead_ref, r1_ref, e46_ref, out_ref):
    half = out_ref.shape[1] // 2 - LANES
    part = e46_ref.shape[0]
    out_ref[:, :half] = ahead_ref[:, :half]
    out_ref[:, half : 2 * half] = r1_ref[:, :half]
    out_ref[:part, 2 * half :] = e46_ref[...]
    out_ref[part:, 2 * half :] = r1_ref[part:, half:]


def copy_kernel(d0_ref, d4_ref, after_any, pair_ref, far_ref):
    variants = d0_ref.shape[1]
    pair_ref[:, :variants] = d0_ref[...]
    pair_ref[:, variants:] = d4_ref[...]
    far_ref[...] = d4_ref[...]


def third_kernel(ahead_ref, r1_ref, r4_ref, e2_ref, e0_ref, terms_ref, far_any, out_ref, kept_ref):
    half = terms_ref.shape[1]
    part = e0_ref.shape[0]
    for ref, own, at in ((out_ref, e2_ref, LANES), (kept_ref, e0_ref, 0)):
        ref[:, :half] = ahead_ref[:, :half]
        ref[:, half : 2 * half] = r1_ref[:, :half]
        ref[:, 2 * half : 4 * half] = r4_ref[:, : 2 * half]
        side = slice(2 * half + at, 2 * half + at + LANES)
        left, right = slice(4 * half, 4 * half + LANES), slice(4 * half + LANES, 4 * half + 2 * LANES)
        ref[:part, left] = own[...]
        ref[:part, right] = r1_ref[:part, half + at : half + at + LANES]
        ref[part:, left] = r4_ref[:part, side]
        ref[part:, right] = r4_ref[part:, side]
    width = out_ref.shape[1]
    terms = terms_ref.shape[0]
    kept_ref[:terms, width:] = terms_ref[...]
    kept_ref[terms:, width:] = jnp.zeros((kept_ref.shape[0] - terms, half), bf16)


def rotate(place_ref, refs, turned_ref, data_scr):
    samples = refs[0].shape[0]
    half = turned_ref.shape[0] // 2
    part = samples // 2
    core = place_ref[1]
    for c, ref in enumerate(refs):
        side = core if c == 0 else 1 - core
        for i in range(4):
            turned_ref[c * half : (c + 1) * half, i * samples : (i + 1) * samples] = (
                ref[:, i * half : (i + 1) * half].astype(f32).T.astype(bf16)
            )
            at = 4 * half + i % 2 * LANES
            data_scr[pl.ds(pl.multiple_of(i * samples + side * part, part), part), :] = ref[
                i // 2 * part : (i // 2 + 1) * part, at : at + LANES
            ]
    data = data_scr[...].astype(f32).T.astype(bf16)
    shares = []
    for ref in refs:
        vecs = jnp.concatenate([ref[:, i * half : (i + 1) * half] for i in range(4)], axis=0)
        shares.append(jnp.dot(data, vecs, preferred_element_type=f32))
    return shares


def half_kernel(place_ref, mine_ref, other_ref, d15_any, turned_ref, share_ref, data_scr):
    half = turned_ref.shape[0] // 2
    for c, share in enumerate(rotate(place_ref, (mine_ref, other_ref), turned_ref, data_scr)):
        share_ref[:, c * half : (c + 1) * half] = share


def weight_kernel(
    place_ref, kept_ref, kept2_ref, mine_ref, other_ref, share_ref, gene_ref,
    turned_ref, weighted_ref, low_ref, power_ref, data_scr,
):
    half = turned_ref.shape[0] // 2
    delta = gene_ref[:, 0:1]
    total = jnp.zeros((delta.shape[0], 1), f32)
    shares = rotate(place_ref, (mine_ref, other_ref), turned_ref, data_scr)
    width = mine_ref.shape[1]
    for c, (share, ref) in enumerate(zip(shares, (kept_ref, kept2_ref))):
        cols = slice(c * half, (c + 1) * half)
        terms = ref[0:16, width:].astype(f32)
        vals = terms[0:1] + terms[1:2] + terms[2:3]
        rotated = (share_ref[:, cols] + share).astype(bf16).astype(f32)
        weight = 1.0 / (vals + delta)
        total += jnp.sum(weight * rotated * rotated, axis=1, keepdims=True)
        weighted_ref[:, cols] = (weight * rotated).astype(bf16)
        low_ref[:, cols] = weight.astype(bf16)
    power_ref[...] = jnp.broadcast_to(total, power_ref.shape)


def score_kernel(place_ref, gene_ref, power_ref, turned_ref, turned2_ref, weighted_ref, low_ref, *refs):
    *dose_refs, keep_ref, pass_ref, dose_scr = refs
    samples, variants = dose_refs[0].shape
    chunks = [(ref, at) for ref in dose_refs for at in range(0, ref.shape[1], variants)]
    order = [0, 1, 3, 2, 4, 5, 7, 6]
    for m, (ref, at) in enumerate(chunks[i] for i in order):
        dose_scr[m * samples : (m + 1) * samples, :] = ref[:, at : at + variants]
    line = turned_ref.shape[1]
    rotated = jnp.dot(turned_ref[...], dose_scr[:line], preferred_element_type=f32)
    rotated += jnp.dot(turned2_ref[...], dose_scr[line:], preferred_element_type=f32)
    rotated = rotated.astype(bf16)
    squared = jnp.square(rotated.astype(f32)).astype(bf16)
    cross = jnp.dot(weighted_ref[...], rotated, preferred_element_type=f32)
    power = jnp.dot(low_ref[...], squared, preferred_element_type=f32)
    core = place_ref[1]
    start = gene_ref[:, 1:2].astype(jnp.int32)
    valid = gene_ref[:, 2:3].astype(jnp.int32)
    genes = cross.shape[0]
    lane = lax.broadcasted_iota(jnp.int32, (genes, LANES), 1)
    own_power = power_ref[...]
    scale = jnp.sqrt(f32(dose_scr.shape[0]))
    blocks = variants // LANES
    for out_ref, half in ((keep_ref, core), (pass_ref, 1 - core)):
        offset = start + half * LANES - core * variants
        block = offset >> 7
        shift = offset & (LANES - 1)
        need = block + (lane < shift).astype(jnp.int32)
        products = [jnp.zeros((genes, LANES), f32)] * 2
        for b in range(blocks):
            here = need == b
            parts = [array[:, b * LANES : (b + 1) * LANES] for array in (cross, power)]
            products = [jnp.where(here, part, product) for part, product in zip(parts, products)]
        inside = (need >= 0) & (need < blocks)
        score = jnp.where(inside, scale * products[0] / jnp.sqrt(products[1] * own_power), 0.0)
        score = jnp.take_along_axis(score, (lane + shift) & (LANES - 1), axis=1)
        out_ref[...] = jnp.where(lane + half * LANES < valid, score, 0.0)


def call(kernel, outs, count, scratch=(), smem=1, anywhere=0, limit=VMEM_LIMIT):
    vmem = pl.BlockSpec(memory_space=pltpu.VMEM)
    return pl.pallas_call(
        kernel,
        out_shape=[jax.ShapeDtypeStruct(*o) for o in outs],
        in_specs=[pl.BlockSpec(memory_space=pltpu.SMEM)] * smem + [vmem] * (count - smem - anywhere) + [pl.BlockSpec(memory_space=pl.ANY)] * anywhere,
        out_specs=[vmem] * len(outs),
        scratch_shapes=list(scratch),
        compiler_params=pltpu.CompilerParams(vmem_limit_bytes=limit),
    )


def near_body(eigvecs, eigvals, expression, dosage, delta, window_start, window_valid, gene_owner):
    rows = lax.axis_size("row")
    row = lax.axis_index("row")
    core = lax.axis_index("col")
    panel, half = eigvecs.shape
    part = panel // 2
    samples = panel * rows
    variants = dosage.shape[1] // 2
    place = jnp.stack([row, core]).astype(jnp.int32)

    def swap(x, m):
        return lax.ppermute(x, "row", [(i, i ^ m) for i in range(rows)])

    def other_core(x):
        return lax.ppermute(x, "col", [(0, 1), (1, 0)])

    ahead, e46, e2, e0, gene, terms, d0 = call(
        route_kernel,
        [
            ((panel, half + 2 * LANES), bf16),
            ((part, 2 * LANES), bf16),
            ((part, LANES), bf16),
            ((part, LANES), bf16),
            ((LANES, LANES), f32),
            ((16, half), bf16),
            ((panel, variants), bf16),
        ],
        9,
        scratch=[pltpu.VMEM((rows, LANES), kind) for kind in (jnp.int32, f32, jnp.int32, jnp.int32)]
        + [pltpu.VMEM((1, half), f32), pltpu.VMEM((part, expression.shape[1]), bf16), pltpu.SemaphoreType.DMA((8,))],
        anywhere=8,
        limit=ROUTE_LIMIT,
    )(
        place,
        *[
            pltpu.with_memory_space_constraint(x, pltpu.HBM)
            for x in (
                gene_owner.reshape(rows, LANES),
                delta.reshape(rows, LANES),
                window_start.reshape(rows, LANES),
                window_valid.reshape(rows, LANES),
                eigvals[None, :],
                eigvecs,
                expression,
                dosage,
            )
        ],
    )
    r1 = swap(ahead, 1)
    d4 = swap(d0, 4)
    d2 = swap(d0, 2)
    to4 = call(second_kernel, [((panel, 2 * half + 2 * LANES), bf16)], 3, smem=0)(ahead, r1, e46)[0]
    r4 = swap(to4, 4)
    pair, far = call(
        copy_kernel, [((panel, 2 * variants), bf16), ((panel, variants), bf16)], 3, smem=0, anywhere=1
    )(d0, d4, to4)
    d6 = swap(far, 2)
    d15 = swap(pair, 1)
    d37 = swap(jnp.concatenate([d2, d6], axis=1), 1)
    width = 4 * half + 2 * LANES
    out, kept = call(
        third_kernel, [((panel, width), bf16), ((panel, width + half), bf16)], 7, smem=0, anywhere=1
    )(ahead, r1, r4, e2, e0, terms, far)
    kept2 = other_core(kept)
    near = swap(out, 2)
    near2 = other_core(near)
    shape = ((2 * half, samples // 2), bf16)
    turned, share = call(
        half_kernel,
        [shape, ((LANES, 2 * half), f32)],
        4,
        scratch=[pltpu.VMEM((samples // 2, LANES), bf16)],
        anywhere=1,
    )(place, kept, kept2, d15)
    turned2, weighted, low, power = call(
        weight_kernel,
        [shape, ((LANES, 2 * half), bf16), ((LANES, 2 * half), bf16), ((LANES, LANES), f32)],
        7,
        scratch=[pltpu.VMEM((samples // 2, LANES), bf16)],
    )(place, kept, kept2, near, near2, share, gene)
    keep, passed = call(
        score_kernel,
        [((LANES, LANES), f32)] * 2,
        13,
        scratch=[pltpu.VMEM((samples, variants), bf16)],
    )(place, gene, power, turned, turned2, weighted, low, d0, d15, d4, d2, d37, d6)
    return keep + other_core(passed)


def body(eigvecs, eigvals, expression, dosage, delta, window_start, window_valid, gene_owner):
    rows = lax.axis_size("row")
    samples = eigvecs.shape[0] * rows
    own = expression.shape[1] // rows
    fits = (
        lax.axis_size("col") == 2
        and own == LANES
        and W == 2 * LANES
        and rows == 8
        and dosage.shape[1] % (2 * LANES) == 0
        and samples * (samples + dosage.shape[1]) <= VMEM_LIMIT // 16
    )
    run = near_body if fits else wide_body
    return run(eigvecs, eigvals, expression, dosage, delta, window_start, window_valid, gene_owner)


def solution(mesh):
    placed = (
        P(("groups", "row"), "col"),
        P(("groups", "col")),
        P(("groups", "row"), None),
        P(("groups", "row"), None),
        P("groups"),
        P("groups"),
        P("groups"),
        P("groups"),
    )
    return jax.shard_map(
        body, mesh=mesh, in_specs=placed, out_specs=P(("groups", "row"), "col"), check_vma=False
    )
```

```python
import jax
import jax.numpy as jnp
from jax import lax
from jax.experimental import pallas as pl
from jax.experimental.pallas import tpu as pltpu
from jax.sharding import PartitionSpec as P

W = 256
LANES = 128
VMEM_LIMIT = 32 * 1024 * 1024
ROUTE_LIMIT = 32 * 1024 * 1024
NT = (((1,), (1,)), ((), ()))
f32 = jnp.float32
bf16 = jnp.bfloat16


def owner_listing(gene_owner):
    total = gene_owner.shape[0]
    return jnp.argsort(gene_owner * total + jnp.arange(total, dtype=jnp.int32))


def earlier_equal(labels):
    places = jnp.arange(labels.shape[0], dtype=jnp.int32)
    same = labels[:, None] == labels[None, :]
    before = places[:, None] > places[None, :]
    return jnp.sum((same & before).astype(jnp.int32), axis=1)


def shift_windows(tables, starts, largest):
    moved_tables = tables
    step_size = 1
    while step_size <= largest:
        bit_set = starts // step_size % 2 == 1
        filler = jnp.zeros(moved_tables.shape[:-1] + (step_size,), moved_tables.dtype)
        moved = jnp.concatenate([moved_tables[..., step_size:], filler], axis=-1)
        moved_tables = jnp.where(bit_set[None, :, None], moved, moved_tables)
        step_size = step_size * 2
    return moved_tables


def wide_body(eigvecs, eigvals, expression, dosage, delta, window_start, window_valid, gene_owner):
    row_count = lax.axis_size("row")
    row_index = lax.axis_index("row")
    genes_all = expression.shape[1]
    own_count = genes_all // row_count
    half_samples = eigvecs.shape[1]
    samples = half_samples * lax.axis_size("col")
    owner_order = owner_listing(gene_owner)
    my_genes = lax.dynamic_slice_in_dim(owner_order, row_index * own_count, own_count)
    expr_panel, dose_panel = (
        lax.all_to_all(expression, "row", split_axis=1, concat_axis=0, tiled=True),
        lax.all_to_all(dosage, "row", split_axis=1, concat_axis=0, tiled=True),
    )
    panel_data = jnp.concatenate([expr_panel, dose_panel], axis=1)
    rotated = lax.dot_general(
        panel_data,
        lax.all_gather(eigvecs, "row", axis=0, tiled=True),
        (((0,), (0,)), ((), ())),
        preferred_element_type=jnp.float32,
    ).astype(jnp.bfloat16)
    rot_expr = rotated[:own_count]
    rot_dose = rotated[own_count:]
    dose_all = lax.all_gather(rot_dose, "row", axis=0, tiled=True)
    capacity = max(2, own_count // row_count)
    destination = lax.dynamic_slice_in_dim(gene_owner, row_index * own_count, own_count)
    position = destination * capacity + earlier_equal(destination)
    slot_ids = jnp.arange(row_count * capacity, dtype=jnp.int32)
    placement_map = (slot_ids[:, None] == position[None, :]).astype(jnp.bfloat16)
    buckets = jnp.dot(placement_map, rot_expr, preferred_element_type=jnp.float32).astype(
        jnp.bfloat16
    )
    received = lax.all_to_all(buckets, "row", split_axis=0, concat_axis=0, tiled=True)
    source = my_genes // own_count
    owned_expr = jnp.take(received, source * capacity + earlier_equal(source), axis=0)
    own_delta = jnp.take(delta, my_genes)
    own_start = jnp.take(window_start, my_genes)
    own_valid = jnp.take(window_valid, my_genes)
    weight = 1.0 / (eigvals[None, :] + own_delta[:, None])
    expr_float = owned_expr.astype(jnp.float32)
    expr_power = jnp.sum(weight * expr_float * expr_float, axis=1)
    weighted = (weight * expr_float).astype(jnp.bfloat16)
    weight_low = weight.astype(jnp.bfloat16)
    dose_sq = jnp.square(dose_all.astype(jnp.float32)).astype(jnp.bfloat16)
    slot_index = jnp.arange(W, dtype=jnp.int32)
    contract = (((1,), (1,)), ((), ()))
    cross_all = lax.dot_general(weighted, dose_all, contract, preferred_element_type=jnp.float32)
    power_all = lax.dot_general(weight_low, dose_sq, contract, preferred_element_type=jnp.float32)
    stacked = jnp.stack([cross_all, power_all], axis=0)
    variants = dose_all.shape[0]
    shifted = shift_windows(stacked, own_start, variants - W)
    cross_sum = shifted[0, :, :W]
    dose_power = shifted[1, :, :W]
    cross_sum, dose_power, expr_power = lax.psum((cross_sum, dose_power, expr_power), "col")
    scale = jnp.sqrt(jnp.float32(samples))
    zscore = jnp.where(
        slot_index[None, :] < own_valid[:, None],
        scale * cross_sum / jnp.sqrt(dose_power * expr_power[:, None]),
        0.0,
    )
    width_part = W // lax.axis_size("col")
    return lax.dynamic_slice_in_dim(zscore, lax.axis_index("col") * width_part, width_part, 1)


def route_kernel(
    place_ref, owner_any, delta_any, start_any, valid_any, vals_any, vecs_any, expr_any, dose_any,
    ahead_ref, e13_ref, e2_ref, e0_ref, gene_ref, terms_ref, half_ref,
    owner_ref, delta_ref, start_ref, valid_ref, vals_ref, expr_ref, sems,
):
    row, core = place_ref[0], place_ref[1]
    half = vecs_any.shape[1]
    part = expr_ref.shape[0]
    variants = half_ref.shape[1]
    pairs = (
        (owner_any, owner_ref),
        (expr_any.at[pl.ds(pl.multiple_of(core * part, part), part)], expr_ref),
        (delta_any, delta_ref),
        (start_any, start_ref),
        (valid_any, valid_ref),
        (vals_any, vals_ref),
        (vecs_any, ahead_ref.at[:, pl.ds(0, half)]),
        (dose_any.at[:, pl.ds(pl.multiple_of(core * variants, LANES), variants)], half_ref),
    )
    copies = [pltpu.make_async_copy(a, b, sems.at[i]) for i, (a, b) in enumerate(pairs)]
    for copy in copies:
        copy.start()
    slices = owner_ref.shape[0]
    capacity = LANES // slices
    before = lax.broadcasted_iota(jnp.int32, (LANES, LANES), 0) < lax.broadcasted_iota(
        jnp.int32, (LANES, LANES), 1
    )
    before = before.astype(bf16)
    slot = lax.broadcasted_iota(jnp.int32, (LANES, LANES), 0)
    own_slot = lax.broadcasted_iota(jnp.int32, (capacity, LANES), 0)
    lane = lax.broadcasted_iota(jnp.int32, (capacity, LANES), 1)
    copies[0].wait()
    owner = owner_ref[...]
    rank = jnp.zeros(owner.shape, f32)
    for o in range(slices):
        same = (owner == o).astype(f32)
        rank += same * jnp.dot(same.astype(bf16), before, preferred_element_type=f32)
    bucket = (owner ^ row) * capacity + rank.astype(jnp.int32)
    for copy in copies[1:]:
        copy.wait()
    sorted_slices = []
    for s in range(slices):
        here = bucket[s : s + 1, :]
        pick = (slot == here).astype(bf16)
        sorted_slices.append(
            lax.dot_general(pick, expr_ref[:, s * LANES : (s + 1) * LANES], NT, preferred_element_type=f32)
        )
        mine = (own_slot == here).astype(f32)
        figures = jnp.zeros((capacity, LANES), f32)
        for i, ref in enumerate((delta_ref, start_ref, valid_ref)):
            line = ref[s : s + 1, :].astype(f32)
            figures = jnp.where(lane == i, jnp.sum(mine * line, axis=1, keepdims=True), figures)
        gene_ref[s * capacity : (s + 1) * capacity, :] = figures
    vals = vals_ref[...]
    high = vals.astype(bf16).astype(f32)
    middle = (vals - high).astype(bf16).astype(f32)
    term = lax.broadcasted_iota(jnp.int32, terms_ref.shape, 0)
    terms = jnp.where(term == 0, high, jnp.where(term == 1, middle, jnp.where(term == 2, vals - high - middle, 0.0)))
    terms_ref[...] = terms.astype(bf16)
    left, right = slice(0, LANES), slice(LANES, 2 * LANES)
    upper, lower = slice(0, part), slice(part, 2 * part)
    targets = {
        0: (e0_ref, upper, left),
        1: (e13_ref, upper, left),
        2: (e2_ref, upper, left),
        3: (e13_ref, upper, right),
        4: (ahead_ref, upper, slice(half, half + LANES)),
        5: (ahead_ref, lower, slice(half, half + LANES)),
        6: (ahead_ref, upper, slice(half + LANES, half + 2 * LANES)),
        7: (ahead_ref, lower, slice(half + LANES, half + 2 * LANES)),
    }
    for m, (ref, down, side) in targets.items():
        block = jnp.concatenate([x[m * capacity : (m + 1) * capacity, :] for x in sorted_slices], axis=0)
        ref[down, side] = block.T.astype(bf16)


def second_kernel(ahead_ref, r4_ref, e13_ref, out_ref):
    half = out_ref.shape[1] // 2 - LANES
    part = e13_ref.shape[0]
    out_ref[:, :half] = ahead_ref[:, :half]
    out_ref[:, half : 2 * half] = r4_ref[:, :half]
    out_ref[:part, 2 * half :] = e13_ref[...]
    out_ref[part:, 2 * half :] = r4_ref[part:, half:]


def copy_kernel(d0_ref, d4_ref, after_any, pair_ref, far_ref):
    variants = d0_ref.shape[1]
    pair_ref[:, :variants] = d0_ref[...]
    pair_ref[:, variants:] = d4_ref[...]
    far_ref[...] = d4_ref[...]


def third_kernel(ahead_ref, r4_ref, r1_ref, e2_ref, e0_ref, terms_ref, far_any, out_ref, kept_ref):
    half = terms_ref.shape[1]
    part = e0_ref.shape[0]
    for ref, own, at in ((out_ref, e2_ref, LANES), (kept_ref, e0_ref, 0)):
        ref[:, :half] = ahead_ref[:, :half]
        ref[:, half : 2 * half] = r4_ref[:, :half]
        ref[:, 2 * half : 4 * half] = r1_ref[:, : 2 * half]
        side = slice(2 * half + at, 2 * half + at + LANES)
        left, right = slice(4 * half, 4 * half + LANES), slice(4 * half + LANES, 4 * half + 2 * LANES)
        ref[:part, left] = own[...]
        ref[:part, right] = r4_ref[:part, half + at : half + at + LANES]
        ref[part:, left] = r1_ref[:part, side]
        ref[part:, right] = r1_ref[part:, side]
    width = out_ref.shape[1]
    terms = terms_ref.shape[0]
    kept_ref[:terms, width:] = terms_ref[...]
    kept_ref[terms:, width:] = jnp.zeros((kept_ref.shape[0] - terms, half), bf16)


def rotate(place_ref, refs, turned_ref, data_scr):
    samples = refs[0].shape[0]
    half = turned_ref.shape[0] // 2
    part = samples // 2
    core = place_ref[1]
    for c, ref in enumerate(refs):
        side = core if c == 0 else 1 - core
        for i in range(4):
            turned_ref[c * half : (c + 1) * half, i * samples : (i + 1) * samples] = (
                ref[:, i * half : (i + 1) * half].astype(f32).T.astype(bf16)
            )
            at = 4 * half + i % 2 * LANES
            data_scr[pl.ds(pl.multiple_of(i * samples + side * part, part), part), :] = ref[
                i // 2 * part : (i // 2 + 1) * part, at : at + LANES
            ]
    data = data_scr[...].astype(f32).T.astype(bf16)
    shares = []
    for ref in refs:
        vecs = jnp.concatenate([ref[:, i * half : (i + 1) * half] for i in range(4)], axis=0)
        shares.append(jnp.dot(data, vecs, preferred_element_type=f32))
    return shares


def half_kernel(place_ref, mine_ref, other_ref, d15_any, turned_ref, share_ref, data_scr):
    half = turned_ref.shape[0] // 2
    for c, share in enumerate(rotate(place_ref, (mine_ref, other_ref), turned_ref, data_scr)):
        share_ref[:, c * half : (c + 1) * half] = share


def weight_kernel(
    place_ref, kept_ref, kept2_ref, mine_ref, other_ref, share_ref, gene_ref,
    turned_ref, weighted_ref, low_ref, power_ref, data_scr,
):
    half = turned_ref.shape[0] // 2
    delta = gene_ref[:, 0:1]
    total = jnp.zeros((delta.shape[0], 1), f32)
    shares = rotate(place_ref, (mine_ref, other_ref), turned_ref, data_scr)
    width = mine_ref.shape[1]
    for c, (share, ref) in enumerate(zip(shares, (kept_ref, kept2_ref))):
        cols = slice(c * half, (c + 1) * half)
        terms = ref[0:16, width:].astype(f32)
        vals = terms[0:1] + terms[1:2] + terms[2:3]
        rotated = (share_ref[:, cols] + share).astype(bf16).astype(f32)
        weight = 1.0 / (vals + delta)
        total += jnp.sum(weight * rotated * rotated, axis=1, keepdims=True)
        weighted_ref[:, cols] = (weight * rotated).astype(bf16)
        low_ref[:, cols] = weight.astype(bf16)
    power_ref[...] = jnp.broadcast_to(total, power_ref.shape)


def score_kernel(place_ref, gene_ref, power_ref, turned_ref, turned2_ref, weighted_ref, low_ref, *refs):
    *dose_refs, keep_ref, pass_ref, dose_scr = refs
    samples, variants = dose_refs[0].shape
    chunks = [(ref, at) for ref in dose_refs for at in range(0, ref.shape[1], variants)]
    order = [0, 3, 1, 2, 4, 7, 5, 6]
    for m, (ref, at) in enumerate(chunks[i] for i in order):
        dose_scr[m * samples : (m + 1) * samples, :] = ref[:, at : at + variants]
    line = turned_ref.shape[1]
    rotated = jnp.dot(turned_ref[...], dose_scr[:line], preferred_element_type=f32)
    rotated += jnp.dot(turned2_ref[...], dose_scr[line:], preferred_element_type=f32)
    rotated = rotated.astype(bf16)
    squared = jnp.square(rotated.astype(f32)).astype(bf16)
    cross = jnp.dot(weighted_ref[...], rotated, preferred_element_type=f32)
    power = jnp.dot(low_ref[...], squared, preferred_element_type=f32)
    core = place_ref[1]
    start = gene_ref[:, 1:2].astype(jnp.int32)
    valid = gene_ref[:, 2:3].astype(jnp.int32)
    genes = cross.shape[0]
    lane = lax.broadcasted_iota(jnp.int32, (genes, LANES), 1)
    own_power = power_ref[...]
    scale = jnp.sqrt(f32(dose_scr.shape[0]))
    blocks = variants // LANES
    for out_ref, half in ((keep_ref, core), (pass_ref, 1 - core)):
        offset = start + half * LANES - core * variants
        block = offset >> 7
        shift = offset & (LANES - 1)
        need = block + (lane < shift).astype(jnp.int32)
        products = [jnp.zeros((genes, LANES), f32)] * 2
        for b in range(blocks):
            here = need == b
            parts = [array[:, b * LANES : (b + 1) * LANES] for array in (cross, power)]
            products = [jnp.where(here, part, product) for part, product in zip(parts, products)]
        inside = (need >= 0) & (need < blocks)
        score = jnp.where(inside, scale * products[0] / jnp.sqrt(products[1] * own_power), 0.0)
        score = jnp.take_along_axis(score, (lane + shift) & (LANES - 1), axis=1)
        out_ref[...] = jnp.where(lane + half * LANES < valid, score, 0.0)


def call(kernel, outs, count, scratch=(), smem=1, anywhere=0, limit=VMEM_LIMIT):
    vmem = pl.BlockSpec(memory_space=pltpu.VMEM)
    return pl.pallas_call(
        kernel,
        out_shape=[jax.ShapeDtypeStruct(*o) for o in outs],
        in_specs=[pl.BlockSpec(memory_space=pltpu.SMEM)] * smem + [vmem] * (count - smem - anywhere) + [pl.BlockSpec(memory_space=pl.ANY)] * anywhere,
        out_specs=[vmem] * len(outs),
        scratch_shapes=list(scratch),
        compiler_params=pltpu.CompilerParams(vmem_limit_bytes=limit),
    )


def near_body(eigvecs, eigvals, expression, dosage, delta, window_start, window_valid, gene_owner):
    rows = lax.axis_size("row")
    row = lax.axis_index("row")
    core = lax.axis_index("col")
    panel, half = eigvecs.shape
    part = panel // 2
    samples = panel * rows
    variants = dosage.shape[1] // 2
    place = jnp.stack([row, core]).astype(jnp.int32)

    def swap(x, m):
        return lax.ppermute(x, "row", [(i, i ^ m) for i in range(rows)])

    def other_core(x):
        return lax.ppermute(x, "col", [(0, 1), (1, 0)])

    ahead, e13, e2, e0, gene, terms, d0 = call(
        route_kernel,
        [
            ((panel, half + 2 * LANES), bf16),
            ((part, 2 * LANES), bf16),
            ((part, LANES), bf16),
            ((part, LANES), bf16),
            ((LANES, LANES), f32),
            ((16, half), bf16),
            ((panel, variants), bf16),
        ],
        9,
        scratch=[pltpu.VMEM((rows, LANES), kind) for kind in (jnp.int32, f32, jnp.int32, jnp.int32)]
        + [pltpu.VMEM((1, half), f32), pltpu.VMEM((part, expression.shape[1]), bf16), pltpu.SemaphoreType.DMA((8,))],
        anywhere=8,
        limit=ROUTE_LIMIT,
    )(
        place,
        *[
            pltpu.with_memory_space_constraint(x, pltpu.HBM)
            for x in (
                gene_owner.reshape(rows, LANES),
                delta.reshape(rows, LANES),
                window_start.reshape(rows, LANES),
                window_valid.reshape(rows, LANES),
                eigvals[None, :],
                eigvecs,
                expression,
                dosage,
            )
        ],
    )
    r4 = swap(ahead, 4)
    d4 = swap(d0, 4)
    d2 = swap(d0, 2)
    to1 = call(second_kernel, [((panel, 2 * half + 2 * LANES), bf16)], 3, smem=0)(ahead, r4, e13)[0]
    r1 = swap(to1, 1)
    pair, far = call(
        copy_kernel, [((panel, 2 * variants), bf16), ((panel, variants), bf16)], 3, smem=0, anywhere=1
    )(d0, d4, to1)
    d6 = swap(far, 2)
    d15 = swap(pair, 1)
    d37 = swap(jnp.concatenate([d2, d6], axis=1), 1)
    width = 4 * half + 2 * LANES
    out, kept = call(
        third_kernel, [((panel, width), bf16), ((panel, width + half), bf16)], 7, smem=0, anywhere=1
    )(ahead, r4, r1, e2, e0, terms, far)
    kept2 = other_core(kept)
    near = swap(out, 2)
    near2 = other_core(near)
    shape = ((2 * half, samples // 2), bf16)
    turned, share = call(
        half_kernel,
        [shape, ((LANES, 2 * half), f32)],
        4,
        scratch=[pltpu.VMEM((samples // 2, LANES), bf16)],
        anywhere=1,
    )(place, kept, kept2, d15)
    turned2, weighted, low, power = call(
        weight_kernel,
        [shape, ((LANES, 2 * half), bf16), ((LANES, 2 * half), bf16), ((LANES, LANES), f32)],
        7,
        scratch=[pltpu.VMEM((samples // 2, LANES), bf16)],
    )(place, kept, kept2, near, near2, share, gene)
    keep, passed = call(
        score_kernel,
        [((LANES, LANES), f32)] * 2,
        13,
        scratch=[pltpu.VMEM((samples, variants), bf16)],
    )(place, gene, power, turned, turned2, weighted, low, d0, d15, d4, d2, d37, d6)
    return keep + other_core(passed)


def body(eigvecs, eigvals, expression, dosage, delta, window_start, window_valid, gene_owner):
    rows = lax.axis_size("row")
    samples = eigvecs.shape[0] * rows
    own = expression.shape[1] // rows
    fits = (
        lax.axis_size("col") == 2
        and own == LANES
        and W == 2 * LANES
        and rows == 8
        and dosage.shape[1] % (2 * LANES) == 0
        and samples * (samples + dosage.shape[1]) <= VMEM_LIMIT // 16
    )
    run = near_body if fits else wide_body
    return run(eigvecs, eigvals, expression, dosage, delta, window_start, window_valid, gene_owner)


def solution(mesh):
    placed = (
        P(("groups", "row"), "col"),
        P(("groups", "col")),
        P(("groups", "row"), None),
        P(("groups", "row"), None),
        P("groups"),
        P("groups"),
        P("groups"),
        P("groups"),
    )
    return jax.shard_map(
        body, mesh=mesh, in_specs=placed, out_specs=P(("groups", "row"), "col"), check_vma=False
    )
```

```python
import jax
import jax.numpy as jnp
from jax import lax
from jax.experimental import pallas as pl
from jax.experimental.pallas import tpu as pltpu
from jax.sharding import PartitionSpec as P

W = 256
LANES = 128
VMEM_LIMIT = 32 * 1024 * 1024
NT = (((1,), (1,)), ((), ()))
f32 = jnp.float32
bf16 = jnp.bfloat16


def owner_listing(gene_owner):
    total = gene_owner.shape[0]
    return jnp.argsort(gene_owner * total + jnp.arange(total, dtype=jnp.int32))


def earlier_equal(labels):
    places = jnp.arange(labels.shape[0], dtype=jnp.int32)
    same = labels[:, None] == labels[None, :]
    before = places[:, None] > places[None, :]
    return jnp.sum((same & before).astype(jnp.int32), axis=1)


def shift_windows(tables, starts, largest):
    moved_tables = tables
    step_size = 1
    while step_size <= largest:
        bit_set = starts // step_size % 2 == 1
        filler = jnp.zeros(moved_tables.shape[:-1] + (step_size,), moved_tables.dtype)
        moved = jnp.concatenate([moved_tables[..., step_size:], filler], axis=-1)
        moved_tables = jnp.where(bit_set[None, :, None], moved, moved_tables)
        step_size = step_size * 2
    return moved_tables


def wide_body(eigvecs, eigvals, expression, dosage, delta, window_start, window_valid, gene_owner):
    row_count = lax.axis_size("row")
    row_index = lax.axis_index("row")
    genes_all = expression.shape[1]
    own_count = genes_all // row_count
    half_samples = eigvecs.shape[1]
    samples = half_samples * lax.axis_size("col")
    owner_order = owner_listing(gene_owner)
    my_genes = lax.dynamic_slice_in_dim(owner_order, row_index * own_count, own_count)
    expr_panel, dose_panel = (
        lax.all_to_all(expression, "row", split_axis=1, concat_axis=0, tiled=True),
        lax.all_to_all(dosage, "row", split_axis=1, concat_axis=0, tiled=True),
    )
    panel_data = jnp.concatenate([expr_panel, dose_panel], axis=1)
    rotated = lax.dot_general(
        panel_data,
        lax.all_gather(eigvecs, "row", axis=0, tiled=True),
        (((0,), (0,)), ((), ())),
        preferred_element_type=jnp.float32,
    ).astype(jnp.bfloat16)
    rot_expr = rotated[:own_count]
    rot_dose = rotated[own_count:]
    dose_all = lax.all_gather(rot_dose, "row", axis=0, tiled=True)
    capacity = max(2, own_count // row_count)
    destination = lax.dynamic_slice_in_dim(gene_owner, row_index * own_count, own_count)
    position = destination * capacity + earlier_equal(destination)
    slot_ids = jnp.arange(row_count * capacity, dtype=jnp.int32)
    placement_map = (slot_ids[:, None] == position[None, :]).astype(jnp.bfloat16)
    buckets = jnp.dot(placement_map, rot_expr, preferred_element_type=jnp.float32).astype(
        jnp.bfloat16
    )
    received = lax.all_to_all(buckets, "row", split_axis=0, concat_axis=0, tiled=True)
    source = my_genes // own_count
    owned_expr = jnp.take(received, source * capacity + earlier_equal(source), axis=0)
    own_delta = jnp.take(delta, my_genes)
    own_start = jnp.take(window_start, my_genes)
    own_valid = jnp.take(window_valid, my_genes)
    weight = 1.0 / (eigvals[None, :] + own_delta[:, None])
    expr_float = owned_expr.astype(jnp.float32)
    expr_power = jnp.sum(weight * expr_float * expr_float, axis=1)
    weighted = (weight * expr_float).astype(jnp.bfloat16)
    weight_low = weight.astype(jnp.bfloat16)
    dose_sq = jnp.square(dose_all.astype(jnp.float32)).astype(jnp.bfloat16)
    slot_index = jnp.arange(W, dtype=jnp.int32)
    contract = (((1,), (1,)), ((), ()))
    cross_all = lax.dot_general(weighted, dose_all, contract, preferred_element_type=jnp.float32)
    power_all = lax.dot_general(weight_low, dose_sq, contract, preferred_element_type=jnp.float32)
    stacked = jnp.stack([cross_all, power_all], axis=0)
    variants = dose_all.shape[0]
    shifted = shift_windows(stacked, own_start, variants - W)
    cross_sum = shifted[0, :, :W]
    dose_power = shifted[1, :, :W]
    cross_sum, dose_power, expr_power = lax.psum((cross_sum, dose_power, expr_power), "col")
    scale = jnp.sqrt(jnp.float32(samples))
    zscore = jnp.where(
        slot_index[None, :] < own_valid[:, None],
        scale * cross_sum / jnp.sqrt(dose_power * expr_power[:, None]),
        0.0,
    )
    width_part = W // lax.axis_size("col")
    return lax.dynamic_slice_in_dim(zscore, lax.axis_index("col") * width_part, width_part, 1)


def route_kernel(
    place_ref, owner_any, expr_any, vecs_any, dose_any,
    ahead_ref, e46_ref, e2_ref, e0_ref, half_ref, bucket_ref,
    owner_ref, expr_ref, sems,
):
    row, core = place_ref[0], place_ref[1]
    half = vecs_any.shape[1]
    part = expr_ref.shape[0]
    variants = half_ref.shape[1]
    pairs = (
        (owner_any, owner_ref),
        (expr_any.at[pl.ds(pl.multiple_of(core * part, part), part)], expr_ref),
        (vecs_any, ahead_ref.at[:, pl.ds(0, half)]),
        (dose_any.at[:, pl.ds(pl.multiple_of(core * variants, LANES), variants)], half_ref),
    )
    copies = [pltpu.make_async_copy(a, b, sems.at[i]) for i, (a, b) in enumerate(pairs)]
    for copy in copies:
        copy.start()
    slices = owner_ref.shape[0]
    capacity = LANES // slices
    before = lax.broadcasted_iota(jnp.int32, (LANES, LANES), 0) < lax.broadcasted_iota(
        jnp.int32, (LANES, LANES), 1
    )
    before = before.astype(bf16)
    slot = lax.broadcasted_iota(jnp.int32, (LANES, LANES), 0)
    copies[0].wait()
    owner = owner_ref[...]
    rank = jnp.zeros(owner.shape, f32)
    for o in range(slices):
        same = (owner == o).astype(f32)
        rank += same * jnp.dot(same.astype(bf16), before, preferred_element_type=f32)
    bucket = (owner ^ row) * capacity + rank.astype(jnp.int32)
    bucket_ref[...] = bucket
    copies[1].wait()
    sorted_slices = []
    for s in range(slices):
        here = bucket[s : s + 1, :]
        pick = (slot == here).astype(bf16)
        sorted_slices.append(
            lax.dot_general(pick, expr_ref[:, s * LANES : (s + 1) * LANES], NT, preferred_element_type=f32)
        )
    left, right = slice(0, LANES), slice(LANES, 2 * LANES)
    upper, lower = slice(0, part), slice(part, 2 * part)
    targets = {
        0: (e0_ref, upper, left),
        1: (ahead_ref, upper, slice(half, half + LANES)),
        2: (e2_ref, upper, left),
        3: (ahead_ref, upper, slice(half + LANES, half + 2 * LANES)),
        4: (e46_ref, upper, left),
        5: (ahead_ref, lower, slice(half, half + LANES)),
        6: (e46_ref, upper, right),
        7: (ahead_ref, lower, slice(half + LANES, half + 2 * LANES)),
    }
    for m, (ref, down, side) in targets.items():
        block = jnp.concatenate([x[m * capacity : (m + 1) * capacity, :] for x in sorted_slices], axis=0)
        ref[down, side] = block.T.astype(bf16)
    for copy in copies[2:]:
        copy.wait()


def gene_kernel(bucket_ref, delta_ref, start_ref, valid_ref, vals_ref, gene_ref, terms_ref):
    slices = bucket_ref.shape[0]
    capacity = LANES // slices
    own_slot = lax.broadcasted_iota(jnp.int32, (capacity, LANES), 0)
    lane = lax.broadcasted_iota(jnp.int32, (capacity, LANES), 1)
    for s in range(slices):
        mine = (own_slot == bucket_ref[s : s + 1, :]).astype(f32)
        figures = jnp.zeros((capacity, LANES), f32)
        for i, ref in enumerate((delta_ref, start_ref, valid_ref)):
            line = ref[s : s + 1, :].astype(f32)
            figures = jnp.where(lane == i, jnp.sum(mine * line, axis=1, keepdims=True), figures)
        gene_ref[s * capacity : (s + 1) * capacity, :] = figures
    vals = vals_ref[...]
    high = vals.astype(bf16).astype(f32)
    middle = (vals - high).astype(bf16).astype(f32)
    term = lax.broadcasted_iota(jnp.int32, terms_ref.shape, 0)
    terms = jnp.where(term == 0, high, jnp.where(term == 1, middle, jnp.where(term == 2, vals - high - middle, 0.0)))
    terms_ref[...] = terms.astype(bf16)


def second_kernel(ahead_ref, r1_ref, e46_ref, out_ref):
    half = out_ref.shape[1] // 2 - LANES
    part = e46_ref.shape[0]
    out_ref[:, :half] = ahead_ref[:, :half]
    out_ref[:, half : 2 * half] = r1_ref[:, :half]
    out_ref[:part, 2 * half :] = e46_ref[...]
    out_ref[part:, 2 * half :] = r1_ref[part:, half:]


def copy_kernel(d0_ref, d4_ref, after_any, pair_ref, far_ref):
    variants = d0_ref.shape[1]
    pair_ref[:, :variants] = d0_ref[...]
    pair_ref[:, variants:] = d4_ref[...]
    far_ref[...] = d4_ref[...]


def third_kernel(ahead_ref, r1_ref, r4_ref, e2_ref, e0_ref, terms_ref, far_any, out_ref, kept_ref):
    half = terms_ref.shape[1]
    part = e0_ref.shape[0]
    for ref, own, at in ((out_ref, e2_ref, LANES), (kept_ref, e0_ref, 0)):
        ref[:, :half] = ahead_ref[:, :half]
        ref[:, half : 2 * half] = r1_ref[:, :half]
        ref[:, 2 * half : 4 * half] = r4_ref[:, : 2 * half]
        side = slice(2 * half + at, 2 * half + at + LANES)
        left, right = slice(4 * half, 4 * half + LANES), slice(4 * half + LANES, 4 * half + 2 * LANES)
        ref[:part, left] = own[...]
        ref[:part, right] = r1_ref[:part, half + at : half + at + LANES]
        ref[part:, left] = r4_ref[:part, side]
        ref[part:, right] = r4_ref[part:, side]
    width = out_ref.shape[1]
    terms = terms_ref.shape[0]
    kept_ref[:terms, width:] = terms_ref[...]
    kept_ref[terms:, width:] = jnp.zeros((kept_ref.shape[0] - terms, half), bf16)


def rotate(place_ref, refs, turned_ref, data_scr):
    samples = refs[0].shape[0]
    half = turned_ref.shape[0] // 2
    part = samples // 2
    core = place_ref[1]
    for c, ref in enumerate(refs):
        side = core if c == 0 else 1 - core
        for i in range(4):
            turned_ref[c * half : (c + 1) * half, i * samples : (i + 1) * samples] = (
                ref[:, i * half : (i + 1) * half].astype(f32).T.astype(bf16)
            )
            at = 4 * half + i % 2 * LANES
            data_scr[pl.ds(pl.multiple_of(i * samples + side * part, part), part), :] = ref[
                i // 2 * part : (i // 2 + 1) * part, at : at + LANES
            ]
    data = data_scr[...].astype(f32).T.astype(bf16)
    shares = []
    for ref in refs:
        vecs = jnp.concatenate([ref[:, i * half : (i + 1) * half] for i in range(4)], axis=0)
        shares.append(jnp.dot(data, vecs, preferred_element_type=f32))
    return shares


def half_kernel(place_ref, mine_ref, other_ref, d15_any, turned_ref, share_ref, data_scr):
    half = turned_ref.shape[0] // 2
    for c, share in enumerate(rotate(place_ref, (mine_ref, other_ref), turned_ref, data_scr)):
        share_ref[:, c * half : (c + 1) * half] = share


def weight_kernel(
    place_ref, kept_ref, kept2_ref, mine_ref, other_ref, share_ref, gene_ref,
    turned_ref, weighted_ref, low_ref, power_ref, data_scr,
):
    half = turned_ref.shape[0] // 2
    delta = gene_ref[:, 0:1]
    total = jnp.zeros((delta.shape[0], 1), f32)
    shares = rotate(place_ref, (mine_ref, other_ref), turned_ref, data_scr)
    width = mine_ref.shape[1]
    for c, (share, ref) in enumerate(zip(shares, (kept_ref, kept2_ref))):
        cols = slice(c * half, (c + 1) * half)
        terms = ref[0:16, width:].astype(f32)
        vals = terms[0:1] + terms[1:2] + terms[2:3]
        rotated = (share_ref[:, cols] + share).astype(bf16).astype(f32)
        weight = 1.0 / (vals + delta)
        total += jnp.sum(weight * rotated * rotated, axis=1, keepdims=True)
        weighted_ref[:, cols] = (weight * rotated).astype(bf16)
        low_ref[:, cols] = weight.astype(bf16)
    power_ref[...] = jnp.broadcast_to(total, power_ref.shape)


def score_kernel(place_ref, gene_ref, power_ref, turned_ref, turned2_ref, weighted_ref, low_ref, *refs):
    *dose_refs, keep_ref, pass_ref, dose_scr = refs
    samples, variants = dose_refs[0].shape
    chunks = [(ref, at) for ref in dose_refs for at in range(0, ref.shape[1], variants)]
    order = [0, 1, 3, 2, 4, 5, 7, 6]
    for m, (ref, at) in enumerate(chunks[i] for i in order):
        dose_scr[m * samples : (m + 1) * samples, :] = ref[:, at : at + variants]
    line = turned_ref.shape[1]
    rotated = jnp.dot(turned_ref[...], dose_scr[:line], preferred_element_type=f32)
    rotated += jnp.dot(turned2_ref[...], dose_scr[line:], preferred_element_type=f32)
    rotated = rotated.astype(bf16)
    squared = jnp.square(rotated.astype(f32)).astype(bf16)
    cross = jnp.dot(weighted_ref[...], rotated, preferred_element_type=f32)
    power = jnp.dot(low_ref[...], squared, preferred_element_type=f32)
    core = place_ref[1]
    start = gene_ref[:, 1:2].astype(jnp.int32)
    valid = gene_ref[:, 2:3].astype(jnp.int32)
    genes = cross.shape[0]
    lane = lax.broadcasted_iota(jnp.int32, (genes, LANES), 1)
    own_power = power_ref[...]
    scale = jnp.sqrt(f32(dose_scr.shape[0]))
    blocks = variants // LANES
    for out_ref, half in ((keep_ref, core), (pass_ref, 1 - core)):
        offset = start + half * LANES - core * variants
        block = offset >> 7
        shift = offset & (LANES - 1)
        need = block + (lane < shift).astype(jnp.int32)
        products = [jnp.zeros((genes, LANES), f32)] * 2
        for b in range(blocks):
            here = need == b
            parts = [array[:, b * LANES : (b + 1) * LANES] for array in (cross, power)]
            products = [jnp.where(here, part, product) for part, product in zip(parts, products)]
        inside = (need >= 0) & (need < blocks)
        score = jnp.where(inside, scale * products[0] / jnp.sqrt(products[1] * own_power), 0.0)
        score = jnp.take_along_axis(score, (lane + shift) & (LANES - 1), axis=1)
        out_ref[...] = jnp.where(lane + half * LANES < valid, score, 0.0)


def call(kernel, outs, count, scratch=(), smem=1, anywhere=0, limit=VMEM_LIMIT):
    vmem = pl.BlockSpec(memory_space=pltpu.VMEM)
    return pl.pallas_call(
        kernel,
        out_shape=[jax.ShapeDtypeStruct(*o) for o in outs],
        in_specs=[pl.BlockSpec(memory_space=pltpu.SMEM)] * smem + [vmem] * (count - smem - anywhere) + [pl.BlockSpec(memory_space=pl.ANY)] * anywhere,
        out_specs=[vmem] * len(outs),
        scratch_shapes=list(scratch),
        compiler_params=pltpu.CompilerParams(vmem_limit_bytes=limit),
    )


def near_body(eigvecs, eigvals, expression, dosage, delta, window_start, window_valid, gene_owner):
    rows = lax.axis_size("row")
    row = lax.axis_index("row")
    core = lax.axis_index("col")
    panel, half = eigvecs.shape
    part = panel // 2
    samples = panel * rows
    variants = dosage.shape[1] // 2
    place = jnp.stack([row, core]).astype(jnp.int32)

    def swap(x, m):
        return lax.ppermute(x, "row", [(i, i ^ m) for i in range(rows)])

    def other_core(x):
        return lax.ppermute(x, "col", [(0, 1), (1, 0)])

    ahead, e46, e2, e0, d0, bucket = call(
        route_kernel,
        [
            ((panel, half + 2 * LANES), bf16),
            ((part, 2 * LANES), bf16),
            ((part, LANES), bf16),
            ((part, LANES), bf16),
            ((panel, variants), bf16),
            ((rows, LANES), jnp.int32),
        ],
        5,
        scratch=[
            pltpu.VMEM((rows, LANES), jnp.int32),
            pltpu.VMEM((part, expression.shape[1]), bf16),
            pltpu.SemaphoreType.DMA((4,)),
        ],
        anywhere=4,
    )(
        place,
        *[
            pltpu.with_memory_space_constraint(x, pltpu.HBM)
            for x in (gene_owner.reshape(rows, LANES), expression, eigvecs, dosage)
        ],
    )
    gene, terms = call(gene_kernel, [((LANES, LANES), f32), ((16, half), bf16)], 5, smem=0)(
        bucket,
        delta.reshape(rows, LANES),
        window_start.reshape(rows, LANES),
        window_valid.reshape(rows, LANES),
        eigvals[None, :],
    )
    r1 = swap(ahead, 1)
    d4 = swap(d0, 4)
    d2 = swap(d0, 2)
    to4 = call(second_kernel, [((panel, 2 * half + 2 * LANES), bf16)], 3, smem=0)(ahead, r1, e46)[0]
    r4 = swap(to4, 4)
    pair, far = call(
        copy_kernel, [((panel, 2 * variants), bf16), ((panel, variants), bf16)], 3, smem=0, anywhere=1
    )(d0, d4, to4)
    d6 = swap(far, 2)
    d15 = swap(pair, 1)
    d37 = swap(jnp.concatenate([d2, d6], axis=1), 1)
    width = 4 * half + 2 * LANES
    out, kept = call(
        third_kernel, [((panel, width), bf16), ((panel, width + half), bf16)], 7, smem=0, anywhere=1
    )(ahead, r1, r4, e2, e0, terms, far)
    kept2 = other_core(kept)
    near = swap(out, 2)
    near2 = other_core(near)
    shape = ((2 * half, samples // 2), bf16)
    turned, share = call(
        half_kernel,
        [shape, ((LANES, 2 * half), f32)],
        4,
        scratch=[pltpu.VMEM((samples // 2, LANES), bf16)],
        anywhere=1,
    )(place, kept, kept2, d15)
    turned2, weighted, low, power = call(
        weight_kernel,
        [shape, ((LANES, 2 * half), bf16), ((LANES, 2 * half), bf16), ((LANES, LANES), f32)],
        7,
        scratch=[pltpu.VMEM((samples // 2, LANES), bf16)],
    )(place, kept, kept2, near, near2, share, gene)
    keep, passed = call(
        score_kernel,
        [((LANES, LANES), f32)] * 2,
        13,
        scratch=[pltpu.VMEM((samples, variants), bf16)],
    )(place, gene, power, turned, turned2, weighted, low, d0, d15, d4, d2, d37, d6)
    return keep + other_core(passed)


def body(eigvecs, eigvals, expression, dosage, delta, window_start, window_valid, gene_owner):
    rows = lax.axis_size("row")
    samples = eigvecs.shape[0] * rows
    own = expression.shape[1] // rows
    fits = (
        lax.axis_size("col") == 2
        and own == LANES
        and W == 2 * LANES
        and rows == 8
        and dosage.shape[1] % (2 * LANES) == 0
        and samples * (samples + dosage.shape[1]) <= VMEM_LIMIT // 16
    )
    run = near_body if fits else wide_body
    return run(eigvecs, eigvals, expression, dosage, delta, window_start, window_valid, gene_owner)


def solution(mesh):
    placed = (
        P(("groups", "row"), "col"),
        P(("groups", "col")),
        P(("groups", "row"), None),
        P(("groups", "row"), None),
        P("groups"),
        P("groups"),
        P("groups"),
        P("groups"),
    )
    return jax.shard_map(
        body, mesh=mesh, in_specs=placed, out_specs=P(("groups", "row"), "col"), check_vma=False
    )
```

```python
import functools

import jax
import jax.numpy as jnp
from jax import lax
from jax.experimental import pallas as pl
from jax.experimental.pallas import tpu as pltpu
from jax.sharding import PartitionSpec as P

W = 256
LANES = 128
VMEM_LIMIT = 32 * 1024 * 1024
NT = (((1,), (1,)), ((), ()))
f32 = jnp.float32
bf16 = jnp.bfloat16


def owner_listing(gene_owner):
    total = gene_owner.shape[0]
    return jnp.argsort(gene_owner * total + jnp.arange(total, dtype=jnp.int32))


def earlier_equal(labels):
    places = jnp.arange(labels.shape[0], dtype=jnp.int32)
    same = labels[:, None] == labels[None, :]
    before = places[:, None] > places[None, :]
    return jnp.sum((same & before).astype(jnp.int32), axis=1)


def shift_windows(tables, starts, largest):
    moved_tables = tables
    step_size = 1
    while step_size <= largest:
        bit_set = starts // step_size % 2 == 1
        filler = jnp.zeros(moved_tables.shape[:-1] + (step_size,), moved_tables.dtype)
        moved = jnp.concatenate([moved_tables[..., step_size:], filler], axis=-1)
        moved_tables = jnp.where(bit_set[None, :, None], moved, moved_tables)
        step_size = step_size * 2
    return moved_tables


def wide_body(eigvecs, eigvals, expression, dosage, delta, window_start, window_valid, gene_owner):
    row_count = lax.axis_size("row")
    row_index = lax.axis_index("row")
    genes_all = expression.shape[1]
    own_count = genes_all // row_count
    half_samples = eigvecs.shape[1]
    samples = half_samples * lax.axis_size("col")
    owner_order = owner_listing(gene_owner)
    my_genes = lax.dynamic_slice_in_dim(owner_order, row_index * own_count, own_count)
    expr_panel, dose_panel = (
        lax.all_to_all(expression, "row", split_axis=1, concat_axis=0, tiled=True),
        lax.all_to_all(dosage, "row", split_axis=1, concat_axis=0, tiled=True),
    )
    panel_data = jnp.concatenate([expr_panel, dose_panel], axis=1)
    rotated = lax.dot_general(
        panel_data,
        lax.all_gather(eigvecs, "row", axis=0, tiled=True),
        (((0,), (0,)), ((), ())),
        preferred_element_type=jnp.float32,
    ).astype(jnp.bfloat16)
    rot_expr = rotated[:own_count]
    rot_dose = rotated[own_count:]
    dose_all = lax.all_gather(rot_dose, "row", axis=0, tiled=True)
    capacity = max(2, own_count // row_count)
    destination = lax.dynamic_slice_in_dim(gene_owner, row_index * own_count, own_count)
    position = destination * capacity + earlier_equal(destination)
    slot_ids = jnp.arange(row_count * capacity, dtype=jnp.int32)
    placement_map = (slot_ids[:, None] == position[None, :]).astype(jnp.bfloat16)
    buckets = jnp.dot(placement_map, rot_expr, preferred_element_type=jnp.float32).astype(
        jnp.bfloat16
    )
    received = lax.all_to_all(buckets, "row", split_axis=0, concat_axis=0, tiled=True)
    source = my_genes // own_count
    owned_expr = jnp.take(received, source * capacity + earlier_equal(source), axis=0)
    own_delta = jnp.take(delta, my_genes)
    own_start = jnp.take(window_start, my_genes)
    own_valid = jnp.take(window_valid, my_genes)
    weight = 1.0 / (eigvals[None, :] + own_delta[:, None])
    expr_float = owned_expr.astype(jnp.float32)
    expr_power = jnp.sum(weight * expr_float * expr_float, axis=1)
    weighted = (weight * expr_float).astype(jnp.bfloat16)
    weight_low = weight.astype(jnp.bfloat16)
    dose_sq = jnp.square(dose_all.astype(jnp.float32)).astype(jnp.bfloat16)
    slot_index = jnp.arange(W, dtype=jnp.int32)
    contract = (((1,), (1,)), ((), ()))
    cross_all = lax.dot_general(weighted, dose_all, contract, preferred_element_type=jnp.float32)
    power_all = lax.dot_general(weight_low, dose_sq, contract, preferred_element_type=jnp.float32)
    stacked = jnp.stack([cross_all, power_all], axis=0)
    variants = dose_all.shape[0]
    shifted = shift_windows(stacked, own_start, variants - W)
    cross_sum = shifted[0, :, :W]
    dose_power = shifted[1, :, :W]
    cross_sum, dose_power, expr_power = lax.psum((cross_sum, dose_power, expr_power), "col")
    scale = jnp.sqrt(jnp.float32(samples))
    zscore = jnp.where(
        slot_index[None, :] < own_valid[:, None],
        scale * cross_sum / jnp.sqrt(dose_power * expr_power[:, None]),
        0.0,
    )
    width_part = W // lax.axis_size("col")
    return lax.dynamic_slice_in_dim(zscore, lax.axis_index("col") * width_part, width_part, 1)


def route_kernel(
    place_ref, owner_any, expr_any, vecs_any, dose_any,
    ahead_ref, e46_ref, e2_ref, e0_ref, half_ref, bucket_ref,
    owner_ref, expr_ref, sems,
):
    row, core = place_ref[0], place_ref[1]
    half = vecs_any.shape[1]
    part = expr_ref.shape[0]
    variants = half_ref.shape[1]
    pairs = (
        (owner_any, owner_ref),
        (expr_any.at[pl.ds(pl.multiple_of(core * part, part), part)], expr_ref),
        (vecs_any, ahead_ref.at[:, pl.ds(0, half)]),
        (dose_any.at[:, pl.ds(pl.multiple_of(core * variants, LANES), variants)], half_ref),
    )
    copies = [pltpu.make_async_copy(a, b, sems.at[i]) for i, (a, b) in enumerate(pairs)]
    for copy in copies:
        copy.start()
    slices = owner_ref.shape[0]
    capacity = LANES // slices
    before = lax.broadcasted_iota(jnp.int32, (LANES, LANES), 0) < lax.broadcasted_iota(
        jnp.int32, (LANES, LANES), 1
    )
    before = before.astype(bf16)
    slot = lax.broadcasted_iota(jnp.int32, (LANES, LANES), 0)
    copies[0].wait()
    owner = owner_ref[...]
    rank = jnp.zeros(owner.shape, f32)
    for o in range(slices):
        same = (owner == o).astype(f32)
        rank += same * jnp.dot(same.astype(bf16), before, preferred_element_type=f32)
    bucket = (owner ^ row) * capacity + rank.astype(jnp.int32)
    bucket_ref[...] = bucket
    copies[1].wait()
    sorted_slices = []
    for s in range(slices):
        here = bucket[s : s + 1, :]
        pick = (slot == here).astype(bf16)
        sorted_slices.append(
            lax.dot_general(pick, expr_ref[:, s * LANES : (s + 1) * LANES], NT, preferred_element_type=f32)
        )
    left, right = slice(0, LANES), slice(LANES, 2 * LANES)
    upper, lower = slice(0, part), slice(part, 2 * part)
    targets = {
        0: (e0_ref, upper, left),
        1: (ahead_ref, upper, slice(half, half + LANES)),
        2: (e2_ref, upper, left),
        3: (ahead_ref, upper, slice(half + LANES, half + 2 * LANES)),
        4: (e46_ref, upper, left),
        5: (ahead_ref, lower, slice(half, half + LANES)),
        6: (e46_ref, upper, right),
        7: (ahead_ref, lower, slice(half + LANES, half + 2 * LANES)),
    }
    for m, (ref, down, side) in targets.items():
        block = jnp.concatenate([x[m * capacity : (m + 1) * capacity, :] for x in sorted_slices], axis=0)
        ref[down, side] = block.T.astype(bf16)
    for copy in copies[2:]:
        copy.wait()


def gene_kernel(bucket_ref, delta_ref, start_ref, valid_ref, vals_ref, gene_ref, terms_ref):
    slices = bucket_ref.shape[0]
    capacity = LANES // slices
    own_slot = lax.broadcasted_iota(jnp.int32, (capacity, LANES), 0)
    lane = lax.broadcasted_iota(jnp.int32, (capacity, LANES), 1)
    for s in range(slices):
        mine = (own_slot == bucket_ref[s : s + 1, :]).astype(f32)
        figures = jnp.zeros((capacity, LANES), f32)
        for i, ref in enumerate((delta_ref, start_ref, valid_ref)):
            line = ref[s : s + 1, :].astype(f32)
            figures = jnp.where(lane == i, jnp.sum(mine * line, axis=1, keepdims=True), figures)
        gene_ref[s * capacity : (s + 1) * capacity, :] = figures
    vals = vals_ref[...]
    high = vals.astype(bf16).astype(f32)
    middle = (vals - high).astype(bf16).astype(f32)
    term = lax.broadcasted_iota(jnp.int32, terms_ref.shape, 0)
    terms = jnp.where(term == 0, high, jnp.where(term == 1, middle, jnp.where(term == 2, vals - high - middle, 0.0)))
    terms_ref[...] = terms.astype(bf16)


def second_kernel(ahead_ref, r1_ref, e46_ref, out_ref):
    half = out_ref.shape[1] // 2 - LANES
    part = e46_ref.shape[0]
    out_ref[:, :half] = ahead_ref[:, :half]
    out_ref[:, half : 2 * half] = r1_ref[:, :half]
    out_ref[:part, 2 * half :] = e46_ref[...]
    out_ref[part:, 2 * half :] = r1_ref[part:, half:]


def copy_kernel(d0_ref, d4_ref, after_any, pair_ref, far_ref):
    variants = d0_ref.shape[1]
    pair_ref[:, :variants] = d0_ref[...]
    pair_ref[:, variants:] = d4_ref[...]
    far_ref[...] = d4_ref[...]


def third_kernel(ahead_ref, r1_ref, r4_ref, e2_ref, e0_ref, terms_ref, far_any, d2_any, out_ref, kept_ref):
    half = terms_ref.shape[1]
    part = e0_ref.shape[0]
    for ref, own, at in ((out_ref, e2_ref, LANES), (kept_ref, e0_ref, 0)):
        ref[:, :half] = ahead_ref[:, :half]
        ref[:, half : 2 * half] = r1_ref[:, :half]
        ref[:, 2 * half : 4 * half] = r4_ref[:, : 2 * half]
        side = slice(2 * half + at, 2 * half + at + LANES)
        left, right = slice(4 * half, 4 * half + LANES), slice(4 * half + LANES, 4 * half + 2 * LANES)
        ref[:part, left] = own[...]
        ref[:part, right] = r1_ref[:part, half + at : half + at + LANES]
        ref[part:, left] = r4_ref[:part, side]
        ref[part:, right] = r4_ref[part:, side]
    width = out_ref.shape[1]
    terms = terms_ref.shape[0]
    kept_ref[:terms, width:] = terms_ref[...]
    kept_ref[terms:, width:] = jnp.zeros((kept_ref.shape[0] - terms, half), bf16)


def rotate(place_ref, refs, turned_ref, data_scr):
    samples = refs[0].shape[0]
    half = turned_ref.shape[0] // 2
    part = samples // 2
    core = place_ref[1]
    for c, ref in enumerate(refs):
        side = core if c == 0 else 1 - core
        for i in range(4):
            turned_ref[c * half : (c + 1) * half, i * samples : (i + 1) * samples] = (
                ref[:, i * half : (i + 1) * half].astype(f32).T.astype(bf16)
            )
            at = 4 * half + i % 2 * LANES
            data_scr[pl.ds(pl.multiple_of(i * samples + side * part, part), part), :] = ref[
                i // 2 * part : (i // 2 + 1) * part, at : at + LANES
            ]
    data = data_scr[...].astype(f32).T.astype(bf16)
    shares = []
    for ref in refs:
        vecs = jnp.concatenate([ref[:, i * half : (i + 1) * half] for i in range(4)], axis=0)
        shares.append(jnp.dot(data, vecs, preferred_element_type=f32))
    return shares


def half_kernel(place_ref, mine_ref, other_ref, d15_any, turned_ref, share_ref, data_scr):
    half = turned_ref.shape[0] // 2
    for c, share in enumerate(rotate(place_ref, (mine_ref, other_ref), turned_ref, data_scr)):
        share_ref[:, c * half : (c + 1) * half] = share


def weight_kernel(
    place_ref, kept_ref, kept2_ref, mine_ref, other_ref, share_ref, gene_ref,
    turned_ref, weighted_ref, low_ref, power_ref, data_scr,
):
    half = turned_ref.shape[0] // 2
    delta = gene_ref[:, 0:1]
    total = jnp.zeros((delta.shape[0], 1), f32)
    shares = rotate(place_ref, (mine_ref, other_ref), turned_ref, data_scr)
    width = mine_ref.shape[1]
    for c, (share, ref) in enumerate(zip(shares, (kept_ref, kept2_ref))):
        cols = slice(c * half, (c + 1) * half)
        terms = ref[0:16, width:].astype(f32)
        vals = terms[0:1] + terms[1:2] + terms[2:3]
        rotated = (share_ref[:, cols] + share).astype(bf16).astype(f32)
        weight = 1.0 / (vals + delta)
        total += jnp.sum(weight * rotated * rotated, axis=1, keepdims=True)
        weighted_ref[:, cols] = (weight * rotated).astype(bf16)
        low_ref[:, cols] = weight.astype(bf16)
    power_ref[...] = jnp.broadcast_to(total, power_ref.shape)


def window(place_ref, gene_ref, power_ref, cross, power, half, samples):
    core = place_ref[1]
    start = gene_ref[:, 1:2].astype(jnp.int32)
    valid = gene_ref[:, 2:3].astype(jnp.int32)
    genes = cross.shape[0]
    lane = lax.broadcasted_iota(jnp.int32, (genes, LANES), 1)
    own_power = power_ref[...]
    scale = jnp.sqrt(f32(samples))
    variants = cross.shape[1]
    blocks = variants // LANES
    offset = start + half * LANES - core * variants
    block = offset >> 7
    shift = offset & (LANES - 1)
    need = block + (lane < shift).astype(jnp.int32)
    products = [jnp.zeros((genes, LANES), f32)] * 2
    for b in range(blocks):
        here = need == b
        parts = [array[:, b * LANES : (b + 1) * LANES] for array in (cross, power)]
        products = [jnp.where(here, part, product) for part, product in zip(parts, products)]
    inside = (need >= 0) & (need < blocks)
    score = jnp.where(inside, scale * products[0] / jnp.sqrt(products[1] * own_power), 0.0)
    score = jnp.take_along_axis(score, (lane + shift) & (LANES - 1), axis=1)
    return jnp.where(lane + half * LANES < valid, score, 0.0)


def score_kernel(place_ref, gene_ref, power_ref, turned_ref, turned2_ref, weighted_ref, low_ref, *refs):
    *dose_refs, cross_ref, product_ref, pass_ref, dose_scr = refs
    samples, variants = dose_refs[0].shape
    chunks = [(ref, at) for ref in dose_refs for at in range(0, ref.shape[1], variants)]
    order = [0, 1, 3, 2, 4, 5, 7, 6]
    for m, (ref, at) in enumerate(chunks[i] for i in order):
        dose_scr[m * samples : (m + 1) * samples, :] = ref[:, at : at + variants]
    line = turned_ref.shape[1]
    rotated = jnp.dot(turned_ref[...], dose_scr[:line], preferred_element_type=f32)
    rotated += jnp.dot(turned2_ref[...], dose_scr[line:], preferred_element_type=f32)
    rotated = rotated.astype(bf16)
    squared = jnp.square(rotated.astype(f32)).astype(bf16)
    cross = jnp.dot(weighted_ref[...], rotated, preferred_element_type=f32)
    power = jnp.dot(low_ref[...], squared, preferred_element_type=f32)
    cross_ref[...] = cross
    product_ref[...] = power
    pass_ref[...] = window(place_ref, gene_ref, power_ref, cross, power, 1 - place_ref[1], dose_scr.shape[0])


def keep_kernel(place_ref, gene_ref, power_ref, cross_ref, product_ref, keep_ref, *, samples):
    keep_ref[...] = window(
        place_ref, gene_ref, power_ref, cross_ref[...], product_ref[...], place_ref[1], samples
    )


def call(kernel, outs, count, scratch=(), smem=1, anywhere=0, limit=VMEM_LIMIT):
    vmem = pl.BlockSpec(memory_space=pltpu.VMEM)
    return pl.pallas_call(
        kernel,
        out_shape=[jax.ShapeDtypeStruct(*o) for o in outs],
        in_specs=[pl.BlockSpec(memory_space=pltpu.SMEM)] * smem + [vmem] * (count - smem - anywhere) + [pl.BlockSpec(memory_space=pl.ANY)] * anywhere,
        out_specs=[vmem] * len(outs),
        scratch_shapes=list(scratch),
        compiler_params=pltpu.CompilerParams(vmem_limit_bytes=limit),
    )


def near_body(eigvecs, eigvals, expression, dosage, delta, window_start, window_valid, gene_owner):
    rows = lax.axis_size("row")
    row = lax.axis_index("row")
    core = lax.axis_index("col")
    panel, half = eigvecs.shape
    part = panel // 2
    samples = panel * rows
    variants = dosage.shape[1] // 2
    place = jnp.stack([row, core]).astype(jnp.int32)

    def swap(x, m):
        return lax.ppermute(x, "row", [(i, i ^ m) for i in range(rows)])

    def other_core(x):
        return lax.ppermute(x, "col", [(0, 1), (1, 0)])

    ahead, e46, e2, e0, d0, bucket = call(
        route_kernel,
        [
            ((panel, half + 2 * LANES), bf16),
            ((part, 2 * LANES), bf16),
            ((part, LANES), bf16),
            ((part, LANES), bf16),
            ((panel, variants), bf16),
            ((rows, LANES), jnp.int32),
        ],
        5,
        scratch=[
            pltpu.VMEM((rows, LANES), jnp.int32),
            pltpu.VMEM((part, expression.shape[1]), bf16),
            pltpu.SemaphoreType.DMA((4,)),
        ],
        anywhere=4,
    )(
        place,
        *[
            pltpu.with_memory_space_constraint(x, pltpu.HBM)
            for x in (gene_owner.reshape(rows, LANES), expression, eigvecs, dosage)
        ],
    )
    gene, terms = call(gene_kernel, [((LANES, LANES), f32), ((16, half), bf16)], 5, smem=0)(
        bucket,
        delta.reshape(rows, LANES),
        window_start.reshape(rows, LANES),
        window_valid.reshape(rows, LANES),
        eigvals[None, :],
    )
    r1 = swap(ahead, 1)
    d4 = swap(d0, 4)
    d2 = swap(d0, 2)
    to4 = call(second_kernel, [((panel, 2 * half + 2 * LANES), bf16)], 3, smem=0)(ahead, r1, e46)[0]
    r4 = swap(to4, 4)
    pair, far = call(
        copy_kernel, [((panel, 2 * variants), bf16), ((panel, variants), bf16)], 3, smem=0, anywhere=1
    )(d0, d4, to4)
    d6 = swap(far, 2)
    d15 = swap(pair, 1)
    d37 = swap(jnp.concatenate([d2, d6], axis=1), 1)
    width = 4 * half + 2 * LANES
    out, kept = call(
        third_kernel, [((panel, width), bf16), ((panel, width + half), bf16)], 8, smem=0, anywhere=2
    )(ahead, r1, r4, e2, e0, terms, far, d2)
    kept2 = other_core(kept)
    near = swap(out, 2)
    near2 = other_core(near)
    shape = ((2 * half, samples // 2), bf16)
    turned, share = call(
        half_kernel,
        [shape, ((LANES, 2 * half), f32)],
        4,
        scratch=[pltpu.VMEM((samples // 2, LANES), bf16)],
        anywhere=1,
    )(place, kept, kept2, d15)
    turned2, weighted, low, power = call(
        weight_kernel,
        [shape, ((LANES, 2 * half), bf16), ((LANES, 2 * half), bf16), ((LANES, LANES), f32)],
        7,
        scratch=[pltpu.VMEM((samples // 2, LANES), bf16)],
    )(place, kept, kept2, near, near2, share, gene)
    cross, product, passed = call(
        score_kernel,
        [((LANES, variants), f32)] * 2 + [((LANES, LANES), f32)],
        13,
        scratch=[pltpu.VMEM((samples, variants), bf16)],
    )(place, gene, power, turned, turned2, weighted, low, d0, d15, d4, d2, d37, d6)
    keep = call(functools.partial(keep_kernel, samples=samples), [((LANES, LANES), f32)], 5)(
        place, gene, power, cross, product
    )[0]
    return keep + other_core(passed)


def body(eigvecs, eigvals, expression, dosage, delta, window_start, window_valid, gene_owner):
    rows = lax.axis_size("row")
    samples = eigvecs.shape[0] * rows
    own = expression.shape[1] // rows
    fits = (
        lax.axis_size("col") == 2
        and own == LANES
        and W == 2 * LANES
        and rows == 8
        and dosage.shape[1] % (2 * LANES) == 0
        and samples * (samples + dosage.shape[1]) <= VMEM_LIMIT // 16
    )
    run = near_body if fits else wide_body
    return run(eigvecs, eigvals, expression, dosage, delta, window_start, window_valid, gene_owner)


def solution(mesh):
    placed = (
        P(("groups", "row"), "col"),
        P(("groups", "col")),
        P(("groups", "row"), None),
        P(("groups", "row"), None),
        P("groups"),
        P("groups"),
        P("groups"),
        P("groups"),
    )
    return jax.shard_map(
        body, mesh=mesh, in_specs=placed, out_specs=P(("groups", "row"), "col"), check_vma=False
    )
```

```python
import functools

import jax
import jax.numpy as jnp
from jax import lax
from jax.experimental import pallas as pl
from jax.experimental.pallas import tpu as pltpu
from jax.sharding import PartitionSpec as P

W = 256
LANES = 128
VMEM_LIMIT = 32 * 1024 * 1024
NT = (((1,), (1,)), ((), ()))
f32 = jnp.float32
bf16 = jnp.bfloat16


def owner_listing(gene_owner):
    total = gene_owner.shape[0]
    return jnp.argsort(gene_owner * total + jnp.arange(total, dtype=jnp.int32))


def earlier_equal(labels):
    places = jnp.arange(labels.shape[0], dtype=jnp.int32)
    same = labels[:, None] == labels[None, :]
    before = places[:, None] > places[None, :]
    return jnp.sum((same & before).astype(jnp.int32), axis=1)


def shift_windows(tables, starts, largest):
    moved_tables = tables
    step_size = 1
    while step_size <= largest:
        bit_set = starts // step_size % 2 == 1
        filler = jnp.zeros(moved_tables.shape[:-1] + (step_size,), moved_tables.dtype)
        moved = jnp.concatenate([moved_tables[..., step_size:], filler], axis=-1)
        moved_tables = jnp.where(bit_set[None, :, None], moved, moved_tables)
        step_size = step_size * 2
    return moved_tables


def wide_body(eigvecs, eigvals, expression, dosage, delta, window_start, window_valid, gene_owner):
    row_count = lax.axis_size("row")
    row_index = lax.axis_index("row")
    genes_all = expression.shape[1]
    own_count = genes_all // row_count
    half_samples = eigvecs.shape[1]
    samples = half_samples * lax.axis_size("col")
    owner_order = owner_listing(gene_owner)
    my_genes = lax.dynamic_slice_in_dim(owner_order, row_index * own_count, own_count)
    expr_panel, dose_panel = (
        lax.all_to_all(expression, "row", split_axis=1, concat_axis=0, tiled=True),
        lax.all_to_all(dosage, "row", split_axis=1, concat_axis=0, tiled=True),
    )
    panel_data = jnp.concatenate([expr_panel, dose_panel], axis=1)
    rotated = lax.dot_general(
        panel_data,
        lax.all_gather(eigvecs, "row", axis=0, tiled=True),
        (((0,), (0,)), ((), ())),
        preferred_element_type=jnp.float32,
    ).astype(jnp.bfloat16)
    rot_expr = rotated[:own_count]
    rot_dose = rotated[own_count:]
    dose_all = lax.all_gather(rot_dose, "row", axis=0, tiled=True)
    capacity = max(2, own_count // row_count)
    destination = lax.dynamic_slice_in_dim(gene_owner, row_index * own_count, own_count)
    position = destination * capacity + earlier_equal(destination)
    slot_ids = jnp.arange(row_count * capacity, dtype=jnp.int32)
    placement_map = (slot_ids[:, None] == position[None, :]).astype(jnp.bfloat16)
    buckets = jnp.dot(placement_map, rot_expr, preferred_element_type=jnp.float32).astype(
        jnp.bfloat16
    )
    received = lax.all_to_all(buckets, "row", split_axis=0, concat_axis=0, tiled=True)
    source = my_genes // own_count
    owned_expr = jnp.take(received, source * capacity + earlier_equal(source), axis=0)
    own_delta = jnp.take(delta, my_genes)
    own_start = jnp.take(window_start, my_genes)
    own_valid = jnp.take(window_valid, my_genes)
    weight = 1.0 / (eigvals[None, :] + own_delta[:, None])
    expr_float = owned_expr.astype(jnp.float32)
    expr_power = jnp.sum(weight * expr_float * expr_float, axis=1)
    weighted = (weight * expr_float).astype(jnp.bfloat16)
    weight_low = weight.astype(jnp.bfloat16)
    dose_sq = jnp.square(dose_all.astype(jnp.float32)).astype(jnp.bfloat16)
    slot_index = jnp.arange(W, dtype=jnp.int32)
    contract = (((1,), (1,)), ((), ()))
    cross_all = lax.dot_general(weighted, dose_all, contract, preferred_element_type=jnp.float32)
    power_all = lax.dot_general(weight_low, dose_sq, contract, preferred_element_type=jnp.float32)
    stacked = jnp.stack([cross_all, power_all], axis=0)
    variants = dose_all.shape[0]
    shifted = shift_windows(stacked, own_start, variants - W)
    cross_sum = shifted[0, :, :W]
    dose_power = shifted[1, :, :W]
    cross_sum, dose_power, expr_power = lax.psum((cross_sum, dose_power, expr_power), "col")
    scale = jnp.sqrt(jnp.float32(samples))
    zscore = jnp.where(
        slot_index[None, :] < own_valid[:, None],
        scale * cross_sum / jnp.sqrt(dose_power * expr_power[:, None]),
        0.0,
    )
    width_part = W // lax.axis_size("col")
    return lax.dynamic_slice_in_dim(zscore, lax.axis_index("col") * width_part, width_part, 1)


def route_kernel(
    place_ref, owner_any, expr_any, vecs_any, dose_any,
    ahead_ref, e46_ref, e2_ref, e0_ref, half_ref, bucket_ref,
    owner_ref, expr_ref, sems,
):
    row, core = place_ref[0], place_ref[1]
    half = vecs_any.shape[1]
    part = expr_ref.shape[0]
    variants = half_ref.shape[1]
    pairs = (
        (owner_any, owner_ref),
        (expr_any.at[pl.ds(pl.multiple_of(core * part, part), part)], expr_ref),
        (vecs_any, ahead_ref.at[:, pl.ds(0, half)]),
        (dose_any.at[:, pl.ds(pl.multiple_of(core * variants, LANES), variants)], half_ref),
    )
    copies = [pltpu.make_async_copy(a, b, sems.at[i]) for i, (a, b) in enumerate(pairs)]
    for copy in copies:
        copy.start()
    slices = owner_ref.shape[0]
    capacity = LANES // slices
    before = lax.broadcasted_iota(jnp.int32, (LANES, LANES), 0) < lax.broadcasted_iota(
        jnp.int32, (LANES, LANES), 1
    )
    before = before.astype(bf16)
    slot = lax.broadcasted_iota(jnp.int32, (LANES, LANES), 0)
    copies[0].wait()
    owner = owner_ref[...]
    rank = jnp.zeros(owner.shape, f32)
    for o in range(slices):
        same = (owner == o).astype(f32)
        rank += same * jnp.dot(same.astype(bf16), before, preferred_element_type=f32)
    bucket = (owner ^ row) * capacity + rank.astype(jnp.int32)
    bucket_ref[...] = bucket
    copies[1].wait()
    sorted_slices = []
    for s in range(slices):
        here = bucket[s : s + 1, :]
        pick = (slot == here).astype(bf16)
        sorted_slices.append(
            lax.dot_general(pick, expr_ref[:, s * LANES : (s + 1) * LANES], NT, preferred_element_type=f32)
        )
    left, right = slice(0, LANES), slice(LANES, 2 * LANES)
    upper, lower = slice(0, part), slice(part, 2 * part)
    targets = {
        0: (e0_ref, upper, left),
        1: (ahead_ref, upper, slice(half, half + LANES)),
        2: (e2_ref, upper, left),
        3: (ahead_ref, upper, slice(half + LANES, half + 2 * LANES)),
        4: (e46_ref, upper, left),
        5: (ahead_ref, lower, slice(half, half + LANES)),
        6: (e46_ref, upper, right),
        7: (ahead_ref, lower, slice(half + LANES, half + 2 * LANES)),
    }
    for m, (ref, down, side) in targets.items():
        block = jnp.concatenate([x[m * capacity : (m + 1) * capacity, :] for x in sorted_slices], axis=0)
        ref[down, side] = block.T.astype(bf16)
    for copy in copies[2:]:
        copy.wait()


def gene_kernel(bucket_ref, delta_ref, start_ref, valid_ref, vals_ref, gene_ref, terms_ref):
    slices = bucket_ref.shape[0]
    capacity = LANES // slices
    own_slot = lax.broadcasted_iota(jnp.int32, (capacity, LANES), 0)
    lane = lax.broadcasted_iota(jnp.int32, (capacity, LANES), 1)
    for s in range(slices):
        mine = (own_slot == bucket_ref[s : s + 1, :]).astype(f32)
        figures = jnp.zeros((capacity, LANES), f32)
        for i, ref in enumerate((delta_ref, start_ref, valid_ref)):
            line = ref[s : s + 1, :].astype(f32)
            figures = jnp.where(lane == i, jnp.sum(mine * line, axis=1, keepdims=True), figures)
        gene_ref[s * capacity : (s + 1) * capacity, :] = figures
    vals = vals_ref[...]
    high = vals.astype(bf16).astype(f32)
    middle = (vals - high).astype(bf16).astype(f32)
    term = lax.broadcasted_iota(jnp.int32, terms_ref.shape, 0)
    terms = jnp.where(term == 0, high, jnp.where(term == 1, middle, jnp.where(term == 2, vals - high - middle, 0.0)))
    terms_ref[...] = terms.astype(bf16)


def second_kernel(ahead_ref, r1_ref, e46_ref, out_ref):
    half = out_ref.shape[1] // 2 - LANES
    part = e46_ref.shape[0]
    out_ref[:, :half] = ahead_ref[:, :half]
    out_ref[:, half : 2 * half] = r1_ref[:, :half]
    out_ref[:part, 2 * half :] = e46_ref[...]
    out_ref[part:, 2 * half :] = r1_ref[part:, half:]


def copy_kernel(dose_ref, after_any, out_ref):
    out_ref[...] = dose_ref[...]


def third_kernel(ahead_ref, r1_ref, r4_ref, e2_ref, e0_ref, terms_ref, far_any, d2_any, out_ref, kept_ref):
    half = terms_ref.shape[1]
    part = e0_ref.shape[0]
    for ref, own, at in ((out_ref, e2_ref, LANES), (kept_ref, e0_ref, 0)):
        ref[:, :half] = ahead_ref[:, :half]
        ref[:, half : 2 * half] = r1_ref[:, :half]
        ref[:, 2 * half : 4 * half] = r4_ref[:, : 2 * half]
        side = slice(2 * half + at, 2 * half + at + LANES)
        left, right = slice(4 * half, 4 * half + LANES), slice(4 * half + LANES, 4 * half + 2 * LANES)
        ref[:part, left] = own[...]
        ref[:part, right] = r1_ref[:part, half + at : half + at + LANES]
        ref[part:, left] = r4_ref[:part, side]
        ref[part:, right] = r4_ref[part:, side]
    width = out_ref.shape[1]
    terms = terms_ref.shape[0]
    kept_ref[:terms, width:] = terms_ref[...]
    kept_ref[terms:, width:] = jnp.zeros((kept_ref.shape[0] - terms, half), bf16)


def rotate(place_ref, refs, turned_ref, data_scr):
    samples = refs[0].shape[0]
    half = turned_ref.shape[0] // 2
    part = samples // 2
    core = place_ref[1]
    for c, ref in enumerate(refs):
        side = core if c == 0 else 1 - core
        for i in range(4):
            turned_ref[c * half : (c + 1) * half, i * samples : (i + 1) * samples] = (
                ref[:, i * half : (i + 1) * half].astype(f32).T.astype(bf16)
            )
            at = 4 * half + i % 2 * LANES
            data_scr[pl.ds(pl.multiple_of(i * samples + side * part, part), part), :] = ref[
                i // 2 * part : (i // 2 + 1) * part, at : at + LANES
            ]
    data = data_scr[...].astype(f32).T.astype(bf16)
    shares = []
    for ref in refs:
        vecs = jnp.concatenate([ref[:, i * half : (i + 1) * half] for i in range(4)], axis=0)
        shares.append(jnp.dot(data, vecs, preferred_element_type=f32))
    return shares


def half_kernel(place_ref, mine_ref, other_ref, d153_any, turned_ref, share_ref, data_scr):
    half = turned_ref.shape[0] // 2
    for c, share in enumerate(rotate(place_ref, (mine_ref, other_ref), turned_ref, data_scr)):
        share_ref[:, c * half : (c + 1) * half] = share


def weight_kernel(
    place_ref, kept_ref, kept2_ref, mine_ref, other_ref, share_ref, gene_ref,
    turned_ref, weighted_ref, low_ref, power_ref, data_scr,
):
    half = turned_ref.shape[0] // 2
    delta = gene_ref[:, 0:1]
    total = jnp.zeros((delta.shape[0], 1), f32)
    shares = rotate(place_ref, (mine_ref, other_ref), turned_ref, data_scr)
    width = mine_ref.shape[1]
    for c, (share, ref) in enumerate(zip(shares, (kept_ref, kept2_ref))):
        cols = slice(c * half, (c + 1) * half)
        terms = ref[0:16, width:].astype(f32)
        vals = terms[0:1] + terms[1:2] + terms[2:3]
        rotated = (share_ref[:, cols] + share).astype(bf16).astype(f32)
        weight = 1.0 / (vals + delta)
        total += jnp.sum(weight * rotated * rotated, axis=1, keepdims=True)
        weighted_ref[:, cols] = (weight * rotated).astype(bf16)
        low_ref[:, cols] = weight.astype(bf16)
    power_ref[...] = jnp.broadcast_to(total, power_ref.shape)


def window(place_ref, gene_ref, power_ref, cross, power, half, samples):
    core = place_ref[1]
    start = gene_ref[:, 1:2].astype(jnp.int32)
    valid = gene_ref[:, 2:3].astype(jnp.int32)
    genes = cross.shape[0]
    lane = lax.broadcasted_iota(jnp.int32, (genes, LANES), 1)
    own_power = power_ref[...]
    scale = jnp.sqrt(f32(samples))
    variants = cross.shape[1]
    blocks = variants // LANES
    offset = start + half * LANES - core * variants
    block = offset >> 7
    shift = offset & (LANES - 1)
    need = block + (lane < shift).astype(jnp.int32)
    products = [jnp.zeros((genes, LANES), f32)] * 2
    for b in range(blocks):
        here = need == b
        parts = [array[:, b * LANES : (b + 1) * LANES] for array in (cross, power)]
        products = [jnp.where(here, part, product) for part, product in zip(parts, products)]
    inside = (need >= 0) & (need < blocks)
    score = jnp.where(inside, scale * products[0] / jnp.sqrt(products[1] * own_power), 0.0)
    score = jnp.take_along_axis(score, (lane + shift) & (LANES - 1), axis=1)
    return jnp.where(lane + half * LANES < valid, score, 0.0)


def score_kernel(place_ref, gene_ref, power_ref, turned_ref, turned2_ref, weighted_ref, low_ref, *refs):
    *dose_refs, cross_ref, product_ref, pass_ref, dose_scr = refs
    samples, variants = dose_refs[0].shape
    chunks = [(ref, at) for ref in dose_refs for at in range(0, ref.shape[1], variants)]
    order = [0, 1, 4, 2, 5, 3, 6, 7]
    for m, (ref, at) in enumerate(chunks[i] for i in order):
        dose_scr[m * samples : (m + 1) * samples, :] = ref[:, at : at + variants]
    line = turned_ref.shape[1]
    rotated = jnp.dot(turned_ref[...], dose_scr[:line], preferred_element_type=f32)
    rotated += jnp.dot(turned2_ref[...], dose_scr[line:], preferred_element_type=f32)
    rotated = rotated.astype(bf16)
    squared = jnp.square(rotated.astype(f32)).astype(bf16)
    cross = jnp.dot(weighted_ref[...], rotated, preferred_element_type=f32)
    power = jnp.dot(low_ref[...], squared, preferred_element_type=f32)
    cross_ref[...] = cross
    product_ref[...] = power
    pass_ref[...] = window(place_ref, gene_ref, power_ref, cross, power, 1 - place_ref[1], dose_scr.shape[0])


def keep_kernel(place_ref, gene_ref, power_ref, cross_ref, product_ref, keep_ref, *, samples):
    keep_ref[...] = window(
        place_ref, gene_ref, power_ref, cross_ref[...], product_ref[...], place_ref[1], samples
    )


def call(kernel, outs, count, scratch=(), smem=1, anywhere=0, limit=VMEM_LIMIT):
    vmem = pl.BlockSpec(memory_space=pltpu.VMEM)
    return pl.pallas_call(
        kernel,
        out_shape=[jax.ShapeDtypeStruct(*o) for o in outs],
        in_specs=[pl.BlockSpec(memory_space=pltpu.SMEM)] * smem + [vmem] * (count - smem - anywhere) + [pl.BlockSpec(memory_space=pl.ANY)] * anywhere,
        out_specs=[vmem] * len(outs),
        scratch_shapes=list(scratch),
        compiler_params=pltpu.CompilerParams(vmem_limit_bytes=limit),
    )


def near_body(eigvecs, eigvals, expression, dosage, delta, window_start, window_valid, gene_owner):
    rows = lax.axis_size("row")
    row = lax.axis_index("row")
    core = lax.axis_index("col")
    panel, half = eigvecs.shape
    part = panel // 2
    samples = panel * rows
    variants = dosage.shape[1] // 2
    place = jnp.stack([row, core]).astype(jnp.int32)

    def swap(x, m):
        return lax.ppermute(x, "row", [(i, i ^ m) for i in range(rows)])

    def other_core(x):
        return lax.ppermute(x, "col", [(0, 1), (1, 0)])

    ahead, e46, e2, e0, d0, bucket = call(
        route_kernel,
        [
            ((panel, half + 2 * LANES), bf16),
            ((part, 2 * LANES), bf16),
            ((part, LANES), bf16),
            ((part, LANES), bf16),
            ((panel, variants), bf16),
            ((rows, LANES), jnp.int32),
        ],
        5,
        scratch=[
            pltpu.VMEM((rows, LANES), jnp.int32),
            pltpu.VMEM((part, expression.shape[1]), bf16),
            pltpu.SemaphoreType.DMA((4,)),
        ],
        anywhere=4,
    )(
        place,
        *[
            pltpu.with_memory_space_constraint(x, pltpu.HBM)
            for x in (gene_owner.reshape(rows, LANES), expression, eigvecs, dosage)
        ],
    )
    gene, terms = call(gene_kernel, [((LANES, LANES), f32), ((16, half), bf16)], 5, smem=0)(
        bucket,
        delta.reshape(rows, LANES),
        window_start.reshape(rows, LANES),
        window_valid.reshape(rows, LANES),
        eigvals[None, :],
    )
    r1 = swap(ahead, 1)
    d4 = swap(d0, 4)
    d2 = swap(d0, 2)
    to4 = call(second_kernel, [((panel, 2 * half + 2 * LANES), bf16)], 3, smem=0)(ahead, r1, e46)[0]
    r4 = swap(to4, 4)
    far = call(copy_kernel, [((panel, variants), bf16)], 2, smem=0, anywhere=1)(d4, to4)[0]
    d6 = swap(far, 2)
    d153 = swap(jnp.concatenate([d0, d4, d2], axis=1), 1)
    d7 = swap(d6, 1)
    width = 4 * half + 2 * LANES
    out, kept = call(
        third_kernel, [((panel, width), bf16), ((panel, width + half), bf16)], 8, smem=0, anywhere=2
    )(ahead, r1, r4, e2, e0, terms, far, d2)
    kept2 = other_core(kept)
    near = swap(out, 2)
    near2 = other_core(near)
    shape = ((2 * half, samples // 2), bf16)
    turned, share = call(
        half_kernel,
        [shape, ((LANES, 2 * half), f32)],
        4,
        scratch=[pltpu.VMEM((samples // 2, LANES), bf16)],
        anywhere=1,
    )(place, kept, kept2, d153)
    turned2, weighted, low, power = call(
        weight_kernel,
        [shape, ((LANES, 2 * half), bf16), ((LANES, 2 * half), bf16), ((LANES, LANES), f32)],
        7,
        scratch=[pltpu.VMEM((samples // 2, LANES), bf16)],
    )(place, kept, kept2, near, near2, share, gene)
    cross, product, passed = call(
        score_kernel,
        [((LANES, variants), f32)] * 2 + [((LANES, LANES), f32)],
        13,
        scratch=[pltpu.VMEM((samples, variants), bf16)],
    )(place, gene, power, turned, turned2, weighted, low, d0, d153, d4, d2, d6, d7)
    keep = call(functools.partial(keep_kernel, samples=samples), [((LANES, LANES), f32)], 5)(
        place, gene, power, cross, product
    )[0]
    return keep + other_core(passed)


def body(eigvecs, eigvals, expression, dosage, delta, window_start, window_valid, gene_owner):
    rows = lax.axis_size("row")
    samples = eigvecs.shape[0] * rows
    own = expression.shape[1] // rows
    fits = (
        lax.axis_size("col") == 2
        and own == LANES
        and W == 2 * LANES
        and rows == 8
        and dosage.shape[1] % (2 * LANES) == 0
        and samples * (samples + dosage.shape[1]) <= VMEM_LIMIT // 16
    )
    run = near_body if fits else wide_body
    return run(eigvecs, eigvals, expression, dosage, delta, window_start, window_valid, gene_owner)


def solution(mesh):
    placed = (
        P(("groups", "row"), "col"),
        P(("groups", "col")),
        P(("groups", "row"), None),
        P(("groups", "row"), None),
        P("groups"),
        P("groups"),
        P("groups"),
        P("groups"),
    )
    return jax.shard_map(
        body, mesh=mesh, in_specs=placed, out_specs=P(("groups", "row"), "col"), check_vma=False
    )
```

```python
import functools

import jax
import jax.numpy as jnp
from jax import lax
from jax.experimental import pallas as pl
from jax.experimental.pallas import tpu as pltpu
from jax.sharding import PartitionSpec as P

W = 256
LANES = 128
VMEM_LIMIT = 32 * 1024 * 1024
NT = (((1,), (1,)), ((), ()))
f32 = jnp.float32
bf16 = jnp.bfloat16


def owner_listing(gene_owner):
    total = gene_owner.shape[0]
    return jnp.argsort(gene_owner * total + jnp.arange(total, dtype=jnp.int32))


def earlier_equal(labels):
    places = jnp.arange(labels.shape[0], dtype=jnp.int32)
    same = labels[:, None] == labels[None, :]
    before = places[:, None] > places[None, :]
    return jnp.sum((same & before).astype(jnp.int32), axis=1)


def shift_windows(tables, starts, largest):
    moved_tables = tables
    step_size = 1
    while step_size <= largest:
        bit_set = starts // step_size % 2 == 1
        filler = jnp.zeros(moved_tables.shape[:-1] + (step_size,), moved_tables.dtype)
        moved = jnp.concatenate([moved_tables[..., step_size:], filler], axis=-1)
        moved_tables = jnp.where(bit_set[None, :, None], moved, moved_tables)
        step_size = step_size * 2
    return moved_tables


def wide_body(eigvecs, eigvals, expression, dosage, delta, window_start, window_valid, gene_owner):
    row_count = lax.axis_size("row")
    row_index = lax.axis_index("row")
    genes_all = expression.shape[1]
    own_count = genes_all // row_count
    half_samples = eigvecs.shape[1]
    samples = half_samples * lax.axis_size("col")
    owner_order = owner_listing(gene_owner)
    my_genes = lax.dynamic_slice_in_dim(owner_order, row_index * own_count, own_count)
    expr_panel, dose_panel = (
        lax.all_to_all(expression, "row", split_axis=1, concat_axis=0, tiled=True),
        lax.all_to_all(dosage, "row", split_axis=1, concat_axis=0, tiled=True),
    )
    panel_data = jnp.concatenate([expr_panel, dose_panel], axis=1)
    rotated = lax.dot_general(
        panel_data,
        lax.all_gather(eigvecs, "row", axis=0, tiled=True),
        (((0,), (0,)), ((), ())),
        preferred_element_type=jnp.float32,
    ).astype(jnp.bfloat16)
    rot_expr = rotated[:own_count]
    rot_dose = rotated[own_count:]
    dose_all = lax.all_gather(rot_dose, "row", axis=0, tiled=True)
    capacity = max(2, own_count // row_count)
    destination = lax.dynamic_slice_in_dim(gene_owner, row_index * own_count, own_count)
    position = destination * capacity + earlier_equal(destination)
    slot_ids = jnp.arange(row_count * capacity, dtype=jnp.int32)
    placement_map = (slot_ids[:, None] == position[None, :]).astype(jnp.bfloat16)
    buckets = jnp.dot(placement_map, rot_expr, preferred_element_type=jnp.float32).astype(
        jnp.bfloat16
    )
    received = lax.all_to_all(buckets, "row", split_axis=0, concat_axis=0, tiled=True)
    source = my_genes // own_count
    owned_expr = jnp.take(received, source * capacity + earlier_equal(source), axis=0)
    own_delta = jnp.take(delta, my_genes)
    own_start = jnp.take(window_start, my_genes)
    own_valid = jnp.take(window_valid, my_genes)
    weight = 1.0 / (eigvals[None, :] + own_delta[:, None])
    expr_float = owned_expr.astype(jnp.float32)
    expr_power = jnp.sum(weight * expr_float * expr_float, axis=1)
    weighted = (weight * expr_float).astype(jnp.bfloat16)
    weight_low = weight.astype(jnp.bfloat16)
    dose_sq = jnp.square(dose_all.astype(jnp.float32)).astype(jnp.bfloat16)
    slot_index = jnp.arange(W, dtype=jnp.int32)
    contract = (((1,), (1,)), ((), ()))
    cross_all = lax.dot_general(weighted, dose_all, contract, preferred_element_type=jnp.float32)
    power_all = lax.dot_general(weight_low, dose_sq, contract, preferred_element_type=jnp.float32)
    stacked = jnp.stack([cross_all, power_all], axis=0)
    variants = dose_all.shape[0]
    shifted = shift_windows(stacked, own_start, variants - W)
    cross_sum = shifted[0, :, :W]
    dose_power = shifted[1, :, :W]
    cross_sum, dose_power, expr_power = lax.psum((cross_sum, dose_power, expr_power), "col")
    scale = jnp.sqrt(jnp.float32(samples))
    zscore = jnp.where(
        slot_index[None, :] < own_valid[:, None],
        scale * cross_sum / jnp.sqrt(dose_power * expr_power[:, None]),
        0.0,
    )
    width_part = W // lax.axis_size("col")
    return lax.dynamic_slice_in_dim(zscore, lax.axis_index("col") * width_part, width_part, 1)


def route_kernel(
    place_ref, owner_any, delta_any, start_any, valid_any, vals_any, vecs_any, expr_any, dose_any,
    ahead_ref, e46_ref, e2_ref, e0_ref, gene_ref, terms_ref, half_ref,
    owner_ref, delta_ref, start_ref, valid_ref, vals_ref, expr_ref, sems,
):
    row, core = place_ref[0], place_ref[1]
    half = vecs_any.shape[1]
    part = expr_ref.shape[0]
    variants = half_ref.shape[1]
    pairs = (
        (owner_any, owner_ref),
        (expr_any.at[pl.ds(pl.multiple_of(core * part, part), part)], expr_ref),
        (delta_any, delta_ref),
        (start_any, start_ref),
        (valid_any, valid_ref),
        (vals_any, vals_ref),
        (vecs_any, ahead_ref.at[:, pl.ds(0, half)]),
        (dose_any.at[:, pl.ds(pl.multiple_of(core * variants, LANES), variants)], half_ref),
    )
    copies = [pltpu.make_async_copy(a, b, sems.at[i]) for i, (a, b) in enumerate(pairs)]
    for copy in copies:
        copy.start()
    slices = owner_ref.shape[0]
    capacity = LANES // slices
    before = lax.broadcasted_iota(jnp.int32, (LANES, LANES), 0) < lax.broadcasted_iota(
        jnp.int32, (LANES, LANES), 1
    )
    before = before.astype(bf16)
    slot = lax.broadcasted_iota(jnp.int32, (LANES, LANES), 0)
    own_slot = lax.broadcasted_iota(jnp.int32, (capacity, LANES), 0)
    lane = lax.broadcasted_iota(jnp.int32, (capacity, LANES), 1)
    copies[0].wait()
    owner = owner_ref[...]
    rank = jnp.zeros(owner.shape, f32)
    for o in range(slices):
        same = (owner == o).astype(f32)
        rank += same * jnp.dot(same.astype(bf16), before, preferred_element_type=f32)
    bucket = (owner ^ row) * capacity + rank.astype(jnp.int32)
    for copy in copies[1:]:
        copy.wait()
    sorted_slices = []
    for s in range(slices):
        here = bucket[s : s + 1, :]
        pick = (slot == here).astype(bf16)
        sorted_slices.append(
            lax.dot_general(pick, expr_ref[:, s * LANES : (s + 1) * LANES], NT, preferred_element_type=f32)
        )
        mine = (own_slot == here).astype(f32)
        figures = jnp.zeros((capacity, LANES), f32)
        for i, ref in enumerate((delta_ref, start_ref, valid_ref)):
            line = ref[s : s + 1, :].astype(f32)
            figures = jnp.where(lane == i, jnp.sum(mine * line, axis=1, keepdims=True), figures)
        gene_ref[s * capacity : (s + 1) * capacity, :] = figures
    vals = vals_ref[...]
    high = vals.astype(bf16).astype(f32)
    middle = (vals - high).astype(bf16).astype(f32)
    term = lax.broadcasted_iota(jnp.int32, terms_ref.shape, 0)
    terms = jnp.where(term == 0, high, jnp.where(term == 1, middle, jnp.where(term == 2, vals - high - middle, 0.0)))
    terms_ref[...] = terms.astype(bf16)
    left, right = slice(0, LANES), slice(LANES, 2 * LANES)
    upper, lower = slice(0, part), slice(part, 2 * part)
    targets = {
        0: (e0_ref, upper, left),
        1: (ahead_ref, upper, slice(half, half + LANES)),
        2: (e2_ref, upper, left),
        3: (ahead_ref, upper, slice(half + LANES, half + 2 * LANES)),
        4: (e46_ref, upper, left),
        5: (ahead_ref, lower, slice(half, half + LANES)),
        6: (e46_ref, upper, right),
        7: (ahead_ref, lower, slice(half + LANES, half + 2 * LANES)),
    }
    for m, (ref, down, side) in targets.items():
        block = jnp.concatenate([x[m * capacity : (m + 1) * capacity, :] for x in sorted_slices], axis=0)
        ref[down, side] = block.T.astype(bf16)


def second_kernel(ahead_ref, r1_ref, e46_ref, out_ref):
    half = out_ref.shape[1] // 2 - LANES
    part = e46_ref.shape[0]
    out_ref[:, :half] = ahead_ref[:, :half]
    out_ref[:, half : 2 * half] = r1_ref[:, :half]
    out_ref[:part, 2 * half :] = e46_ref[...]
    out_ref[part:, 2 * half :] = r1_ref[part:, half:]


def copy_kernel(d0_ref, d4_ref, after_any, pair_ref, far_ref):
    variants = d0_ref.shape[1]
    pair_ref[:, :variants] = d0_ref[...]
    pair_ref[:, variants:] = d4_ref[...]
    far_ref[...] = d4_ref[...]


def third_kernel(ahead_ref, r1_ref, r4_ref, e2_ref, e0_ref, terms_ref, far_any, d2_any, out_ref, kept_ref):
    half = terms_ref.shape[1]
    part = e0_ref.shape[0]
    for ref, own, at in ((out_ref, e2_ref, LANES), (kept_ref, e0_ref, 0)):
        ref[:, :half] = ahead_ref[:, :half]
        ref[:, half : 2 * half] = r1_ref[:, :half]
        ref[:, 2 * half : 4 * half] = r4_ref[:, : 2 * half]
        side = slice(2 * half + at, 2 * half + at + LANES)
        left, right = slice(4 * half, 4 * half + LANES), slice(4 * half + LANES, 4 * half + 2 * LANES)
        ref[:part, left] = own[...]
        ref[:part, right] = r1_ref[:part, half + at : half + at + LANES]
        ref[part:, left] = r4_ref[:part, side]
        ref[part:, right] = r4_ref[part:, side]
    width = out_ref.shape[1]
    terms = terms_ref.shape[0]
    kept_ref[:terms, width:] = terms_ref[...]
    kept_ref[terms:, width:] = jnp.zeros((kept_ref.shape[0] - terms, half), bf16)


def rotate(place_ref, refs, turned_ref, data_scr, turned=(0, 1)):
    samples = refs[0].shape[0]
    half = turned_ref.shape[0] // len(turned)
    part = samples // 2
    core = place_ref[1]
    for c, ref in enumerate(refs):
        side = core if c == 0 else 1 - core
        for i in range(4):
            if c in turned:
                at = turned.index(c) * half
                turned_ref[at : at + half, i * samples : (i + 1) * samples] = (
                    ref[:, i * half : (i + 1) * half].astype(f32).T.astype(bf16)
                )
            at = 4 * half + i % 2 * LANES
            data_scr[pl.ds(pl.multiple_of(i * samples + side * part, part), part), :] = ref[
                i // 2 * part : (i // 2 + 1) * part, at : at + LANES
            ]
    data = data_scr[...].astype(f32).T.astype(bf16)
    shares = []
    for ref in refs:
        vecs = jnp.concatenate([ref[:, i * half : (i + 1) * half] for i in range(4)], axis=0)
        shares.append(jnp.dot(data, vecs, preferred_element_type=f32))
    return shares


def own_kernel(mine_ref, turned_ref):
    samples = mine_ref.shape[0]
    half = turned_ref.shape[0]
    for i in range(4):
        turned_ref[:, i * samples : (i + 1) * samples] = (
            mine_ref[:, i * half : (i + 1) * half].astype(f32).T.astype(bf16)
        )


def half_kernel(place_ref, mine_ref, other_ref, d15_any, turned_ref, share_ref, data_scr):
    half = turned_ref.shape[0] // 2
    for c, share in enumerate(rotate(place_ref, (mine_ref, other_ref), turned_ref, data_scr)):
        share_ref[:, c * half : (c + 1) * half] = share


def weight_kernel(
    place_ref, kept_ref, kept2_ref, mine_ref, other_ref, share_ref, gene_ref,
    turned_ref, weighted_ref, low_ref, power_ref, data_scr,
):
    half = turned_ref.shape[0]
    delta = gene_ref[:, 0:1]
    total = jnp.zeros((delta.shape[0], 1), f32)
    shares = rotate(place_ref, (mine_ref, other_ref), turned_ref, data_scr, turned=(1,))
    width = mine_ref.shape[1]
    for c, (share, ref) in enumerate(zip(shares, (kept_ref, kept2_ref))):
        cols = slice(c * half, (c + 1) * half)
        terms = ref[0:16, width:].astype(f32)
        vals = terms[0:1] + terms[1:2] + terms[2:3]
        rotated = (share_ref[:, cols] + share).astype(bf16).astype(f32)
        weight = 1.0 / (vals + delta)
        total += jnp.sum(weight * rotated * rotated, axis=1, keepdims=True)
        weighted_ref[:, cols] = (weight * rotated).astype(bf16)
        low_ref[:, cols] = weight.astype(bf16)
    power_ref[...] = jnp.broadcast_to(total, power_ref.shape)


def window(place_ref, gene_ref, power_ref, cross, power, half, samples):
    core = place_ref[1]
    start = gene_ref[:, 1:2].astype(jnp.int32)
    valid = gene_ref[:, 2:3].astype(jnp.int32)
    genes = cross.shape[0]
    lane = lax.broadcasted_iota(jnp.int32, (genes, LANES), 1)
    own_power = power_ref[...]
    scale = jnp.sqrt(f32(samples))
    variants = cross.shape[1]
    blocks = variants // LANES
    offset = start + half * LANES - core * variants
    block = offset >> 7
    shift = offset & (LANES - 1)
    need = block + (lane < shift).astype(jnp.int32)
    products = [jnp.zeros((genes, LANES), f32)] * 2
    for b in range(blocks):
        here = need == b
        parts = [array[:, b * LANES : (b + 1) * LANES] for array in (cross, power)]
        products = [jnp.where(here, part, product) for part, product in zip(parts, products)]
    inside = (need >= 0) & (need < blocks)
    score = jnp.where(inside, scale * products[0] / jnp.sqrt(products[1] * own_power), 0.0)
    score = jnp.take_along_axis(score, (lane + shift) & (LANES - 1), axis=1)
    return jnp.where(lane + half * LANES < valid, score, 0.0)


def score_kernel(place_ref, gene_ref, power_ref, turned_ref, own_ref, other_ref, weighted_ref, low_ref, *refs):
    *dose_refs, cross_ref, product_ref, pass_ref, dose_scr = refs
    samples, variants = dose_refs[0].shape
    chunks = [(ref, at) for ref in dose_refs for at in range(0, ref.shape[1], variants)]
    order = [0, 1, 3, 2, 4, 5, 7, 6]
    for m, (ref, at) in enumerate(chunks[i] for i in order):
        dose_scr[m * samples : (m + 1) * samples, :] = ref[:, at : at + variants]
    line = turned_ref.shape[1]
    rotated = jnp.dot(turned_ref[...], dose_scr[:line], preferred_element_type=f32)
    rotated += jnp.dot(jnp.concatenate([own_ref[...], other_ref[...]], axis=0), dose_scr[line:], preferred_element_type=f32)
    rotated = rotated.astype(bf16)
    squared = jnp.square(rotated.astype(f32)).astype(bf16)
    cross = jnp.dot(weighted_ref[...], rotated, preferred_element_type=f32)
    power = jnp.dot(low_ref[...], squared, preferred_element_type=f32)
    cross_ref[...] = cross
    product_ref[...] = power
    pass_ref[...] = window(place_ref, gene_ref, power_ref, cross, power, 1 - place_ref[1], dose_scr.shape[0])


def keep_kernel(place_ref, gene_ref, power_ref, cross_ref, product_ref, keep_ref, *, samples):
    keep_ref[...] = window(
        place_ref, gene_ref, power_ref, cross_ref[...], product_ref[...], place_ref[1], samples
    )


def call(kernel, outs, count, scratch=(), smem=1, anywhere=0, limit=VMEM_LIMIT):
    vmem = pl.BlockSpec(memory_space=pltpu.VMEM)
    return pl.pallas_call(
        kernel,
        out_shape=[jax.ShapeDtypeStruct(*o) for o in outs],
        in_specs=[pl.BlockSpec(memory_space=pltpu.SMEM)] * smem + [vmem] * (count - smem - anywhere) + [pl.BlockSpec(memory_space=pl.ANY)] * anywhere,
        out_specs=[vmem] * len(outs),
        scratch_shapes=list(scratch),
        compiler_params=pltpu.CompilerParams(vmem_limit_bytes=limit),
    )


def near_body(eigvecs, eigvals, expression, dosage, delta, window_start, window_valid, gene_owner):
    rows = lax.axis_size("row")
    row = lax.axis_index("row")
    core = lax.axis_index("col")
    panel, half = eigvecs.shape
    part = panel // 2
    samples = panel * rows
    variants = dosage.shape[1] // 2
    place = jnp.stack([row, core]).astype(jnp.int32)

    def swap(x, m):
        return lax.ppermute(x, "row", [(i, i ^ m) for i in range(rows)])

    def other_core(x):
        return lax.ppermute(x, "col", [(0, 1), (1, 0)])

    ahead, e46, e2, e0, gene, terms, d0 = call(
        route_kernel,
        [
            ((panel, half + 2 * LANES), bf16),
            ((part, 2 * LANES), bf16),
            ((part, LANES), bf16),
            ((part, LANES), bf16),
            ((LANES, LANES), f32),
            ((16, half), bf16),
            ((panel, variants), bf16),
        ],
        9,
        scratch=[pltpu.VMEM((rows, LANES), kind) for kind in (jnp.int32, f32, jnp.int32, jnp.int32)]
        + [pltpu.VMEM((1, half), f32), pltpu.VMEM((part, expression.shape[1]), bf16), pltpu.SemaphoreType.DMA((8,))],
        anywhere=8,
        limit=VMEM_LIMIT,
    )(
        place,
        *[
            pltpu.with_memory_space_constraint(x, pltpu.HBM)
            for x in (
                gene_owner.reshape(rows, LANES),
                delta.reshape(rows, LANES),
                window_start.reshape(rows, LANES),
                window_valid.reshape(rows, LANES),
                eigvals[None, :],
                eigvecs,
                expression,
                dosage,
            )
        ],
    )
    r1 = swap(ahead, 1)
    d4 = swap(d0, 4)
    d2 = swap(d0, 2)
    to4 = call(second_kernel, [((panel, 2 * half + 2 * LANES), bf16)], 3, smem=0)(ahead, r1, e46)[0]
    r4 = swap(to4, 4)
    pair, far = call(
        copy_kernel, [((panel, 2 * variants), bf16), ((panel, variants), bf16)], 3, smem=0, anywhere=1
    )(d0, d4, to4)
    d6 = swap(far, 2)
    d15 = swap(pair, 1)
    d37 = swap(jnp.concatenate([d2, d6], axis=1), 1)
    width = 4 * half + 2 * LANES
    out, kept = call(
        third_kernel, [((panel, width), bf16), ((panel, width + half), bf16)], 8, smem=0, anywhere=2
    )(ahead, r1, r4, e2, e0, terms, far, d2)
    kept2 = other_core(kept)
    near = swap(out, 2)
    near2 = other_core(near)
    shape = ((2 * half, samples // 2), bf16)
    turned, share = call(
        half_kernel,
        [shape, ((LANES, 2 * half), f32)],
        4,
        scratch=[pltpu.VMEM((samples // 2, LANES), bf16)],
        anywhere=1,
    )(place, kept, kept2, d15)
    own = call(own_kernel, [((half, samples // 2), bf16)], 1, smem=0)(near)[0]
    turned2, weighted, low, power = call(
        weight_kernel,
        [((half, samples // 2), bf16), ((LANES, 2 * half), bf16), ((LANES, 2 * half), bf16), ((LANES, LANES), f32)],
        7,
        scratch=[pltpu.VMEM((samples // 2, LANES), bf16)],
    )(place, kept, kept2, near, near2, share, gene)
    cross, product, passed = call(
        score_kernel,
        [((LANES, variants), f32)] * 2 + [((LANES, LANES), f32)],
        14,
        scratch=[pltpu.VMEM((samples, variants), bf16)],
    )(place, gene, power, turned, own, turned2, weighted, low, d0, d15, d4, d2, d37, d6)
    keep = call(functools.partial(keep_kernel, samples=samples), [((LANES, LANES), f32)], 5)(
        place, gene, power, cross, product
    )[0]
    return keep + other_core(passed)


def body(eigvecs, eigvals, expression, dosage, delta, window_start, window_valid, gene_owner):
    rows = lax.axis_size("row")
    samples = eigvecs.shape[0] * rows
    own = expression.shape[1] // rows
    fits = (
        lax.axis_size("col") == 2
        and own == LANES
        and W == 2 * LANES
        and rows == 8
        and dosage.shape[1] % (2 * LANES) == 0
        and samples * (samples + dosage.shape[1]) <= VMEM_LIMIT // 16
    )
    run = near_body if fits else wide_body
    return run(eigvecs, eigvals, expression, dosage, delta, window_start, window_valid, gene_owner)


def solution(mesh):
    placed = (
        P(("groups", "row"), "col"),
        P(("groups", "col")),
        P(("groups", "row"), None),
        P(("groups", "row"), None),
        P("groups"),
        P("groups"),
        P("groups"),
        P("groups"),
    )
    return jax.shard_map(
        body, mesh=mesh, in_specs=placed, out_specs=P(("groups", "row"), "col"), check_vma=False
    )
```

```python
import functools

import jax
import jax.numpy as jnp
from jax import lax
from jax.experimental import pallas as pl
from jax.experimental.pallas import tpu as pltpu
from jax.sharding import PartitionSpec as P

W = 256
LANES = 128
VMEM_LIMIT = 32 * 1024 * 1024
NT = (((1,), (1,)), ((), ()))
f32 = jnp.float32
bf16 = jnp.bfloat16


def owner_listing(gene_owner):
    total = gene_owner.shape[0]
    return jnp.argsort(gene_owner * total + jnp.arange(total, dtype=jnp.int32))


def earlier_equal(labels):
    places = jnp.arange(labels.shape[0], dtype=jnp.int32)
    same = labels[:, None] == labels[None, :]
    before = places[:, None] > places[None, :]
    return jnp.sum((same & before).astype(jnp.int32), axis=1)


def shift_windows(tables, starts, largest):
    moved_tables = tables
    step_size = 1
    while step_size <= largest:
        bit_set = starts // step_size % 2 == 1
        filler = jnp.zeros(moved_tables.shape[:-1] + (step_size,), moved_tables.dtype)
        moved = jnp.concatenate([moved_tables[..., step_size:], filler], axis=-1)
        moved_tables = jnp.where(bit_set[None, :, None], moved, moved_tables)
        step_size = step_size * 2
    return moved_tables


def wide_body(eigvecs, eigvals, expression, dosage, delta, window_start, window_valid, gene_owner):
    row_count = lax.axis_size("row")
    row_index = lax.axis_index("row")
    genes_all = expression.shape[1]
    own_count = genes_all // row_count
    half_samples = eigvecs.shape[1]
    samples = half_samples * lax.axis_size("col")
    owner_order = owner_listing(gene_owner)
    my_genes = lax.dynamic_slice_in_dim(owner_order, row_index * own_count, own_count)
    expr_panel, dose_panel = (
        lax.all_to_all(expression, "row", split_axis=1, concat_axis=0, tiled=True),
        lax.all_to_all(dosage, "row", split_axis=1, concat_axis=0, tiled=True),
    )
    panel_data = jnp.concatenate([expr_panel, dose_panel], axis=1)
    rotated = lax.dot_general(
        panel_data,
        lax.all_gather(eigvecs, "row", axis=0, tiled=True),
        (((0,), (0,)), ((), ())),
        preferred_element_type=jnp.float32,
    ).astype(jnp.bfloat16)
    rot_expr = rotated[:own_count]
    rot_dose = rotated[own_count:]
    dose_all = lax.all_gather(rot_dose, "row", axis=0, tiled=True)
    capacity = max(2, own_count // row_count)
    destination = lax.dynamic_slice_in_dim(gene_owner, row_index * own_count, own_count)
    position = destination * capacity + earlier_equal(destination)
    slot_ids = jnp.arange(row_count * capacity, dtype=jnp.int32)
    placement_map = (slot_ids[:, None] == position[None, :]).astype(jnp.bfloat16)
    buckets = jnp.dot(placement_map, rot_expr, preferred_element_type=jnp.float32).astype(
        jnp.bfloat16
    )
    received = lax.all_to_all(buckets, "row", split_axis=0, concat_axis=0, tiled=True)
    source = my_genes // own_count
    owned_expr = jnp.take(received, source * capacity + earlier_equal(source), axis=0)
    own_delta = jnp.take(delta, my_genes)
    own_start = jnp.take(window_start, my_genes)
    own_valid = jnp.take(window_valid, my_genes)
    weight = 1.0 / (eigvals[None, :] + own_delta[:, None])
    expr_float = owned_expr.astype(jnp.float32)
    expr_power = jnp.sum(weight * expr_float * expr_float, axis=1)
    weighted = (weight * expr_float).astype(jnp.bfloat16)
    weight_low = weight.astype(jnp.bfloat16)
    dose_sq = jnp.square(dose_all.astype(jnp.float32)).astype(jnp.bfloat16)
    slot_index = jnp.arange(W, dtype=jnp.int32)
    contract = (((1,), (1,)), ((), ()))
    cross_all = lax.dot_general(weighted, dose_all, contract, preferred_element_type=jnp.float32)
    power_all = lax.dot_general(weight_low, dose_sq, contract, preferred_element_type=jnp.float32)
    stacked = jnp.stack([cross_all, power_all], axis=0)
    variants = dose_all.shape[0]
    shifted = shift_windows(stacked, own_start, variants - W)
    cross_sum = shifted[0, :, :W]
    dose_power = shifted[1, :, :W]
    cross_sum, dose_power, expr_power = lax.psum((cross_sum, dose_power, expr_power), "col")
    scale = jnp.sqrt(jnp.float32(samples))
    zscore = jnp.where(
        slot_index[None, :] < own_valid[:, None],
        scale * cross_sum / jnp.sqrt(dose_power * expr_power[:, None]),
        0.0,
    )
    width_part = W // lax.axis_size("col")
    return lax.dynamic_slice_in_dim(zscore, lax.axis_index("col") * width_part, width_part, 1)


def route_kernel(
    place_ref, owner_any, expr_any, vecs_any, dose_any,
    ahead_ref, e46_ref, e2_ref, e0_ref, half_ref, bucket_ref,
    owner_ref, expr_ref, sems,
):
    row, core = place_ref[0], place_ref[1]
    half = vecs_any.shape[1]
    part = expr_ref.shape[0]
    variants = half_ref.shape[1]
    pairs = (
        (owner_any, owner_ref),
        (expr_any.at[pl.ds(pl.multiple_of(core * part, part), part)], expr_ref),
        (vecs_any, ahead_ref.at[:, pl.ds(0, half)]),
        (dose_any.at[:, pl.ds(pl.multiple_of(core * variants, LANES), variants)], half_ref),
    )
    copies = [pltpu.make_async_copy(a, b, sems.at[i]) for i, (a, b) in enumerate(pairs)]
    for copy in copies:
        copy.start()
    slices = owner_ref.shape[0]
    capacity = LANES // slices
    before = lax.broadcasted_iota(jnp.int32, (LANES, LANES), 0) < lax.broadcasted_iota(
        jnp.int32, (LANES, LANES), 1
    )
    before = before.astype(bf16)
    slot = lax.broadcasted_iota(jnp.int32, (LANES, LANES), 0)
    copies[0].wait()
    owner = owner_ref[...]
    rank = jnp.zeros(owner.shape, f32)
    for o in range(slices):
        same = (owner == o).astype(f32)
        rank += same * jnp.dot(same.astype(bf16), before, preferred_element_type=f32)
    bucket = (owner ^ row) * capacity + rank.astype(jnp.int32)
    bucket_ref[...] = bucket
    copies[1].wait()
    sorted_slices = []
    for s in range(slices):
        here = bucket[s : s + 1, :]
        pick = (slot == here).astype(bf16)
        sorted_slices.append(
            lax.dot_general(pick, expr_ref[:, s * LANES : (s + 1) * LANES], NT, preferred_element_type=f32)
        )
    left, right = slice(0, LANES), slice(LANES, 2 * LANES)
    upper, lower = slice(0, part), slice(part, 2 * part)
    targets = {
        0: (e0_ref, upper, left),
        1: (ahead_ref, upper, slice(half, half + LANES)),
        2: (e2_ref, upper, left),
        3: (ahead_ref, upper, slice(half + LANES, half + 2 * LANES)),
        4: (e46_ref, upper, left),
        5: (ahead_ref, lower, slice(half, half + LANES)),
        6: (e46_ref, upper, right),
        7: (ahead_ref, lower, slice(half + LANES, half + 2 * LANES)),
    }
    for m, (ref, down, side) in targets.items():
        block = jnp.concatenate([x[m * capacity : (m + 1) * capacity, :] for x in sorted_slices], axis=0)
        ref[down, side] = block.T.astype(bf16)
    for copy in copies[2:]:
        copy.wait()


def gene_kernel(bucket_ref, delta_ref, start_ref, valid_ref, vals_ref, gene_ref, terms_ref):
    slices = bucket_ref.shape[0]
    capacity = LANES // slices
    own_slot = lax.broadcasted_iota(jnp.int32, (capacity, LANES), 0)
    lane = lax.broadcasted_iota(jnp.int32, (capacity, LANES), 1)
    for s in range(slices):
        mine = (own_slot == bucket_ref[s : s + 1, :]).astype(f32)
        figures = jnp.zeros((capacity, LANES), f32)
        for i, ref in enumerate((delta_ref, start_ref, valid_ref)):
            line = ref[s : s + 1, :].astype(f32)
            figures = jnp.where(lane == i, jnp.sum(mine * line, axis=1, keepdims=True), figures)
        gene_ref[s * capacity : (s + 1) * capacity, :] = figures
    vals = vals_ref[...]
    high = vals.astype(bf16).astype(f32)
    middle = (vals - high).astype(bf16).astype(f32)
    term = lax.broadcasted_iota(jnp.int32, terms_ref.shape, 0)
    terms = jnp.where(term == 0, high, jnp.where(term == 1, middle, jnp.where(term == 2, vals - high - middle, 0.0)))
    terms_ref[...] = terms.astype(bf16)


def second_kernel(ahead_ref, r1_ref, e46_ref, out_ref):
    half = out_ref.shape[1] // 2 - LANES
    part = e46_ref.shape[0]
    out_ref[:, :half] = ahead_ref[:, :half]
    out_ref[:, half : 2 * half] = r1_ref[:, :half]
    out_ref[:part, 2 * half :] = e46_ref[...]
    out_ref[part:, 2 * half :] = r1_ref[part:, half:]


def copy_kernel(d0_ref, d4_ref, after_any, pair_ref, far_ref):
    variants = d0_ref.shape[1]
    pair_ref[:, :variants] = d0_ref[...]
    pair_ref[:, variants:] = d4_ref[...]
    far_ref[...] = d4_ref[...]


def third_kernel(ahead_ref, r1_ref, r4_ref, e2_ref, e0_ref, terms_ref, d2_ref, far_any, out_ref, kept_ref):
    half = terms_ref.shape[1]
    part = e0_ref.shape[0]
    kept_ref[:, :half] = ahead_ref[:, :half]
    for ref, own, at, first in ((out_ref, e2_ref, LANES, 0), (kept_ref, e0_ref, 0, half)):
        ref[:, first : first + half] = r1_ref[:, :half]
        ref[:, first + half : first + 3 * half] = r4_ref[:, : 2 * half]
        side = slice(2 * half + at, 2 * half + at + LANES)
        middle = first + 3 * half + LANES
        left, right = slice(middle - LANES, middle), slice(middle, middle + LANES)
        ref[:part, left] = own[...]
        ref[:part, right] = r1_ref[:part, half + at : half + at + LANES]
        ref[part:, left] = r4_ref[:part, side]
        ref[part:, right] = r4_ref[part:, side]
    width = out_ref.shape[1] + half
    terms = terms_ref.shape[0]
    kept_ref[:terms, width : width + half] = terms_ref[...]
    kept_ref[terms:, width : width + half] = jnp.zeros((kept_ref.shape[0] - terms, half), bf16)
    kept_ref[:, width + half :] = d2_ref[:, d2_ref.shape[1] - half :]


def rotate(place_ref, refs, turned_ref, data_scr, panels, data_at):
    samples = refs[0].shape[0]
    half = turned_ref.shape[0] // 2
    part = samples // 2
    core = place_ref[1]
    for c, ref in enumerate(refs):
        side = core if c == 0 else 1 - core
        for i in range(4):
            panel, at = panels[c][i]
            turned_ref[c * half : (c + 1) * half, i * samples : (i + 1) * samples] = (
                panel[:, at : at + half].astype(f32).T.astype(bf16)
            )
            at = data_at + i % 2 * LANES
            data_scr[pl.ds(pl.multiple_of(i * samples + side * part, part), part), :] = ref[
                i // 2 * part : (i // 2 + 1) * part, at : at + LANES
            ]
    data = data_scr[...].astype(f32).T.astype(bf16)
    shares = []
    for c in range(2):
        vecs = jnp.concatenate([panel[:, at : at + half] for panel, at in panels[c]], axis=0)
        shares.append(jnp.dot(data, vecs, preferred_element_type=f32))
    return shares


def half_kernel(place_ref, mine_ref, other_ref, d15_any, turned_ref, share_ref, data_scr):
    half = turned_ref.shape[0] // 2
    refs = (mine_ref, other_ref)
    panels = [[(ref, i * half) for i in range(4)] for ref in refs]
    for c, share in enumerate(rotate(place_ref, refs, turned_ref, data_scr, panels, 4 * half)):
        share_ref[:, c * half : (c + 1) * half] = share


def weight_kernel(
    place_ref, kept_ref, kept2_ref, mine_ref, other_ref, share_ref, gene_ref,
    turned_ref, weighted_ref, low_ref, power_ref, data_scr,
):
    half = turned_ref.shape[0] // 2
    delta = gene_ref[:, 0:1]
    total = jnp.zeros((delta.shape[0], 1), f32)
    width = mine_ref.shape[1] + half
    panels = [
        [(kept, width + half)] + [(ref, i * half) for i in range(3)]
        for kept, ref in ((kept_ref, mine_ref), (kept2_ref, other_ref))
    ]
    shares = rotate(place_ref, (mine_ref, other_ref), turned_ref, data_scr, panels, 3 * half)
    for c, (share, ref) in enumerate(zip(shares, (kept_ref, kept2_ref))):
        cols = slice(c * half, (c + 1) * half)
        terms = ref[0:16, width : width + half].astype(f32)
        vals = terms[0:1] + terms[1:2] + terms[2:3]
        rotated = (share_ref[:, cols] + share).astype(bf16).astype(f32)
        weight = 1.0 / (vals + delta)
        total += jnp.sum(weight * rotated * rotated, axis=1, keepdims=True)
        weighted_ref[:, cols] = (weight * rotated).astype(bf16)
        low_ref[:, cols] = weight.astype(bf16)
    power_ref[...] = jnp.broadcast_to(total, power_ref.shape)


def window(place_ref, gene_ref, power_ref, cross, power, half, samples):
    core = place_ref[1]
    start = gene_ref[:, 1:2].astype(jnp.int32)
    valid = gene_ref[:, 2:3].astype(jnp.int32)
    genes = cross.shape[0]
    lane = lax.broadcasted_iota(jnp.int32, (genes, LANES), 1)
    own_power = power_ref[...]
    scale = jnp.sqrt(f32(samples))
    variants = cross.shape[1]
    blocks = variants // LANES
    offset = start + half * LANES - core * variants
    block = offset >> 7
    shift = offset & (LANES - 1)
    need = block + (lane < shift).astype(jnp.int32)
    products = [jnp.zeros((genes, LANES), f32)] * 2
    for b in range(blocks):
        here = need == b
        parts = [array[:, b * LANES : (b + 1) * LANES] for array in (cross, power)]
        products = [jnp.where(here, part, product) for part, product in zip(parts, products)]
    inside = (need >= 0) & (need < blocks)
    score = jnp.where(inside, scale * products[0] / jnp.sqrt(products[1] * own_power), 0.0)
    score = jnp.take_along_axis(score, (lane + shift) & (LANES - 1), axis=1)
    return jnp.where(lane + half * LANES < valid, score, 0.0)


def score_kernel(place_ref, gene_ref, power_ref, turned_ref, turned2_ref, weighted_ref, low_ref, *refs):
    *dose_refs, cross_ref, product_ref, pass_ref, dose_scr = refs
    samples, variants = dose_refs[0].shape
    chunks = [(ref, at) for ref in dose_refs for at in range(0, ref.shape[1] - variants + 1, variants)]
    order = [0, 1, 3, 2, 4, 5, 7, 6]
    for m, (ref, at) in enumerate(chunks[i] for i in order):
        dose_scr[m * samples : (m + 1) * samples, :] = ref[:, at : at + variants]
    line = turned_ref.shape[1]
    rotated = jnp.dot(turned_ref[...], dose_scr[:line], preferred_element_type=f32)
    rotated += jnp.dot(turned2_ref[...], dose_scr[line:], preferred_element_type=f32)
    rotated = rotated.astype(bf16)
    squared = jnp.square(rotated.astype(f32)).astype(bf16)
    cross = jnp.dot(weighted_ref[...], rotated, preferred_element_type=f32)
    power = jnp.dot(low_ref[...], squared, preferred_element_type=f32)
    cross_ref[...] = cross
    product_ref[...] = power
    pass_ref[...] = window(place_ref, gene_ref, power_ref, cross, power, 1 - place_ref[1], dose_scr.shape[0])


def keep_kernel(place_ref, gene_ref, power_ref, cross_ref, product_ref, keep_ref, *, samples):
    keep_ref[...] = window(
        place_ref, gene_ref, power_ref, cross_ref[...], product_ref[...], place_ref[1], samples
    )


def call(kernel, outs, count, scratch=(), smem=1, anywhere=0, limit=VMEM_LIMIT):
    vmem = pl.BlockSpec(memory_space=pltpu.VMEM)
    return pl.pallas_call(
        kernel,
        out_shape=[jax.ShapeDtypeStruct(*o) for o in outs],
        in_specs=[pl.BlockSpec(memory_space=pltpu.SMEM)] * smem + [vmem] * (count - smem - anywhere) + [pl.BlockSpec(memory_space=pl.ANY)] * anywhere,
        out_specs=[vmem] * len(outs),
        scratch_shapes=list(scratch),
        compiler_params=pltpu.CompilerParams(vmem_limit_bytes=limit),
    )


def near_body(eigvecs, eigvals, expression, dosage, delta, window_start, window_valid, gene_owner):
    rows = lax.axis_size("row")
    row = lax.axis_index("row")
    core = lax.axis_index("col")
    panel, half = eigvecs.shape
    part = panel // 2
    samples = panel * rows
    variants = dosage.shape[1] // 2
    place = jnp.stack([row, core]).astype(jnp.int32)

    def swap(x, m):
        return lax.ppermute(x, "row", [(i, i ^ m) for i in range(rows)])

    def other_core(x):
        return lax.ppermute(x, "col", [(0, 1), (1, 0)])

    ahead, e46, e2, e0, d0, bucket = call(
        route_kernel,
        [
            ((panel, half + 2 * LANES), bf16),
            ((part, 2 * LANES), bf16),
            ((part, LANES), bf16),
            ((part, LANES), bf16),
            ((panel, variants), bf16),
            ((rows, LANES), jnp.int32),
        ],
        5,
        scratch=[
            pltpu.VMEM((rows, LANES), jnp.int32),
            pltpu.VMEM((part, expression.shape[1]), bf16),
            pltpu.SemaphoreType.DMA((4,)),
        ],
        anywhere=4,
    )(
        place,
        *[
            pltpu.with_memory_space_constraint(x, pltpu.HBM)
            for x in (gene_owner.reshape(rows, LANES), expression, eigvecs, dosage)
        ],
    )
    gene, terms = call(gene_kernel, [((LANES, LANES), f32), ((16, half), bf16)], 5, smem=0)(
        bucket,
        delta.reshape(rows, LANES),
        window_start.reshape(rows, LANES),
        window_valid.reshape(rows, LANES),
        eigvals[None, :],
    )
    r1 = swap(ahead, 1)
    d4 = swap(d0, 4)
    d2 = swap(jnp.concatenate([d0, ahead[:, :half]], axis=1), 2)
    to4 = call(second_kernel, [((panel, 2 * half + 2 * LANES), bf16)], 3, smem=0)(ahead, r1, e46)[0]
    r4 = swap(to4, 4)
    pair, far = call(
        copy_kernel, [((panel, 2 * variants), bf16), ((panel, variants), bf16)], 3, smem=0, anywhere=1
    )(d0, d4, to4)
    d6 = swap(far, 2)
    d15 = swap(pair, 1)
    d37 = swap(jnp.concatenate([d2[:, :variants], d6], axis=1), 1)
    width = 4 * half + 2 * LANES
    out, kept = call(
        third_kernel,
        [((panel, width - half), bf16), ((panel, width + 2 * half), bf16)],
        8,
        smem=0,
        anywhere=1,
    )(ahead, r1, r4, e2, e0, terms, d2, far)
    kept2 = other_core(kept)
    near = swap(out, 2)
    near2 = other_core(near)
    shape = ((2 * half, samples // 2), bf16)
    turned, share = call(
        half_kernel,
        [shape, ((LANES, 2 * half), f32)],
        4,
        scratch=[pltpu.VMEM((samples // 2, LANES), bf16)],
        anywhere=1,
    )(place, kept, kept2, d15)
    turned2, weighted, low, power = call(
        weight_kernel,
        [shape, ((LANES, 2 * half), bf16), ((LANES, 2 * half), bf16), ((LANES, LANES), f32)],
        7,
        scratch=[pltpu.VMEM((samples // 2, LANES), bf16)],
    )(place, kept, kept2, near, near2, share, gene)
    cross, product, passed = call(
        score_kernel,
        [((LANES, variants), f32)] * 2 + [((LANES, LANES), f32)],
        13,
        scratch=[pltpu.VMEM((samples, variants), bf16)],
    )(place, gene, power, turned, turned2, weighted, low, d0, d15, d4, d2, d37, d6)
    keep = call(functools.partial(keep_kernel, samples=samples), [((LANES, LANES), f32)], 5)(
        place, gene, power, cross, product
    )[0]
    return keep + other_core(passed)


def body(eigvecs, eigvals, expression, dosage, delta, window_start, window_valid, gene_owner):
    rows = lax.axis_size("row")
    samples = eigvecs.shape[0] * rows
    own = expression.shape[1] // rows
    fits = (
        lax.axis_size("col") == 2
        and own == LANES
        and W == 2 * LANES
        and rows == 8
        and dosage.shape[1] % (2 * LANES) == 0
        and samples * (samples + dosage.shape[1]) <= VMEM_LIMIT // 16
    )
    run = near_body if fits else wide_body
    return run(eigvecs, eigvals, expression, dosage, delta, window_start, window_valid, gene_owner)


def solution(mesh):
    placed = (
        P(("groups", "row"), "col"),
        P(("groups", "col")),
        P(("groups", "row"), None),
        P(("groups", "row"), None),
        P("groups"),
        P("groups"),
        P("groups"),
        P("groups"),
    )
    return jax.shard_map(
        body, mesh=mesh, in_specs=placed, out_specs=P(("groups", "row"), "col"), check_vma=False
    )
```

```python
import functools

import jax
import jax.numpy as jnp
from jax import lax
from jax.experimental import pallas as pl
from jax.experimental.pallas import tpu as pltpu
from jax.sharding import PartitionSpec as P

W = 256
LANES = 128
VMEM_LIMIT = 32 * 1024 * 1024
NT = (((1,), (1,)), ((), ()))
f32 = jnp.float32
bf16 = jnp.bfloat16


def owner_listing(gene_owner):
    total = gene_owner.shape[0]
    return jnp.argsort(gene_owner * total + jnp.arange(total, dtype=jnp.int32))


def earlier_equal(labels):
    places = jnp.arange(labels.shape[0], dtype=jnp.int32)
    same = labels[:, None] == labels[None, :]
    before = places[:, None] > places[None, :]
    return jnp.sum((same & before).astype(jnp.int32), axis=1)


def shift_windows(tables, starts, largest):
    moved_tables = tables
    step_size = 1
    while step_size <= largest:
        bit_set = starts // step_size % 2 == 1
        filler = jnp.zeros(moved_tables.shape[:-1] + (step_size,), moved_tables.dtype)
        moved = jnp.concatenate([moved_tables[..., step_size:], filler], axis=-1)
        moved_tables = jnp.where(bit_set[None, :, None], moved, moved_tables)
        step_size = step_size * 2
    return moved_tables


def wide_body(eigvecs, eigvals, expression, dosage, delta, window_start, window_valid, gene_owner):
    row_count = lax.axis_size("row")
    row_index = lax.axis_index("row")
    genes_all = expression.shape[1]
    own_count = genes_all // row_count
    half_samples = eigvecs.shape[1]
    samples = half_samples * lax.axis_size("col")
    owner_order = owner_listing(gene_owner)
    my_genes = lax.dynamic_slice_in_dim(owner_order, row_index * own_count, own_count)
    expr_panel, dose_panel = (
        lax.all_to_all(expression, "row", split_axis=1, concat_axis=0, tiled=True),
        lax.all_to_all(dosage, "row", split_axis=1, concat_axis=0, tiled=True),
    )
    panel_data = jnp.concatenate([expr_panel, dose_panel], axis=1)
    rotated = lax.dot_general(
        panel_data,
        lax.all_gather(eigvecs, "row", axis=0, tiled=True),
        (((0,), (0,)), ((), ())),
        preferred_element_type=jnp.float32,
    ).astype(jnp.bfloat16)
    rot_expr = rotated[:own_count]
    rot_dose = rotated[own_count:]
    dose_all = lax.all_gather(rot_dose, "row", axis=0, tiled=True)
    capacity = max(2, own_count // row_count)
    destination = lax.dynamic_slice_in_dim(gene_owner, row_index * own_count, own_count)
    position = destination * capacity + earlier_equal(destination)
    slot_ids = jnp.arange(row_count * capacity, dtype=jnp.int32)
    placement_map = (slot_ids[:, None] == position[None, :]).astype(jnp.bfloat16)
    buckets = jnp.dot(placement_map, rot_expr, preferred_element_type=jnp.float32).astype(
        jnp.bfloat16
    )
    received = lax.all_to_all(buckets, "row", split_axis=0, concat_axis=0, tiled=True)
    source = my_genes // own_count
    owned_expr = jnp.take(received, source * capacity + earlier_equal(source), axis=0)
    own_delta = jnp.take(delta, my_genes)
    own_start = jnp.take(window_start, my_genes)
    own_valid = jnp.take(window_valid, my_genes)
    weight = 1.0 / (eigvals[None, :] + own_delta[:, None])
    expr_float = owned_expr.astype(jnp.float32)
    expr_power = jnp.sum(weight * expr_float * expr_float, axis=1)
    weighted = (weight * expr_float).astype(jnp.bfloat16)
    weight_low = weight.astype(jnp.bfloat16)
    dose_sq = jnp.square(dose_all.astype(jnp.float32)).astype(jnp.bfloat16)
    slot_index = jnp.arange(W, dtype=jnp.int32)
    contract = (((1,), (1,)), ((), ()))
    cross_all = lax.dot_general(weighted, dose_all, contract, preferred_element_type=jnp.float32)
    power_all = lax.dot_general(weight_low, dose_sq, contract, preferred_element_type=jnp.float32)
    stacked = jnp.stack([cross_all, power_all], axis=0)
    variants = dose_all.shape[0]
    shifted = shift_windows(stacked, own_start, variants - W)
    cross_sum = shifted[0, :, :W]
    dose_power = shifted[1, :, :W]
    cross_sum, dose_power, expr_power = lax.psum((cross_sum, dose_power, expr_power), "col")
    scale = jnp.sqrt(jnp.float32(samples))
    zscore = jnp.where(
        slot_index[None, :] < own_valid[:, None],
        scale * cross_sum / jnp.sqrt(dose_power * expr_power[:, None]),
        0.0,
    )
    width_part = W // lax.axis_size("col")
    return lax.dynamic_slice_in_dim(zscore, lax.axis_index("col") * width_part, width_part, 1)


def route_kernel(
    place_ref, owner_any, delta_any, start_any, valid_any, vals_any, vecs_any, expr_any, dose_any,
    ahead_ref, e46_ref, e2_ref, e0_ref, gene_ref, terms_ref, half_ref,
    owner_ref, delta_ref, start_ref, valid_ref, vals_ref, expr_ref, sems,
):
    row, core = place_ref[0], place_ref[1]
    half = vecs_any.shape[1]
    part = expr_ref.shape[0]
    variants = half_ref.shape[1]
    pairs = (
        (owner_any, owner_ref),
        (expr_any.at[pl.ds(pl.multiple_of(core * part, part), part)], expr_ref),
        (delta_any, delta_ref),
        (start_any, start_ref),
        (valid_any, valid_ref),
        (vals_any, vals_ref),
        (vecs_any, ahead_ref.at[:, pl.ds(0, half)]),
        (dose_any.at[:, pl.ds(pl.multiple_of(core * variants, LANES), variants)], half_ref),
    )
    copies = [pltpu.make_async_copy(a, b, sems.at[i]) for i, (a, b) in enumerate(pairs)]
    for copy in copies:
        copy.start()
    slices = owner_ref.shape[0]
    capacity = LANES // slices
    before = lax.broadcasted_iota(jnp.int32, (LANES, LANES), 0) < lax.broadcasted_iota(
        jnp.int32, (LANES, LANES), 1
    )
    before = before.astype(bf16)
    slot = lax.broadcasted_iota(jnp.int32, (LANES, LANES), 0)
    own_slot = lax.broadcasted_iota(jnp.int32, (capacity, LANES), 0)
    lane = lax.broadcasted_iota(jnp.int32, (capacity, LANES), 1)
    copies[0].wait()
    owner = owner_ref[...]
    rank = jnp.zeros(owner.shape, f32)
    for o in range(slices):
        same = (owner == o).astype(f32)
        rank += same * jnp.dot(same.astype(bf16), before, preferred_element_type=f32)
    bucket = (owner ^ row) * capacity + rank.astype(jnp.int32)
    for copy in copies[1:]:
        copy.wait()
    sorted_slices = []
    for s in range(slices):
        here = bucket[s : s + 1, :]
        pick = (slot == here).astype(bf16)
        sorted_slices.append(
            lax.dot_general(pick, expr_ref[:, s * LANES : (s + 1) * LANES], NT, preferred_element_type=f32)
        )
        mine = (own_slot == here).astype(f32)
        figures = jnp.zeros((capacity, LANES), f32)
        for i, ref in enumerate((delta_ref, start_ref, valid_ref)):
            line = ref[s : s + 1, :].astype(f32)
            figures = jnp.where(lane == i, jnp.sum(mine * line, axis=1, keepdims=True), figures)
        gene_ref[s * capacity : (s + 1) * capacity, :] = figures
    vals = vals_ref[...]
    high = vals.astype(bf16).astype(f32)
    middle = (vals - high).astype(bf16).astype(f32)
    term = lax.broadcasted_iota(jnp.int32, terms_ref.shape, 0)
    terms = jnp.where(term == 0, high, jnp.where(term == 1, middle, jnp.where(term == 2, vals - high - middle, 0.0)))
    terms_ref[...] = terms.astype(bf16)
    left, right = slice(0, LANES), slice(LANES, 2 * LANES)
    upper, lower = slice(0, part), slice(part, 2 * part)
    targets = {
        0: (e0_ref, upper, left),
        1: (ahead_ref, upper, slice(half, half + LANES)),
        2: (e2_ref, upper, left),
        3: (ahead_ref, upper, slice(half + LANES, half + 2 * LANES)),
        4: (e46_ref, upper, left),
        5: (ahead_ref, lower, slice(half, half + LANES)),
        6: (e46_ref, upper, right),
        7: (ahead_ref, lower, slice(half + LANES, half + 2 * LANES)),
    }
    for m, (ref, down, side) in targets.items():
        block = jnp.concatenate([x[m * capacity : (m + 1) * capacity, :] for x in sorted_slices], axis=0)
        ref[down, side] = block.T.astype(bf16)


def second_kernel(ahead_ref, r1_ref, e46_ref, out_ref):
    half = out_ref.shape[1] // 2 - LANES
    part = e46_ref.shape[0]
    out_ref[:, :half] = ahead_ref[:, :half]
    out_ref[:, half : 2 * half] = r1_ref[:, :half]
    out_ref[:part, 2 * half :] = e46_ref[...]
    out_ref[part:, 2 * half :] = r1_ref[part:, half:]


def copy_kernel(d0_ref, d4_ref, after_any, pair_ref, far_ref):
    variants = d0_ref.shape[1]
    pair_ref[:, :variants] = d0_ref[...]
    pair_ref[:, variants:] = d4_ref[...]
    far_ref[...] = d4_ref[...]


def third_kernel(ahead_ref, r1_ref, r4_ref, e2_ref, e0_ref, terms_ref, d2_ref, far_any, out_ref, kept_ref):
    half = terms_ref.shape[1]
    part = e0_ref.shape[0]
    kept_ref[:, :half] = ahead_ref[:, :half]
    for ref, own, at, first in ((out_ref, e2_ref, LANES, 0), (kept_ref, e0_ref, 0, half)):
        ref[:, first : first + half] = r1_ref[:, :half]
        ref[:, first + half : first + 3 * half] = r4_ref[:, : 2 * half]
        side = slice(2 * half + at, 2 * half + at + LANES)
        middle = first + 3 * half + LANES
        left, right = slice(middle - LANES, middle), slice(middle, middle + LANES)
        ref[:part, left] = own[...]
        ref[:part, right] = r1_ref[:part, half + at : half + at + LANES]
        ref[part:, left] = r4_ref[:part, side]
        ref[part:, right] = r4_ref[part:, side]
    width = out_ref.shape[1] + half
    terms = terms_ref.shape[0]
    kept_ref[:terms, width : width + half] = terms_ref[...]
    kept_ref[terms:, width : width + half] = jnp.zeros((kept_ref.shape[0] - terms, half), bf16)
    kept_ref[:, width + half :] = d2_ref[:, d2_ref.shape[1] - half :]


def rotate(place_ref, refs, turned_ref, data_scr, panels, data_at):
    samples = refs[0].shape[0]
    half = turned_ref.shape[0] // 2
    part = samples // 2
    core = place_ref[1]
    for c, ref in enumerate(refs):
        side = core if c == 0 else 1 - core
        for i in range(4):
            panel, at = panels[c][i]
            turned_ref[c * half : (c + 1) * half, i * samples : (i + 1) * samples] = (
                panel[:, at : at + half].astype(f32).T.astype(bf16)
            )
            at = data_at + i % 2 * LANES
            data_scr[pl.ds(pl.multiple_of(i * samples + side * part, part), part), :] = ref[
                i // 2 * part : (i // 2 + 1) * part, at : at + LANES
            ]
    data = data_scr[...].astype(f32).T.astype(bf16)
    shares = []
    for c in range(2):
        vecs = jnp.concatenate([panel[:, at : at + half] for panel, at in panels[c]], axis=0)
        shares.append(jnp.dot(data, vecs, preferred_element_type=f32))
    return shares


def half_kernel(place_ref, mine_ref, other_ref, d15_any, turned_ref, share_ref, data_scr):
    half = turned_ref.shape[0] // 2
    refs = (mine_ref, other_ref)
    panels = [[(ref, i * half) for i in range(4)] for ref in refs]
    for c, share in enumerate(rotate(place_ref, refs, turned_ref, data_scr, panels, 4 * half)):
        share_ref[:, c * half : (c + 1) * half] = share


def weight_kernel(
    place_ref, kept_ref, kept2_ref, mine_ref, other_ref, share_ref, gene_ref,
    turned_ref, weighted_ref, low_ref, power_ref, data_scr,
):
    half = turned_ref.shape[0] // 2
    delta = gene_ref[:, 0:1]
    total = jnp.zeros((delta.shape[0], 1), f32)
    width = mine_ref.shape[1] + half
    panels = [
        [(kept, width + half)] + [(ref, i * half) for i in range(3)]
        for kept, ref in ((kept_ref, mine_ref), (kept2_ref, other_ref))
    ]
    shares = rotate(place_ref, (mine_ref, other_ref), turned_ref, data_scr, panels, 3 * half)
    for c, (share, ref) in enumerate(zip(shares, (kept_ref, kept2_ref))):
        cols = slice(c * half, (c + 1) * half)
        terms = ref[0:16, width : width + half].astype(f32)
        vals = terms[0:1] + terms[1:2] + terms[2:3]
        rotated = (share_ref[:, cols] + share).astype(bf16).astype(f32)
        weight = 1.0 / (vals + delta)
        total += jnp.sum(weight * rotated * rotated, axis=1, keepdims=True)
        weighted_ref[:, cols] = (weight * rotated).astype(bf16)
        low_ref[:, cols] = weight.astype(bf16)
    power_ref[...] = jnp.broadcast_to(total, power_ref.shape)


def window(place_ref, gene_ref, power_ref, cross, power, half, samples):
    core = place_ref[1]
    start = gene_ref[:, 1:2].astype(jnp.int32)
    valid = gene_ref[:, 2:3].astype(jnp.int32)
    genes = cross.shape[0]
    lane = lax.broadcasted_iota(jnp.int32, (genes, LANES), 1)
    own_power = power_ref[...]
    scale = jnp.sqrt(f32(samples))
    variants = cross.shape[1]
    blocks = variants // LANES
    offset = start + half * LANES - core * variants
    block = offset >> 7
    shift = offset & (LANES - 1)
    need = block + (lane < shift).astype(jnp.int32)
    products = [jnp.zeros((genes, LANES), f32)] * 2
    for b in range(blocks):
        here = need == b
        parts = [array[:, b * LANES : (b + 1) * LANES] for array in (cross, power)]
        products = [jnp.where(here, part, product) for part, product in zip(parts, products)]
    inside = (need >= 0) & (need < blocks)
    score = jnp.where(inside, scale * products[0] / jnp.sqrt(products[1] * own_power), 0.0)
    score = jnp.take_along_axis(score, (lane + shift) & (LANES - 1), axis=1)
    return jnp.where(lane + half * LANES < valid, score, 0.0)


def score_kernel(place_ref, gene_ref, power_ref, turned_ref, turned2_ref, weighted_ref, low_ref, *refs):
    *dose_refs, cross_ref, product_ref, pass_ref, dose_scr = refs
    samples, variants = dose_refs[0].shape
    chunks = [(ref, at) for ref in dose_refs for at in range(0, ref.shape[1] - variants + 1, variants)]
    order = [0, 1, 3, 2, 4, 5, 7, 6]
    for m, (ref, at) in enumerate(chunks[i] for i in order):
        dose_scr[m * samples : (m + 1) * samples, :] = ref[:, at : at + variants]
    line = turned_ref.shape[1]
    rotated = jnp.dot(turned_ref[...], dose_scr[:line], preferred_element_type=f32)
    rotated += jnp.dot(turned2_ref[...], dose_scr[line:], preferred_element_type=f32)
    rotated = rotated.astype(bf16)
    squared = jnp.square(rotated.astype(f32)).astype(bf16)
    cross = jnp.dot(weighted_ref[...], rotated, preferred_element_type=f32)
    power = jnp.dot(low_ref[...], squared, preferred_element_type=f32)
    cross_ref[...] = cross
    product_ref[...] = power
    pass_ref[...] = window(place_ref, gene_ref, power_ref, cross, power, 1 - place_ref[1], dose_scr.shape[0])


def keep_kernel(place_ref, gene_ref, power_ref, cross_ref, product_ref, keep_ref, *, samples):
    keep_ref[...] = window(
        place_ref, gene_ref, power_ref, cross_ref[...], product_ref[...], place_ref[1], samples
    )


def call(kernel, outs, count, scratch=(), smem=1, anywhere=0, limit=VMEM_LIMIT):
    vmem = pl.BlockSpec(memory_space=pltpu.VMEM)
    return pl.pallas_call(
        kernel,
        out_shape=[jax.ShapeDtypeStruct(*o) for o in outs],
        in_specs=[pl.BlockSpec(memory_space=pltpu.SMEM)] * smem + [vmem] * (count - smem - anywhere) + [pl.BlockSpec(memory_space=pl.ANY)] * anywhere,
        out_specs=[vmem] * len(outs),
        scratch_shapes=list(scratch),
        compiler_params=pltpu.CompilerParams(vmem_limit_bytes=limit),
    )


def near_body(eigvecs, eigvals, expression, dosage, delta, window_start, window_valid, gene_owner):
    rows = lax.axis_size("row")
    row = lax.axis_index("row")
    core = lax.axis_index("col")
    panel, half = eigvecs.shape
    part = panel // 2
    samples = panel * rows
    variants = dosage.shape[1] // 2
    place = jnp.stack([row, core]).astype(jnp.int32)

    def swap(x, m):
        return lax.ppermute(x, "row", [(i, i ^ m) for i in range(rows)])

    def other_core(x):
        return lax.ppermute(x, "col", [(0, 1), (1, 0)])

    ahead, e46, e2, e0, gene, terms, d0 = call(
        route_kernel,
        [
            ((panel, half + 2 * LANES), bf16),
            ((part, 2 * LANES), bf16),
            ((part, LANES), bf16),
            ((part, LANES), bf16),
            ((LANES, LANES), f32),
            ((16, half), bf16),
            ((panel, variants), bf16),
        ],
        9,
        scratch=[pltpu.VMEM((rows, LANES), kind) for kind in (jnp.int32, f32, jnp.int32, jnp.int32)]
        + [pltpu.VMEM((1, half), f32), pltpu.VMEM((part, expression.shape[1]), bf16), pltpu.SemaphoreType.DMA((8,))],
        anywhere=8,
        limit=VMEM_LIMIT,
    )(
        place,
        *[
            pltpu.with_memory_space_constraint(x, pltpu.HBM)
            for x in (
                gene_owner.reshape(rows, LANES),
                delta.reshape(rows, LANES),
                window_start.reshape(rows, LANES),
                window_valid.reshape(rows, LANES),
                eigvals[None, :],
                eigvecs,
                expression,
                dosage,
            )
        ],
    )
    r1 = swap(ahead, 1)
    d4 = swap(d0, 4)
    d2 = swap(jnp.concatenate([d0, ahead[:, :half]], axis=1), 2)
    to4 = call(second_kernel, [((panel, 2 * half + 2 * LANES), bf16)], 3, smem=0)(ahead, r1, e46)[0]
    r4 = swap(to4, 4)
    pair, far = call(
        copy_kernel, [((panel, 2 * variants), bf16), ((panel, variants), bf16)], 3, smem=0, anywhere=1
    )(d0, d4, to4)
    d6 = swap(far, 2)
    d15 = swap(pair, 1)
    d37 = swap(jnp.concatenate([d2[:, :variants], d6], axis=1), 1)
    width = 4 * half + 2 * LANES
    out, kept = call(
        third_kernel,
        [((panel, width - half), bf16), ((panel, width + 2 * half), bf16)],
        8,
        smem=0,
        anywhere=1,
    )(ahead, r1, r4, e2, e0, terms, d2, far)
    kept2 = other_core(kept)
    near = swap(out, 2)
    near2 = other_core(near)
    shape = ((2 * half, samples // 2), bf16)
    turned, share = call(
        half_kernel,
        [shape, ((LANES, 2 * half), f32)],
        4,
        scratch=[pltpu.VMEM((samples // 2, LANES), bf16)],
        anywhere=1,
    )(place, kept, kept2, d15)
    turned2, weighted, low, power = call(
        weight_kernel,
        [shape, ((LANES, 2 * half), bf16), ((LANES, 2 * half), bf16), ((LANES, LANES), f32)],
        7,
        scratch=[pltpu.VMEM((samples // 2, LANES), bf16)],
    )(place, kept, kept2, near, near2, share, gene)
    cross, product, passed = call(
        score_kernel,
        [((LANES, variants), f32)] * 2 + [((LANES, LANES), f32)],
        13,
        scratch=[pltpu.VMEM((samples, variants), bf16)],
    )(place, gene, power, turned, turned2, weighted, low, d0, d15, d4, d2, d37, d6)
    keep = call(functools.partial(keep_kernel, samples=samples), [((LANES, LANES), f32)], 5)(
        place, gene, power, cross, product
    )[0]
    return keep + other_core(passed)


def body(eigvecs, eigvals, expression, dosage, delta, window_start, window_valid, gene_owner):
    rows = lax.axis_size("row")
    samples = eigvecs.shape[0] * rows
    own = expression.shape[1] // rows
    fits = (
        lax.axis_size("col") == 2
        and own == LANES
        and W == 2 * LANES
        and rows == 8
        and dosage.shape[1] % (2 * LANES) == 0
        and samples * (samples + dosage.shape[1]) <= VMEM_LIMIT // 16
    )
    run = near_body if fits else wide_body
    return run(eigvecs, eigvals, expression, dosage, delta, window_start, window_valid, gene_owner)


def solution(mesh):
    placed = (
        P(("groups", "row"), "col"),
        P(("groups", "col")),
        P(("groups", "row"), None),
        P(("groups", "row"), None),
        P("groups"),
        P("groups"),
        P("groups"),
        P("groups"),
    )
    return jax.shard_map(
        body, mesh=mesh, in_specs=placed, out_specs=P(("groups", "row"), "col"), check_vma=False
    )
```

```python
import functools

import jax
import jax.numpy as jnp
from jax import lax
from jax.experimental import pallas as pl
from jax.experimental.pallas import tpu as pltpu
from jax.sharding import PartitionSpec as P

W = 256
LANES = 128
VMEM_LIMIT = 32 * 1024 * 1024
NT = (((1,), (1,)), ((), ()))
f32 = jnp.float32
bf16 = jnp.bfloat16


def owner_listing(gene_owner):
    total = gene_owner.shape[0]
    return jnp.argsort(gene_owner * total + jnp.arange(total, dtype=jnp.int32))


def earlier_equal(labels):
    places = jnp.arange(labels.shape[0], dtype=jnp.int32)
    same = labels[:, None] == labels[None, :]
    before = places[:, None] > places[None, :]
    return jnp.sum((same & before).astype(jnp.int32), axis=1)


def shift_windows(tables, starts, largest):
    moved_tables = tables
    step_size = 1
    while step_size <= largest:
        bit_set = starts // step_size % 2 == 1
        filler = jnp.zeros(moved_tables.shape[:-1] + (step_size,), moved_tables.dtype)
        moved = jnp.concatenate([moved_tables[..., step_size:], filler], axis=-1)
        moved_tables = jnp.where(bit_set[None, :, None], moved, moved_tables)
        step_size = step_size * 2
    return moved_tables


def wide_body(eigvecs, eigvals, expression, dosage, delta, window_start, window_valid, gene_owner):
    row_count = lax.axis_size("row")
    row_index = lax.axis_index("row")
    genes_all = expression.shape[1]
    own_count = genes_all // row_count
    half_samples = eigvecs.shape[1]
    samples = half_samples * lax.axis_size("col")
    owner_order = owner_listing(gene_owner)
    my_genes = lax.dynamic_slice_in_dim(owner_order, row_index * own_count, own_count)
    expr_panel, dose_panel = (
        lax.all_to_all(expression, "row", split_axis=1, concat_axis=0, tiled=True),
        lax.all_to_all(dosage, "row", split_axis=1, concat_axis=0, tiled=True),
    )
    panel_data = jnp.concatenate([expr_panel, dose_panel], axis=1)
    rotated = lax.dot_general(
        panel_data,
        lax.all_gather(eigvecs, "row", axis=0, tiled=True),
        (((0,), (0,)), ((), ())),
        preferred_element_type=jnp.float32,
    ).astype(jnp.bfloat16)
    rot_expr = rotated[:own_count]
    rot_dose = rotated[own_count:]
    dose_all = lax.all_gather(rot_dose, "row", axis=0, tiled=True)
    capacity = max(2, own_count // row_count)
    destination = lax.dynamic_slice_in_dim(gene_owner, row_index * own_count, own_count)
    position = destination * capacity + earlier_equal(destination)
    slot_ids = jnp.arange(row_count * capacity, dtype=jnp.int32)
    placement_map = (slot_ids[:, None] == position[None, :]).astype(jnp.bfloat16)
    buckets = jnp.dot(placement_map, rot_expr, preferred_element_type=jnp.float32).astype(
        jnp.bfloat16
    )
    received = lax.all_to_all(buckets, "row", split_axis=0, concat_axis=0, tiled=True)
    source = my_genes // own_count
    owned_expr = jnp.take(received, source * capacity + earlier_equal(source), axis=0)
    own_delta = jnp.take(delta, my_genes)
    own_start = jnp.take(window_start, my_genes)
    own_valid = jnp.take(window_valid, my_genes)
    weight = 1.0 / (eigvals[None, :] + own_delta[:, None])
    expr_float = owned_expr.astype(jnp.float32)
    expr_power = jnp.sum(weight * expr_float * expr_float, axis=1)
    weighted = (weight * expr_float).astype(jnp.bfloat16)
    weight_low = weight.astype(jnp.bfloat16)
    dose_sq = jnp.square(dose_all.astype(jnp.float32)).astype(jnp.bfloat16)
    slot_index = jnp.arange(W, dtype=jnp.int32)
    contract = (((1,), (1,)), ((), ()))
    cross_all = lax.dot_general(weighted, dose_all, contract, preferred_element_type=jnp.float32)
    power_all = lax.dot_general(weight_low, dose_sq, contract, preferred_element_type=jnp.float32)
    stacked = jnp.stack([cross_all, power_all], axis=0)
    variants = dose_all.shape[0]
    shifted = shift_windows(stacked, own_start, variants - W)
    cross_sum = shifted[0, :, :W]
    dose_power = shifted[1, :, :W]
    cross_sum, dose_power, expr_power = lax.psum((cross_sum, dose_power, expr_power), "col")
    scale = jnp.sqrt(jnp.float32(samples))
    zscore = jnp.where(
        slot_index[None, :] < own_valid[:, None],
        scale * cross_sum / jnp.sqrt(dose_power * expr_power[:, None]),
        0.0,
    )
    width_part = W // lax.axis_size("col")
    return lax.dynamic_slice_in_dim(zscore, lax.axis_index("col") * width_part, width_part, 1)


def route_kernel(
    place_ref, owner_any, delta_any, start_any, valid_any, vals_any, vecs_any, expr_any, dose_any,
    ahead_ref, e46_ref, e2_ref, e0_ref, gene_ref, terms_ref, half_ref,
    owner_ref, delta_ref, start_ref, valid_ref, vals_ref, expr_ref, sems,
):
    row, core = place_ref[0], place_ref[1]
    half = vecs_any.shape[1]
    part = expr_ref.shape[0]
    variants = half_ref.shape[1]
    pairs = (
        (owner_any, owner_ref),
        (expr_any.at[pl.ds(pl.multiple_of(core * part, part), part)], expr_ref),
        (delta_any, delta_ref),
        (start_any, start_ref),
        (valid_any, valid_ref),
        (vals_any, vals_ref),
        (vecs_any, ahead_ref.at[:, pl.ds(0, half)]),
        (dose_any.at[:, pl.ds(pl.multiple_of(core * variants, LANES), variants)], half_ref),
    )
    copies = [pltpu.make_async_copy(a, b, sems.at[i]) for i, (a, b) in enumerate(pairs)]
    for copy in copies:
        copy.start()
    slices = owner_ref.shape[0]
    capacity = LANES // slices
    before = lax.broadcasted_iota(jnp.int32, (LANES, LANES), 0) < lax.broadcasted_iota(
        jnp.int32, (LANES, LANES), 1
    )
    before = before.astype(bf16)
    slot = lax.broadcasted_iota(jnp.int32, (LANES, LANES), 0)
    own_slot = lax.broadcasted_iota(jnp.int32, (capacity, LANES), 0)
    lane = lax.broadcasted_iota(jnp.int32, (capacity, LANES), 1)
    copies[0].wait()
    owner = owner_ref[...]
    rank = jnp.zeros(owner.shape, f32)
    for o in range(slices):
        same = (owner == o).astype(f32)
        rank += same * jnp.dot(same.astype(bf16), before, preferred_element_type=f32)
    bucket = (owner ^ row) * capacity + rank.astype(jnp.int32)
    for copy in copies[1:]:
        copy.wait()
    sorted_slices = []
    for s in range(slices):
        here = bucket[s : s + 1, :]
        pick = (slot == here).astype(bf16)
        sorted_slices.append(
            lax.dot_general(pick, expr_ref[:, s * LANES : (s + 1) * LANES], NT, preferred_element_type=f32)
        )
        mine = (own_slot == here).astype(f32)
        figures = jnp.zeros((capacity, LANES), f32)
        for i, ref in enumerate((delta_ref, start_ref, valid_ref)):
            line = ref[s : s + 1, :].astype(f32)
            figures = jnp.where(lane == i, jnp.sum(mine * line, axis=1, keepdims=True), figures)
        gene_ref[s * capacity : (s + 1) * capacity, :] = figures
    vals = vals_ref[...]
    high = vals.astype(bf16).astype(f32)
    middle = (vals - high).astype(bf16).astype(f32)
    term = lax.broadcasted_iota(jnp.int32, terms_ref.shape, 0)
    terms = jnp.where(term == 0, high, jnp.where(term == 1, middle, jnp.where(term == 2, vals - high - middle, 0.0)))
    terms_ref[...] = terms.astype(bf16)
    left, right = slice(0, LANES), slice(LANES, 2 * LANES)
    upper, lower = slice(0, part), slice(part, 2 * part)
    targets = {
        0: (e0_ref, upper, left),
        1: (ahead_ref, upper, slice(half, half + LANES)),
        2: (e2_ref, upper, left),
        3: (ahead_ref, upper, slice(half + LANES, half + 2 * LANES)),
        4: (e46_ref, upper, left),
        5: (ahead_ref, lower, slice(half, half + LANES)),
        6: (e46_ref, upper, right),
        7: (ahead_ref, lower, slice(half + LANES, half + 2 * LANES)),
    }
    for m, (ref, down, side) in targets.items():
        block = jnp.concatenate([x[m * capacity : (m + 1) * capacity, :] for x in sorted_slices], axis=0)
        ref[down, side] = block.T.astype(bf16)


def second_kernel(ahead_ref, r1_ref, e46_ref, out_ref):
    half = out_ref.shape[1] // 2 - LANES
    part = e46_ref.shape[0]
    out_ref[:, :half] = ahead_ref[:, :half]
    out_ref[:, half : 2 * half] = r1_ref[:, :half]
    out_ref[:part, 2 * half :] = e46_ref[...]
    out_ref[part:, 2 * half :] = r1_ref[part:, half:]


def copy_kernel(dose_ref, after_any, out_ref):
    out_ref[...] = dose_ref[...]


def third_kernel(ahead_ref, r1_ref, r4_ref, e2_ref, e0_ref, terms_ref, d2_ref, far_any, d1_any, out_ref, kept_ref):
    half = terms_ref.shape[1]
    part = e0_ref.shape[0]
    kept_ref[:, :half] = ahead_ref[:, :half]
    for ref, own, at, first in ((out_ref, e2_ref, LANES, 0), (kept_ref, e0_ref, 0, half)):
        ref[:, first : first + half] = r1_ref[:, :half]
        ref[:, first + half : first + 3 * half] = r4_ref[:, : 2 * half]
        side = slice(2 * half + at, 2 * half + at + LANES)
        middle = first + 3 * half + LANES
        left, right = slice(middle - LANES, middle), slice(middle, middle + LANES)
        ref[:part, left] = own[...]
        ref[:part, right] = r1_ref[:part, half + at : half + at + LANES]
        ref[part:, left] = r4_ref[:part, side]
        ref[part:, right] = r4_ref[part:, side]
    width = out_ref.shape[1] + half
    terms = terms_ref.shape[0]
    kept_ref[:terms, width : width + half] = terms_ref[...]
    kept_ref[terms:, width : width + half] = jnp.zeros((kept_ref.shape[0] - terms, half), bf16)
    kept_ref[:, width + half :] = d2_ref[:, d2_ref.shape[1] - half :]


def rotate(place_ref, refs, turned_ref, data_scr, panels, data_at):
    samples = refs[0].shape[0]
    half = turned_ref.shape[0] // 2
    part = samples // 2
    core = place_ref[1]
    for c, ref in enumerate(refs):
        side = core if c == 0 else 1 - core
        for i in range(4):
            panel, at = panels[c][i]
            turned_ref[c * half : (c + 1) * half, i * samples : (i + 1) * samples] = (
                panel[:, at : at + half].astype(f32).T.astype(bf16)
            )
            at = data_at + i % 2 * LANES
            data_scr[pl.ds(pl.multiple_of(i * samples + side * part, part), part), :] = ref[
                i // 2 * part : (i // 2 + 1) * part, at : at + LANES
            ]
    data = data_scr[...].astype(f32).T.astype(bf16)
    shares = []
    for c in range(2):
        vecs = jnp.concatenate([panel[:, at : at + half] for panel, at in panels[c]], axis=0)
        shares.append(jnp.dot(data, vecs, preferred_element_type=f32))
    return shares


def half_kernel(place_ref, mine_ref, other_ref, d5_any, turned_ref, share_ref, data_scr):
    half = turned_ref.shape[0] // 2
    refs = (mine_ref, other_ref)
    panels = [[(ref, i * half) for i in range(4)] for ref in refs]
    for c, share in enumerate(rotate(place_ref, refs, turned_ref, data_scr, panels, 4 * half)):
        share_ref[:, c * half : (c + 1) * half] = share


def weight_kernel(
    place_ref, kept_ref, kept2_ref, mine_ref, other_ref, share_ref, gene_ref,
    turned_ref, weighted_ref, low_ref, power_ref, data_scr,
):
    half = turned_ref.shape[0] // 2
    delta = gene_ref[:, 0:1]
    total = jnp.zeros((delta.shape[0], 1), f32)
    width = mine_ref.shape[1] + half
    panels = [
        [(kept, width + half)] + [(ref, i * half) for i in range(3)]
        for kept, ref in ((kept_ref, mine_ref), (kept2_ref, other_ref))
    ]
    shares = rotate(place_ref, (mine_ref, other_ref), turned_ref, data_scr, panels, 3 * half)
    for c, (share, ref) in enumerate(zip(shares, (kept_ref, kept2_ref))):
        cols = slice(c * half, (c + 1) * half)
        terms = ref[0:16, width : width + half].astype(f32)
        vals = terms[0:1] + terms[1:2] + terms[2:3]
        rotated = (share_ref[:, cols] + share).astype(bf16).astype(f32)
        weight = 1.0 / (vals + delta)
        total += jnp.sum(weight * rotated * rotated, axis=1, keepdims=True)
        weighted_ref[:, cols] = (weight * rotated).astype(bf16)
        low_ref[:, cols] = weight.astype(bf16)
    power_ref[...] = jnp.broadcast_to(total, power_ref.shape)


def window(place_ref, gene_ref, power_ref, cross, power, half, samples):
    core = place_ref[1]
    start = gene_ref[:, 1:2].astype(jnp.int32)
    valid = gene_ref[:, 2:3].astype(jnp.int32)
    genes = cross.shape[0]
    lane = lax.broadcasted_iota(jnp.int32, (genes, LANES), 1)
    own_power = power_ref[...]
    scale = jnp.sqrt(f32(samples))
    variants = cross.shape[1]
    blocks = variants // LANES
    offset = start + half * LANES - core * variants
    block = offset >> 7
    shift = offset & (LANES - 1)
    need = block + (lane < shift).astype(jnp.int32)
    products = [jnp.zeros((genes, LANES), f32)] * 2
    for b in range(blocks):
        here = need == b
        parts = [array[:, b * LANES : (b + 1) * LANES] for array in (cross, power)]
        products = [jnp.where(here, part, product) for part, product in zip(parts, products)]
    inside = (need >= 0) & (need < blocks)
    score = jnp.where(inside, scale * products[0] / jnp.sqrt(products[1] * own_power), 0.0)
    score = jnp.take_along_axis(score, (lane + shift) & (LANES - 1), axis=1)
    return jnp.where(lane + half * LANES < valid, score, 0.0)


def score_kernel(place_ref, gene_ref, power_ref, turned_ref, turned2_ref, weighted_ref, low_ref, *refs):
    *dose_refs, cross_ref, product_ref, pass_ref, dose_scr = refs
    samples, variants = dose_refs[0].shape
    chunks = [(ref, at) for ref in dose_refs for at in range(0, ref.shape[1] - variants + 1, variants)]
    order = [0, 1, 2, 3, 4, 5, 7, 6]
    for m, (ref, at) in enumerate(chunks[i] for i in order):
        dose_scr[m * samples : (m + 1) * samples, :] = ref[:, at : at + variants]
    line = turned_ref.shape[1]
    rotated = jnp.dot(turned_ref[...], dose_scr[:line], preferred_element_type=f32)
    rotated += jnp.dot(turned2_ref[...], dose_scr[line:], preferred_element_type=f32)
    rotated = rotated.astype(bf16)
    squared = jnp.square(rotated.astype(f32)).astype(bf16)
    cross = jnp.dot(weighted_ref[...], rotated, preferred_element_type=f32)
    power = jnp.dot(low_ref[...], squared, preferred_element_type=f32)
    cross_ref[...] = cross
    product_ref[...] = power
    pass_ref[...] = window(place_ref, gene_ref, power_ref, cross, power, 1 - place_ref[1], dose_scr.shape[0])


def keep_kernel(place_ref, gene_ref, power_ref, cross_ref, product_ref, keep_ref, *, samples):
    keep_ref[...] = window(
        place_ref, gene_ref, power_ref, cross_ref[...], product_ref[...], place_ref[1], samples
    )


def call(kernel, outs, count, scratch=(), smem=1, anywhere=0, limit=VMEM_LIMIT):
    vmem = pl.BlockSpec(memory_space=pltpu.VMEM)
    return pl.pallas_call(
        kernel,
        out_shape=[jax.ShapeDtypeStruct(*o) for o in outs],
        in_specs=[pl.BlockSpec(memory_space=pltpu.SMEM)] * smem + [vmem] * (count - smem - anywhere) + [pl.BlockSpec(memory_space=pl.ANY)] * anywhere,
        out_specs=[vmem] * len(outs),
        scratch_shapes=list(scratch),
        compiler_params=pltpu.CompilerParams(vmem_limit_bytes=limit),
    )


def near_body(eigvecs, eigvals, expression, dosage, delta, window_start, window_valid, gene_owner):
    rows = lax.axis_size("row")
    row = lax.axis_index("row")
    core = lax.axis_index("col")
    panel, half = eigvecs.shape
    part = panel // 2
    samples = panel * rows
    variants = dosage.shape[1] // 2
    place = jnp.stack([row, core]).astype(jnp.int32)

    def swap(x, m):
        return lax.ppermute(x, "row", [(i, i ^ m) for i in range(rows)])

    def other_core(x):
        return lax.ppermute(x, "col", [(0, 1), (1, 0)])

    ahead, e46, e2, e0, gene, terms, d0 = call(
        route_kernel,
        [
            ((panel, half + 2 * LANES), bf16),
            ((part, 2 * LANES), bf16),
            ((part, LANES), bf16),
            ((part, LANES), bf16),
            ((LANES, LANES), f32),
            ((16, half), bf16),
            ((panel, variants), bf16),
        ],
        9,
        scratch=[pltpu.VMEM((rows, LANES), kind) for kind in (jnp.int32, f32, jnp.int32, jnp.int32)]
        + [pltpu.VMEM((1, half), f32), pltpu.VMEM((part, expression.shape[1]), bf16), pltpu.SemaphoreType.DMA((8,))],
        anywhere=8,
        limit=VMEM_LIMIT,
    )(
        place,
        *[
            pltpu.with_memory_space_constraint(x, pltpu.HBM)
            for x in (
                gene_owner.reshape(rows, LANES),
                delta.reshape(rows, LANES),
                window_start.reshape(rows, LANES),
                window_valid.reshape(rows, LANES),
                eigvals[None, :],
                eigvecs,
                expression,
                dosage,
            )
        ],
    )
    r1 = swap(ahead, 1)
    d4 = swap(d0, 4)
    d2 = swap(jnp.concatenate([d0, ahead[:, :half]], axis=1), 2)
    to4 = call(second_kernel, [((panel, 2 * half + 2 * LANES), bf16)], 3, smem=0)(ahead, r1, e46)[0]
    r4 = swap(to4, 4)
    own = call(copy_kernel, [((panel, variants), bf16)], 2, smem=0, anywhere=1)(d0, to4)[0]
    d1 = swap(own, 1)
    far = call(copy_kernel, [((panel, variants), bf16)], 2, smem=0, anywhere=1)(d4, to4)[0]
    d6 = swap(far, 2)
    d5 = swap(far, 1)
    d37 = swap(jnp.concatenate([d2[:, :variants], d6], axis=1), 1)
    width = 4 * half + 2 * LANES
    out, kept = call(
        third_kernel,
        [((panel, width - half), bf16), ((panel, width + 2 * half), bf16)],
        9,
        smem=0,
        anywhere=2,
    )(ahead, r1, r4, e2, e0, terms, d2, far, d1)
    kept2 = other_core(kept)
    near = swap(out, 2)
    near2 = other_core(near)
    shape = ((2 * half, samples // 2), bf16)
    turned, share = call(
        half_kernel,
        [shape, ((LANES, 2 * half), f32)],
        4,
        scratch=[pltpu.VMEM((samples // 2, LANES), bf16)],
        anywhere=1,
    )(place, kept, kept2, d5)
    turned2, weighted, low, power = call(
        weight_kernel,
        [shape, ((LANES, 2 * half), bf16), ((LANES, 2 * half), bf16), ((LANES, LANES), f32)],
        7,
        scratch=[pltpu.VMEM((samples // 2, LANES), bf16)],
    )(place, kept, kept2, near, near2, share, gene)
    cross, product, passed = call(
        score_kernel,
        [((LANES, variants), f32)] * 2 + [((LANES, LANES), f32)],
        14,
        scratch=[pltpu.VMEM((samples, variants), bf16)],
    )(place, gene, power, turned, turned2, weighted, low, d0, d1, d4, d5, d2, d37, d6)
    keep = call(functools.partial(keep_kernel, samples=samples), [((LANES, LANES), f32)], 5)(
        place, gene, power, cross, product
    )[0]
    return keep + other_core(passed)


def body(eigvecs, eigvals, expression, dosage, delta, window_start, window_valid, gene_owner):
    rows = lax.axis_size("row")
    samples = eigvecs.shape[0] * rows
    own = expression.shape[1] // rows
    fits = (
        lax.axis_size("col") == 2
        and own == LANES
        and W == 2 * LANES
        and rows == 8
        and dosage.shape[1] % (2 * LANES) == 0
        and samples * (samples + dosage.shape[1]) <= VMEM_LIMIT // 16
    )
    run = near_body if fits else wide_body
    return run(eigvecs, eigvals, expression, dosage, delta, window_start, window_valid, gene_owner)


def solution(mesh):
    placed = (
        P(("groups", "row"), "col"),
        P(("groups", "col")),
        P(("groups", "row"), None),
        P(("groups", "row"), None),
        P("groups"),
        P("groups"),
        P("groups"),
        P("groups"),
    )
    return jax.shard_map(
        body, mesh=mesh, in_specs=placed, out_specs=P(("groups", "row"), "col"), check_vma=False
    )
```

```python
import functools

import jax
import jax.numpy as jnp
from jax import lax
from jax.experimental import pallas as pl
from jax.experimental.pallas import tpu as pltpu
from jax.sharding import PartitionSpec as P

W = 256
LANES = 128
VMEM_LIMIT = 32 * 1024 * 1024
NT = (((1,), (1,)), ((), ()))
f32 = jnp.float32
bf16 = jnp.bfloat16


def owner_listing(gene_owner):
    total = gene_owner.shape[0]
    return jnp.argsort(gene_owner * total + jnp.arange(total, dtype=jnp.int32))


def earlier_equal(labels):
    places = jnp.arange(labels.shape[0], dtype=jnp.int32)
    same = labels[:, None] == labels[None, :]
    before = places[:, None] > places[None, :]
    return jnp.sum((same & before).astype(jnp.int32), axis=1)


def shift_windows(tables, starts, largest):
    moved_tables = tables
    step_size = 1
    while step_size <= largest:
        bit_set = starts // step_size % 2 == 1
        filler = jnp.zeros(moved_tables.shape[:-1] + (step_size,), moved_tables.dtype)
        moved = jnp.concatenate([moved_tables[..., step_size:], filler], axis=-1)
        moved_tables = jnp.where(bit_set[None, :, None], moved, moved_tables)
        step_size = step_size * 2
    return moved_tables


def wide_body(eigvecs, eigvals, expression, dosage, delta, window_start, window_valid, gene_owner):
    row_count = lax.axis_size("row")
    row_index = lax.axis_index("row")
    genes_all = expression.shape[1]
    own_count = genes_all // row_count
    half_samples = eigvecs.shape[1]
    samples = half_samples * lax.axis_size("col")
    owner_order = owner_listing(gene_owner)
    my_genes = lax.dynamic_slice_in_dim(owner_order, row_index * own_count, own_count)
    expr_panel, dose_panel = (
        lax.all_to_all(expression, "row", split_axis=1, concat_axis=0, tiled=True),
        lax.all_to_all(dosage, "row", split_axis=1, concat_axis=0, tiled=True),
    )
    panel_data = jnp.concatenate([expr_panel, dose_panel], axis=1)
    rotated = lax.dot_general(
        panel_data,
        lax.all_gather(eigvecs, "row", axis=0, tiled=True),
        (((0,), (0,)), ((), ())),
        preferred_element_type=jnp.float32,
    ).astype(jnp.bfloat16)
    rot_expr = rotated[:own_count]
    rot_dose = rotated[own_count:]
    dose_all = lax.all_gather(rot_dose, "row", axis=0, tiled=True)
    capacity = max(2, own_count // row_count)
    destination = lax.dynamic_slice_in_dim(gene_owner, row_index * own_count, own_count)
    position = destination * capacity + earlier_equal(destination)
    slot_ids = jnp.arange(row_count * capacity, dtype=jnp.int32)
    placement_map = (slot_ids[:, None] == position[None, :]).astype(jnp.bfloat16)
    buckets = jnp.dot(placement_map, rot_expr, preferred_element_type=jnp.float32).astype(
        jnp.bfloat16
    )
    received = lax.all_to_all(buckets, "row", split_axis=0, concat_axis=0, tiled=True)
    source = my_genes // own_count
    owned_expr = jnp.take(received, source * capacity + earlier_equal(source), axis=0)
    own_delta = jnp.take(delta, my_genes)
    own_start = jnp.take(window_start, my_genes)
    own_valid = jnp.take(window_valid, my_genes)
    weight = 1.0 / (eigvals[None, :] + own_delta[:, None])
    expr_float = owned_expr.astype(jnp.float32)
    expr_power = jnp.sum(weight * expr_float * expr_float, axis=1)
    weighted = (weight * expr_float).astype(jnp.bfloat16)
    weight_low = weight.astype(jnp.bfloat16)
    dose_sq = jnp.square(dose_all.astype(jnp.float32)).astype(jnp.bfloat16)
    slot_index = jnp.arange(W, dtype=jnp.int32)
    contract = (((1,), (1,)), ((), ()))
    cross_all = lax.dot_general(weighted, dose_all, contract, preferred_element_type=jnp.float32)
    power_all = lax.dot_general(weight_low, dose_sq, contract, preferred_element_type=jnp.float32)
    stacked = jnp.stack([cross_all, power_all], axis=0)
    variants = dose_all.shape[0]
    shifted = shift_windows(stacked, own_start, variants - W)
    cross_sum = shifted[0, :, :W]
    dose_power = shifted[1, :, :W]
    cross_sum, dose_power, expr_power = lax.psum((cross_sum, dose_power, expr_power), "col")
    scale = jnp.sqrt(jnp.float32(samples))
    zscore = jnp.where(
        slot_index[None, :] < own_valid[:, None],
        scale * cross_sum / jnp.sqrt(dose_power * expr_power[:, None]),
        0.0,
    )
    width_part = W // lax.axis_size("col")
    return lax.dynamic_slice_in_dim(zscore, lax.axis_index("col") * width_part, width_part, 1)


def route_kernel(
    place_ref, owner_any, expr_any, vecs_any, dose_any,
    ahead_ref, e46_ref, e2_ref, e0_ref, half_ref, bucket_ref,
    owner_ref, expr_ref, sems,
):
    row, core = place_ref[0], place_ref[1]
    half = vecs_any.shape[1]
    part = expr_ref.shape[0]
    variants = half_ref.shape[1]
    pairs = (
        (owner_any, owner_ref),
        (expr_any.at[pl.ds(pl.multiple_of(core * part, part), part)], expr_ref),
        (vecs_any, ahead_ref.at[:, pl.ds(0, half)]),
        (dose_any.at[:, pl.ds(pl.multiple_of(core * variants, LANES), variants)], half_ref),
    )
    copies = [pltpu.make_async_copy(a, b, sems.at[i]) for i, (a, b) in enumerate(pairs)]
    for copy in copies:
        copy.start()
    slices = owner_ref.shape[0]
    capacity = LANES // slices
    before = lax.broadcasted_iota(jnp.int32, (LANES, LANES), 0) < lax.broadcasted_iota(
        jnp.int32, (LANES, LANES), 1
    )
    before = before.astype(bf16)
    slot = lax.broadcasted_iota(jnp.int32, (LANES, LANES), 0)
    copies[0].wait()
    owner = owner_ref[...]
    rank = jnp.zeros(owner.shape, f32)
    for o in range(slices):
        same = (owner == o).astype(f32)
        rank += same * jnp.dot(same.astype(bf16), before, preferred_element_type=f32)
    bucket = (owner ^ row) * capacity + rank.astype(jnp.int32)
    bucket_ref[...] = bucket
    copies[1].wait()
    sorted_slices = []
    for s in range(slices):
        here = bucket[s : s + 1, :]
        pick = (slot == here).astype(bf16)
        sorted_slices.append(
            lax.dot_general(pick, expr_ref[:, s * LANES : (s + 1) * LANES], NT, preferred_element_type=f32)
        )
    left, right = slice(0, LANES), slice(LANES, 2 * LANES)
    upper, lower = slice(0, part), slice(part, 2 * part)
    targets = {
        0: (e0_ref, upper, left),
        1: (ahead_ref, upper, slice(half, half + LANES)),
        2: (e2_ref, upper, left),
        3: (ahead_ref, upper, slice(half + LANES, half + 2 * LANES)),
        4: (e46_ref, upper, left),
        5: (ahead_ref, lower, slice(half, half + LANES)),
        6: (e46_ref, upper, right),
        7: (ahead_ref, lower, slice(half + LANES, half + 2 * LANES)),
    }
    for m, (ref, down, side) in targets.items():
        block = jnp.concatenate([x[m * capacity : (m + 1) * capacity, :] for x in sorted_slices], axis=0)
        ref[down, side] = block.T.astype(bf16)
    for copy in copies[2:]:
        copy.wait()


def gene_kernel(bucket_ref, delta_ref, start_ref, valid_ref, vals_ref, gene_ref, terms_ref):
    slices = bucket_ref.shape[0]
    capacity = LANES // slices
    own_slot = lax.broadcasted_iota(jnp.int32, (capacity, LANES), 0)
    lane = lax.broadcasted_iota(jnp.int32, (capacity, LANES), 1)
    for s in range(slices):
        mine = (own_slot == bucket_ref[s : s + 1, :]).astype(f32)
        figures = jnp.zeros((capacity, LANES), f32)
        for i, ref in enumerate((delta_ref, start_ref, valid_ref)):
            line = ref[s : s + 1, :].astype(f32)
            figures = jnp.where(lane == i, jnp.sum(mine * line, axis=1, keepdims=True), figures)
        gene_ref[s * capacity : (s + 1) * capacity, :] = figures
    vals = vals_ref[...]
    high = vals.astype(bf16).astype(f32)
    middle = (vals - high).astype(bf16).astype(f32)
    term = lax.broadcasted_iota(jnp.int32, terms_ref.shape, 0)
    terms = jnp.where(term == 0, high, jnp.where(term == 1, middle, jnp.where(term == 2, vals - high - middle, 0.0)))
    terms_ref[...] = terms.astype(bf16)


def second_kernel(ahead_ref, r1_ref, e46_ref, out_ref):
    half = out_ref.shape[1] // 2 - LANES
    part = e46_ref.shape[0]
    out_ref[:, :half] = ahead_ref[:, :half]
    out_ref[:, half : 2 * half] = r1_ref[:, :half]
    out_ref[:part, 2 * half :] = e46_ref[...]
    out_ref[part:, 2 * half :] = r1_ref[part:, half:]


def copy_kernel(d0_ref, d4_ref, after_any, pair_ref, far_ref):
    variants = d0_ref.shape[1]
    pair_ref[:, :variants] = d0_ref[...]
    pair_ref[:, variants:] = d4_ref[...]
    far_ref[...] = d4_ref[...]


def third_kernel(ahead_ref, r1_ref, r4_ref, e2_ref, e0_ref, terms_ref, d2_ref, far_any, out_ref, kept_ref):
    half = terms_ref.shape[1]
    part = e0_ref.shape[0]
    kept_ref[:, :half] = ahead_ref[:, :half]
    for ref, own, at, first in ((out_ref, e2_ref, LANES, 0), (kept_ref, e0_ref, 0, half)):
        ref[:, first : first + half] = r1_ref[:, :half]
        ref[:, first + half : first + 3 * half] = r4_ref[:, : 2 * half]
        side = slice(2 * half + at, 2 * half + at + LANES)
        middle = first + 3 * half + LANES
        left, right = slice(middle - LANES, middle), slice(middle, middle + LANES)
        ref[:part, left] = own[...]
        ref[:part, right] = r1_ref[:part, half + at : half + at + LANES]
        ref[part:, left] = r4_ref[:part, side]
        ref[part:, right] = r4_ref[part:, side]
    width = out_ref.shape[1] + half
    terms = terms_ref.shape[0]
    kept_ref[:terms, width : width + half] = terms_ref[...]
    kept_ref[terms:, width : width + half] = jnp.zeros((kept_ref.shape[0] - terms, half), bf16)
    kept_ref[:, width + half :] = d2_ref[:, d2_ref.shape[1] - half :]


def rotate(place_ref, refs, turned_ref, data_scr, panels, data_at):
    samples = refs[0].shape[0]
    half = turned_ref.shape[0] // 2
    part = samples // 2
    core = place_ref[1]
    for c, ref in enumerate(refs):
        side = core if c == 0 else 1 - core
        for i in range(4):
            panel, at = panels[c][i]
            turned_ref[c * half : (c + 1) * half, i * samples : (i + 1) * samples] = (
                panel[:, at : at + half].astype(f32).T.astype(bf16)
            )
            at = data_at + i % 2 * LANES
            data_scr[pl.ds(pl.multiple_of(i * samples + side * part, part), part), :] = ref[
                i // 2 * part : (i // 2 + 1) * part, at : at + LANES
            ]
    data = data_scr[...].astype(f32).T.astype(bf16)
    shares = []
    for c in range(2):
        vecs = jnp.concatenate([panel[:, at : at + half] for panel, at in panels[c]], axis=0)
        shares.append(jnp.dot(data, vecs, preferred_element_type=f32))
    return shares


def half_kernel(place_ref, mine_ref, other_ref, d0_ref, d15_ref, d4_ref, line_ref, share_ref, data_scr, turned_ref, dose_scr):
    half = turned_ref.shape[0] // 2
    refs = (mine_ref, other_ref)
    panels = [[(ref, i * half) for i in range(4)] for ref in refs]
    for c, share in enumerate(rotate(place_ref, refs, turned_ref, data_scr, panels, 4 * half)):
        share_ref[:, c * half : (c + 1) * half] = share
    samples, variants = d0_ref.shape
    dose_scr[:samples, :] = d0_ref[...]
    dose_scr[samples : 2 * samples, :] = d15_ref[:, :variants]
    dose_scr[2 * samples : 3 * samples, :] = d4_ref[...]
    dose_scr[3 * samples :, :] = d15_ref[:, variants:]
    line_ref[...] = jnp.dot(turned_ref[...], dose_scr[...], preferred_element_type=f32)


def weight_kernel(
    place_ref, kept_ref, kept2_ref, mine_ref, other_ref, share_ref, gene_ref,
    turned_ref, weighted_ref, low_ref, power_ref, data_scr,
):
    half = turned_ref.shape[0] // 2
    delta = gene_ref[:, 0:1]
    total = jnp.zeros((delta.shape[0], 1), f32)
    width = mine_ref.shape[1] + half
    panels = [
        [(kept, width + half)] + [(ref, i * half) for i in range(3)]
        for kept, ref in ((kept_ref, mine_ref), (kept2_ref, other_ref))
    ]
    shares = rotate(place_ref, (mine_ref, other_ref), turned_ref, data_scr, panels, 3 * half)
    for c, (share, ref) in enumerate(zip(shares, (kept_ref, kept2_ref))):
        cols = slice(c * half, (c + 1) * half)
        terms = ref[0:16, width : width + half].astype(f32)
        vals = terms[0:1] + terms[1:2] + terms[2:3]
        rotated = (share_ref[:, cols] + share).astype(bf16).astype(f32)
        weight = 1.0 / (vals + delta)
        total += jnp.sum(weight * rotated * rotated, axis=1, keepdims=True)
        weighted_ref[:, cols] = (weight * rotated).astype(bf16)
        low_ref[:, cols] = weight.astype(bf16)
    power_ref[...] = jnp.broadcast_to(total, power_ref.shape)


def window(place_ref, gene_ref, power_ref, cross, power, half, samples):
    core = place_ref[1]
    start = gene_ref[:, 1:2].astype(jnp.int32)
    valid = gene_ref[:, 2:3].astype(jnp.int32)
    genes = cross.shape[0]
    lane = lax.broadcasted_iota(jnp.int32, (genes, LANES), 1)
    own_power = power_ref[...]
    scale = jnp.sqrt(f32(samples))
    variants = cross.shape[1]
    blocks = variants // LANES
    offset = start + half * LANES - core * variants
    block = offset >> 7
    shift = offset & (LANES - 1)
    need = block + (lane < shift).astype(jnp.int32)
    products = [jnp.zeros((genes, LANES), f32)] * 2
    for b in range(blocks):
        here = need == b
        parts = [array[:, b * LANES : (b + 1) * LANES] for array in (cross, power)]
        products = [jnp.where(here, part, product) for part, product in zip(parts, products)]
    inside = (need >= 0) & (need < blocks)
    score = jnp.where(inside, scale * products[0] / jnp.sqrt(products[1] * own_power), 0.0)
    score = jnp.take_along_axis(score, (lane + shift) & (LANES - 1), axis=1)
    return jnp.where(lane + half * LANES < valid, score, 0.0)


def score_kernel(place_ref, gene_ref, power_ref, line_ref, turned_ref, weighted_ref, low_ref, *refs):
    *dose_refs, cross_ref, product_ref, pass_ref, dose_scr = refs
    samples, variants = dose_refs[2].shape
    chunks = [(ref, at) for ref in dose_refs for at in range(0, ref.shape[1] - variants + 1, variants)]
    order = [0, 1, 3, 2]
    for m, (ref, at) in enumerate(chunks[i] for i in order):
        dose_scr[m * samples : (m + 1) * samples, :] = ref[:, at : at + variants]
    rotated = line_ref[...] + jnp.dot(turned_ref[...], dose_scr[...], preferred_element_type=f32)
    rotated = rotated.astype(bf16)
    squared = jnp.square(rotated.astype(f32)).astype(bf16)
    cross = jnp.dot(weighted_ref[...], rotated, preferred_element_type=f32)
    power = jnp.dot(low_ref[...], squared, preferred_element_type=f32)
    cross_ref[...] = cross
    product_ref[...] = power
    pass_ref[...] = window(place_ref, gene_ref, power_ref, cross, power, 1 - place_ref[1], line_ref.shape[0])


def keep_kernel(place_ref, gene_ref, power_ref, cross_ref, product_ref, keep_ref, *, samples):
    keep_ref[...] = window(
        place_ref, gene_ref, power_ref, cross_ref[...], product_ref[...], place_ref[1], samples
    )


def call(kernel, outs, count, scratch=(), smem=1, anywhere=0, limit=VMEM_LIMIT):
    vmem = pl.BlockSpec(memory_space=pltpu.VMEM)
    return pl.pallas_call(
        kernel,
        out_shape=[jax.ShapeDtypeStruct(*o) for o in outs],
        in_specs=[pl.BlockSpec(memory_space=pltpu.SMEM)] * smem + [vmem] * (count - smem - anywhere) + [pl.BlockSpec(memory_space=pl.ANY)] * anywhere,
        out_specs=[vmem] * len(outs),
        scratch_shapes=list(scratch),
        compiler_params=pltpu.CompilerParams(vmem_limit_bytes=limit),
    )


def near_body(eigvecs, eigvals, expression, dosage, delta, window_start, window_valid, gene_owner):
    rows = lax.axis_size("row")
    row = lax.axis_index("row")
    core = lax.axis_index("col")
    panel, half = eigvecs.shape
    part = panel // 2
    samples = panel * rows
    variants = dosage.shape[1] // 2
    place = jnp.stack([row, core]).astype(jnp.int32)

    def swap(x, m):
        return lax.ppermute(x, "row", [(i, i ^ m) for i in range(rows)])

    def other_core(x):
        return lax.ppermute(x, "col", [(0, 1), (1, 0)])

    ahead, e46, e2, e0, d0, bucket = call(
        route_kernel,
        [
            ((panel, half + 2 * LANES), bf16),
            ((part, 2 * LANES), bf16),
            ((part, LANES), bf16),
            ((part, LANES), bf16),
            ((panel, variants), bf16),
            ((rows, LANES), jnp.int32),
        ],
        5,
        scratch=[
            pltpu.VMEM((rows, LANES), jnp.int32),
            pltpu.VMEM((part, expression.shape[1]), bf16),
            pltpu.SemaphoreType.DMA((4,)),
        ],
        anywhere=4,
    )(
        place,
        *[
            pltpu.with_memory_space_constraint(x, pltpu.HBM)
            for x in (gene_owner.reshape(rows, LANES), expression, eigvecs, dosage)
        ],
    )
    gene, terms = call(gene_kernel, [((LANES, LANES), f32), ((16, half), bf16)], 5, smem=0)(
        bucket,
        delta.reshape(rows, LANES),
        window_start.reshape(rows, LANES),
        window_valid.reshape(rows, LANES),
        eigvals[None, :],
    )
    r1 = swap(ahead, 1)
    d4 = swap(d0, 4)
    d2 = swap(jnp.concatenate([d0, ahead[:, :half]], axis=1), 2)
    to4 = call(second_kernel, [((panel, 2 * half + 2 * LANES), bf16)], 3, smem=0)(ahead, r1, e46)[0]
    r4 = swap(to4, 4)
    pair, far = call(
        copy_kernel, [((panel, 2 * variants), bf16), ((panel, variants), bf16)], 3, smem=0, anywhere=1
    )(d0, d4, to4)
    d6 = swap(far, 2)
    d15 = swap(pair, 1)
    d37 = swap(jnp.concatenate([d2[:, :variants], d6], axis=1), 1)
    width = 4 * half + 2 * LANES
    out, kept = call(
        third_kernel,
        [((panel, width - half), bf16), ((panel, width + 2 * half), bf16)],
        8,
        smem=0,
        anywhere=1,
    )(ahead, r1, r4, e2, e0, terms, d2, far)
    kept2 = other_core(kept)
    near = swap(out, 2)
    near2 = other_core(near)
    shape = ((2 * half, samples // 2), bf16)
    line, share = call(
        half_kernel,
        [((2 * half, variants), f32), ((LANES, 2 * half), f32)],
        6,
        scratch=[
            pltpu.VMEM((samples // 2, LANES), bf16),
            pltpu.VMEM((2 * half, samples // 2), bf16),
            pltpu.VMEM((samples // 2, variants), bf16),
        ],
    )(place, kept, kept2, d0, d15, d4)
    turned2, weighted, low, power = call(
        weight_kernel,
        [shape, ((LANES, 2 * half), bf16), ((LANES, 2 * half), bf16), ((LANES, LANES), f32)],
        7,
        scratch=[pltpu.VMEM((samples // 2, LANES), bf16)],
    )(place, kept, kept2, near, near2, share, gene)
    cross, product, passed = call(
        score_kernel,
        [((LANES, variants), f32)] * 2 + [((LANES, LANES), f32)],
        10,
        scratch=[pltpu.VMEM((samples // 2, variants), bf16)],
    )(place, gene, power, line, turned2, weighted, low, d2, d37, d6)
    keep = call(functools.partial(keep_kernel, samples=samples), [((LANES, LANES), f32)], 5)(
        place, gene, power, cross, product
    )[0]
    return keep + other_core(passed)


def body(eigvecs, eigvals, expression, dosage, delta, window_start, window_valid, gene_owner):
    rows = lax.axis_size("row")
    samples = eigvecs.shape[0] * rows
    own = expression.shape[1] // rows
    fits = (
        lax.axis_size("col") == 2
        and own == LANES
        and W == 2 * LANES
        and rows == 8
        and dosage.shape[1] % (2 * LANES) == 0
        and samples * (samples + dosage.shape[1]) <= VMEM_LIMIT // 16
    )
    run = near_body if fits else wide_body
    return run(eigvecs, eigvals, expression, dosage, delta, window_start, window_valid, gene_owner)


def solution(mesh):
    placed = (
        P(("groups", "row"), "col"),
        P(("groups", "col")),
        P(("groups", "row"), None),
        P(("groups", "row"), None),
        P("groups"),
        P("groups"),
        P("groups"),
        P("groups"),
    )
    return jax.shard_map(
        body, mesh=mesh, in_specs=placed, out_specs=P(("groups", "row"), "col"), check_vma=False
    )
```
